32 devices in a mesh: rows: 8 (over z, y), ch: 4 (over x, core).
Axes of the slice: x: 2, y: 2, z: 4, core: 2. Of those that a mesh axis runs over, the one named last changes fastest.
Arguments:
- inputs: bfloat16 [8, 1024, 1024], P('rows', 'ch'), may hold values from -6 to 6
- segment_ids: int32 [8, 1024], P('rows'), may hold values from 0 to 3, never falling along the last dimension, each value on 1 to 512 neighbouring positions
- mixer_gain: float32 [1024], replicated, may hold values from 0.1 to 1.9
- branch_weight: bfloat16 [1024, 1536], P(None, 'ch'), may hold values from -0.1875 to 0.1875
- input_weight: bfloat16 [1024, 1536], P(None, 'ch'), may hold values from -0.1875 to 0.1875
- conv_weight: float32 [4, 1536], P(None, 'ch'), may hold values from -3 to 3
- conv_bias: float32 [1536], P('ch'), may hold values from -3 to 3
- recur_weight: bfloat16 [8, 192, 192], P('ch'), may hold values from -0.4375 to 0.4375
- recur_bias: float32 [1536], P('ch'), may hold values from -3 to 3
- gate_weight: bfloat16 [8, 192, 192], P('ch'), may hold values from -0.4375 to 0.4375
- gate_bias: float32 [1536], P('ch'), may hold values from -3 to 3
- decay_param: float32 [1536], P('ch'), may hold values from -11 to -3
- out_weight: bfloat16 [1536, 1024], P('ch'), may hold values from -0.4375 to 0.4375
- mlp_gain: float32 [1024], replicated, may hold values from 0.1 to 1.9
- mlp_gate: bfloat16 [1024, 3072], P(None, 'ch'), may hold values from -0.1875 to 0.1875
- mlp_up: bfloat16 [1024, 3072], P(None, 'ch'), may hold values from -0.1875 to 0.1875
- mlp_down: bfloat16 [3072, 1024], P('ch'), may hold values from -0.21875 to 0.21875
- cotangent: bfloat16 [8, 1024, 1024], P('rows', 'ch'), may hold values from -6 to 6
Outputs:
- output: bfloat16 [8, 1024, 1024], P('rows', 'ch')
- input_grad: float32 [8, 1024, 1024], P('rows', 'ch')
- mixer_gain_grad: float32 [1024], replicated
- branch_weight_grad: float32 [1024, 1536], P(None, 'ch')
- input_weight_grad: float32 [1024, 1536], P(None, 'ch')
- conv_weight_grad: float32 [4, 1536], P(None, 'ch')
- conv_bias_grad: float32 [1536], P('ch')
- recur_weight_grad: float32 [8, 192, 192], P('ch')
- recur_bias_grad: float32 [1536], P('ch')
- gate_weight_grad: float32 [8, 192, 192], P('ch')
- gate_bias_grad: float32 [1536], P('ch')
- decay_param_grad: float32 [1536], P('ch')
- out_weight_grad: float32 [1536, 1024], P('ch')
- mlp_gain_grad: float32 [1024], replicated
- mlp_gate_grad: float32 [1024, 3072], P(None, 'ch')
- mlp_up_grad: float32 [1024, 3072], P(None, 'ch')
- mlp_down_grad: float32 [3072, 1024], P('ch')
The draws below stay inside these ranges and needn't reach their ends.
Inputs may be any that keep to these rules, and one draw needn't show every extreme that they name: `segment_ids`: along each row the ids never fall; a row holds up to 4 segments, none longer than 512 positions.
All inputs are finite; a program needn't handle non-finite values.
Results may differ from the reference program's by a relative error of at most 0.011.
Values may be sent and summed in bfloat16 or wider, within the bound.
No kernel may reach another device: no remote copies, remote signals or barrier semaphores. Data moves between devices by JAX's collectives and lax.ppermute only.
A program may use at most 192 MiB of HBM per device.

```python
import math
import jax
import jax.numpy as jnp
import numpy as np
from jax import lax

D = 1024
HEADS = 8
HD = 192
MLP = 3072
TAPS = 4
SEQ = 1024
SEGS = 4
RNN = 1536
ROWS = 8


def block_scale(stream_key, shape, shards, least, top_value):
    level = 1.0
    for dim, shards_of in shards:
        heights = jax.random.uniform(jax.random.fold_in(jax.random.fold_in(stream_key, 6), dim), (shards_of,), jnp.float32, least / len(shards), top_value / len(shards))
        level = level * jnp.repeat(jnp.exp(heights), shape[dim] // shards_of).reshape((-1,) + (1,) * (len(shape) - 1 - dim))
    return level


def split_up(amount, total, reach, slope):
    loads = [(1 << 20) // math.isqrt(standing ** slope) + 1 for standing in range(2, amount + 1)]
    spare, holding = total - reach - (amount - 1), [1] * (amount - 1)
    while spare > 0:
        candidates = [i for i in range(amount - 1) if holding[i] < reach]
        whole, left = sum([loads[i] for i in candidates]), spare
        for i in candidates:
            more = min(reach - holding[i], max(1, left * loads[i] // whole), spare)
            holding[i] = holding[i] + more
            spare = spare - more
    return np.array([reach] + holding)


def ragged_sizes(stream_key, number_of, total, bound, lean):
    if number_of == 2:
        one = jax.random.randint(stream_key, (), max(1, total - bound), min(bound, total - 1) + 1)
        return jnp.stack([one, total - one])
    tallies = jnp.asarray(split_up(number_of, total, bound, lean), jnp.int32)
    twos = (number_of - 1) // 2
    source_of, receiver = tallies[1:1 + 2 * twos:2], tallies[2:2 + 2 * twos:2]
    room = jnp.minimum(source_of - 1, bound - receiver)
    passed = jax.random.randint(jax.random.fold_in(stream_key, 1), (twos,), 0, 1 << 20) % (room + 1)
    tallies = tallies.at[1:1 + 2 * twos:2].set(source_of - passed).at[2:2 + 2 * twos:2].set(receiver + passed)
    return tallies[jax.random.permutation(jax.random.fold_in(stream_key, 2), number_of)]


def noise(key, dims, width, most, cuts=(), held_as=jnp.bfloat16):
    values = jax.random.normal(key, dims, jnp.float32) * width
    if len(cuts) > 0:
        values = block_scale(key, dims, cuts, -0.22, 0.18) * values
    return jnp.clip(values, min=-most, max=most).astype(held_as)


def setup_inputs(seed: int = 0) -> dict:
    splits = jax.random.split(jax.random.key(seed), 19)
    return {
        "inputs": noise(splits[0], (ROWS, SEQ, D), 1.0, 6.0, ((0, 8), (1, 4))),
        "segment_ids": jax.vmap(lambda own: jnp.searchsorted(jnp.cumsum(ragged_sizes(own, SEGS, SEQ, SEQ // 2, 0)), jnp.arange(SEQ), side="right"))(jax.random.split(splits[1], ROWS)).reshape((ROWS, SEQ)).astype(jnp.int32),
        "mixer_gain": jnp.clip(1.0 + 0.18 * jax.random.normal(splits[2], (D,), jnp.float32), 0.1, 1.9),
        "branch_weight": noise(splits[3], (D, RNN), D ** -0.5, 0.1875, ((1, 4),)),
        "input_weight": noise(splits[4], (D, RNN), D ** -0.5, 0.1875, ((1, 4),)),
        "conv_weight": noise(splits[5], (TAPS, RNN), TAPS ** -0.5, 3.0, ((1, 4),), jnp.float32),
        "conv_bias": noise(splits[6], (RNN,), 0.5, 3.0, ((0, 4),), jnp.float32),
        "recur_weight": noise(splits[7], (HEADS, HD, HD), HD ** -0.5, 0.4375, ((0, 4),)),
        "recur_bias": noise(splits[8], (RNN,), 0.5, 3.0, ((0, 4),), jnp.float32),
        "gate_weight": noise(splits[9], (HEADS, HD, HD), HD ** -0.5, 0.4375, ((0, 4),)),
        "gate_bias": noise(splits[10], (RNN,), 0.5, 3.0, ((0, 4),), jnp.float32),
        "decay_param": jnp.clip(-11.0 + 8.0 * jax.random.uniform(splits[11], (RNN,), jnp.float32) ** block_scale(splits[11], (RNN,), ((0, 4),), -0.2, 0.2), -11.0, -3.0),
        "out_weight": noise(splits[12], (RNN, D), (RNN // 8) ** -0.5, 0.4375, ((0, 4),)),
        "mlp_gain": jnp.clip(1.0 + 0.18 * jax.random.normal(splits[13], (D,), jnp.float32), 0.1, 1.9),
        "mlp_gate": noise(splits[14], (D, MLP), D ** -0.5, 0.1875, ((1, 4),)),
        "mlp_up": noise(splits[15], (D, MLP), D ** -0.5, 0.1875, ((1, 4),)),
        "mlp_down": noise(splits[16], (MLP, D), (MLP // 4) ** -0.5, 0.21875, ((0, 4),)),
        "cotangent": noise(splits[17], (ROWS, SEQ, D), 1.0, 6.0, ((0, 8), (1, 4))),
    }


@jax.custom_vjp
def low(v):
    return lax.optimization_barrier(v.astype(jnp.bfloat16)).astype(jnp.float32)

@jax.custom_vjp
def low_back(v):
    return v

def low_keep(v):
    return (low(v), None)

def low_pass(kept, grad):
    return (grad,)

def back_keep(v):
    return (v, None)

def back_low(kept, grad):
    return (low(grad),)
low.defvjp(low_keep, low_pass)
low_back.defvjp(back_keep, back_low)
EPSILON = 1e-06

def rms_norm(values, gain_vec):
    inverse = lax.rsqrt(lax.optimization_barrier(jnp.mean(values * values, axis=-1, keepdims=True)) + EPSILON)
    return values * inverse * gain_vec

def convolve(signal, segments, taps_weight, taps_bias):
    length = signal.shape[1]
    summed = taps_bias + taps_weight[0] * signal
    for offset in range(1, taps_weight.shape[0]):
        shifted = jnp.pad(signal, ((0, 0), (offset, 0), (0, 0)))[:, :length]
        shifted_ids = jnp.pad(segments, ((0, 0), (offset, 0)), constant_values=-1)[:, :length]
        same_mask = (shifted_ids == segments).astype(signal.dtype)[..., None]
        summed = summed + taps_weight[offset] * shifted * same_mask
    return summed

def link_steps(earlier, latest):
    return (earlier[0] * latest[0], latest[0] * earlier[1] + latest[1])

def recurrence(conv_in, recur_in, gate_in, decay_in, segments):
    recur_gate = jax.nn.sigmoid(recur_in)
    input_gate = jax.nn.sigmoid(gate_in)
    forget = jnp.exp(-8.0 * recur_gate * jax.nn.softplus(decay_in))
    scale_in = jnp.sqrt(jnp.maximum(1.0 - forget * forget, 0.001))
    previous = jnp.pad(segments, ((0, 0), (1, 0)), constant_values=-1)[:, :-1]
    keep_mask = (previous == segments).astype(conv_in.dtype)[..., None]
    carried = forget * keep_mask
    driven = scale_in * input_gate * conv_in
    _, states = lax.associative_scan(link_steps, (carried, driven), axis=1)
    return states

def matmul_rows(values, weight):
    return jnp.einsum('rsd,de->rse', values, weight, precision=lax.Precision.HIGHEST)

def heads_apply(values, weight):
    leading = values.shape[:-1]
    split_heads = values.reshape(leading + (weight.shape[0], weight.shape[1]))
    result = jnp.einsum('rshd,hde->rshe', split_heads, weight, precision=lax.Precision.HIGHEST)
    return result.reshape(leading + (weight.shape[0] * weight.shape[2],))

def forward(block_in, segments, mixer_gain, branch_weight, input_weight, conv_weight, conv_bias, recur_weight, recur_bias, gate_weight, gate_bias, decay_param, out_weight, mlp_gain, mlp_gate, mlp_up, mlp_down):
    normed = low(rms_norm(block_in, mixer_gain))
    branch_pre = low_back(matmul_rows(normed, branch_weight))
    recur_in = low_back(matmul_rows(normed, input_weight))
    conv_out = low(convolve(recur_in, segments, conv_weight, conv_bias))
    recur_pre = low_back(heads_apply(conv_out, recur_weight) + recur_bias)
    gate_pre = low_back(heads_apply(conv_out, gate_weight) + gate_bias)
    states = recurrence(conv_out, recur_pre, gate_pre, decay_param, segments)
    mixed_act = low(jax.nn.gelu(branch_pre) * states)
    branch_out = low_back(matmul_rows(mixed_act, out_weight))
    middle = block_in + branch_out
    normed2 = low(rms_norm(middle, mlp_gain))
    gate_act = low_back(matmul_rows(normed2, mlp_gate))
    up_act = low_back(matmul_rows(normed2, mlp_up))
    hidden = low(jax.nn.gelu(gate_act) * up_act)
    return middle + low_back(matmul_rows(hidden, mlp_down))

def reference(inputs, segment_ids, mixer_gain, branch_weight, input_weight, conv_weight, conv_bias, recur_weight, recur_bias, gate_weight, gate_bias, decay_param, out_weight, mlp_gain, mlp_gate, mlp_up, mlp_down, cotangent):
    params = tuple((p.astype(jnp.float32) for p in (mixer_gain, branch_weight, input_weight, conv_weight, conv_bias, recur_weight, recur_bias, gate_weight, gate_bias, decay_param, out_weight, mlp_gain, mlp_gate, mlp_up, mlp_down)))
    group_rows = math.gcd(ROWS, max(1, 4096 // SEQ))
    blocks = ROWS // group_rows
    block_inputs = inputs.astype(jnp.float32).reshape(blocks, group_rows, SEQ, D)
    block_ids = segment_ids.reshape(blocks, group_rows, SEQ).astype(jnp.int32)
    block_cots = cotangent.astype(jnp.float32).reshape(blocks, group_rows, SEQ, D)

    def step(totals, pieces):
        piece_in, piece_ids, piece_cot = pieces

        def local_forward(block_in, *weights):
            return forward(block_in, piece_ids, *weights)
        result, pullback = jax.vjp(local_forward, piece_in, *params)
        gradients = pullback(piece_cot)
        updated = tuple((t + g for t, g in zip(totals, gradients[1:])))
        return (updated, (result.astype(jnp.bfloat16), gradients[0]))
    initial = tuple((jnp.zeros_like(p) for p in params))
    totals, (outputs, input_grads) = lax.scan(step, initial, (block_inputs, block_ids, block_cots))
    return (outputs.reshape(ROWS, SEQ, D), input_grads.reshape(ROWS, SEQ, D), totals[0], totals[1], totals[2], totals[3], totals[4], totals[5], totals[6], totals[7], totals[8], totals[9], totals[10], totals[11], totals[12], totals[13], totals[14])
```

```python
import functools

import jax
import jax.numpy as jnp
from jax import lax
from jax.experimental import pallas as pl
from jax.experimental.pallas import tpu as pltpu
from jax.sharding import PartitionSpec as P

EPSILON = 1e-06
BF = jnp.bfloat16
F32 = jnp.float32
VMEM_LIMIT = 56 * 1024 * 1024
GELU_C = 0.7978845608028654
GELU_A = 0.044715


def mm(a, b):
    return lax.dot_general(a, b, (((1,), (0,)), ((), ())), preferred_element_type=F32)


def mm_nt(a, b):
    return lax.dot_general(a, b, (((1,), (1,)), ((), ())), preferred_element_type=F32)


def mm_tn(a, b):
    return lax.dot_general(a, b, (((0,), (0,)), ((), ())), preferred_element_type=F32)


def sigmoid(v):
    return 0.5 * jnp.tanh(0.5 * v) + 0.5


def gelu_both(v):
    sq = v * v
    th = jnp.tanh(GELU_C * v * (1.0 + GELU_A * sq))
    half = 0.5 * th + 0.5
    slope = half + (0.5 * GELU_C) * v * (1.0 - th * th) * (1.0 + (3.0 * GELU_A) * sq)
    return v * half, slope


def gelu_only(v):
    th = jnp.tanh(GELU_C * v * (1.0 + GELU_A * (v * v)))
    return v * (0.5 * th + 0.5)


def scan_groups(mult, add, start, back):
    rows, cols = mult.shape
    a = mult.reshape(rows // 8, 8, cols)
    d = add.reshape(rows // 8, 8, cols)
    sub = lax.broadcasted_iota(jnp.int32, (1, 8, cols), 1)
    for k in (1, 2, 4):
        ok = sub < 8 - k if back else sub >= k
        turn = 8 - k if back else k
        d = d + a * jnp.where(ok, pltpu.roll(d, turn, 1), 0.0)
        a = a * jnp.where(ok, pltpu.roll(a, turn, 1), 1.0)
    state = start
    got = [None] * (rows // 8)
    order = range(rows // 8)
    for g in reversed(order) if back else order:
        now = d[g] + a[g] * state
        state = now[0:1] if back else now[7:8]
        got[g] = now
    return jnp.concatenate(got, axis=0), state


def gate_values(conv, pre, c8, width):
    rg = sigmoid(pre[:, :width])
    ig = sigmoid(pre[:, width:])
    forget = jnp.exp(c8 * rg)
    om = 1.0 - forget * forget
    top = jnp.maximum(om, 0.001)
    inv = lax.rsqrt(top)
    return rg, ig, forget, om, top * inv, inv


def mixer_fwd(
    me_ref, b0, b1, b2, b3, gain, wb, wi, cw, cb, wrg, brg, c8, wo, masks,
    normed_o, br_o, ri_o, cv_o, sp_o, mix_o, p0, p1, p2, p3,
    xs, ext, state, sext,
):
    t = pl.program_id(0)
    r = jnp.bitwise_xor(t, me_ref[0])
    for i, ref in enumerate((b0, b1, b2, b3)):
        @pl.when(r == i)
        def _():
            xs[...] = ref[...]

    rows, width = br_o.shape[1], br_o.shape[2]

    @pl.when(t == 0)
    def _():
        ext[0:8] = jnp.zeros((8, width), F32)
        state[...] = jnp.zeros(state.shape, F32)

    x = xs[...].astype(F32)
    inv = lax.rsqrt(jnp.mean(x * x, axis=-1, keepdims=True) + EPSILON)
    normed = (x * inv * gain[...]).astype(BF)
    normed_o[0] = normed
    br = mm(normed, wb[...])
    ri = mm(normed, wi[...])
    br_o[0] = br
    ri_o[0] = ri.astype(BF)
    ext[8:8 + rows] = ri
    m = masks[0]
    conv = cb[...] + cw[0:1] * ri
    for k in (1, 2, 3):
        conv = conv + cw[k:k + 1] * (ext[8 - k:8 - k + rows] * m[:, k - 1:k])
    ext[0:8] = ext[rows:rows + 8]
    cv = conv.astype(BF)
    cv_o[0] = cv
    cvf = cv.astype(F32)
    pre = mm(cv, wrg[...]) + brg[...]
    rg, ig, forget, om, scale, _ = gate_values(cvf, pre, c8[...], width)
    keep = m[:, 0:1]
    first = state[0:1]
    states, last = scan_groups(forget * keep, scale * ig * cvf, first, False)
    sext[8:8 + rows] = states
    sext[7:8] = first
    sp_o[0] = sext[7:7 + rows] * keep
    state[0:1] = last
    mix = (gelu_only(br) * states).astype(BF)
    mix_o[0] = mix
    part = mm(mix, wo[...]).astype(BF)
    for i, ref in enumerate((p0, p1, p2, p3)):
        @pl.when(r == i)
        def _():
            ref[...] = part


def mixer_bwd(
    me_ref, b0, b1, b2, b3, wb, wi, cw, wrg, brg, c8, wo, masks, br_i, ri_i, cv_i, sp_i,
    gb_o, gbr_o, gri_o, n0, n1, n2, n3, dw_o, sm_o,
    gs, aext, state, zext,
):
    step = pl.program_id(0)
    t = pl.num_programs(0) - 1 - step
    r = jnp.bitwise_xor(t, me_ref[0])
    for i, ref in enumerate((b0, b1, b2, b3)):
        @pl.when(r == i)
        def _():
            gs[...] = ref[...]

    rows, width = br_i.shape[1], br_i.shape[2]

    @pl.when(step == 0)
    def _():
        aext[rows:rows + 8] = jnp.zeros((8, width), F32)
        state[...] = jnp.zeros(state.shape, F32)
        zext[:, rows:rows + 8] = jnp.zeros((3, 8, width), F32)
        dw_o[...] = jnp.zeros(dw_o.shape, F32)
        sm_o[...] = jnp.zeros(sm_o.shape, F32)

    gb = gs[...]
    gb_o[0] = gb
    gmix = mm_nt(gb, wo[...])
    gl, slope = gelu_both(br_i[0])
    cv = cv_i[0]
    cvf = cv.astype(F32)
    c8v = c8[...]
    pre = mm(cv, wrg[...]) + brg[...]
    rg, ig, forget, om, scale, inv = gate_values(cvf, pre, c8v, width)
    m = masks[0]
    carried = forget * m[:, 0:1]
    before = sp_i[0]
    igc = ig * cvf
    states = forget * before + scale * igc
    gbr = (gmix * states * slope).astype(BF)
    gbr_o[0] = gbr
    aext[0:rows] = carried
    later = aext[1:1 + rows]
    aext[rows:rows + 8] = aext[0:8]
    adj, head = scan_groups(later, gmix * gl, state[0:1], True)
    state[0:1] = head
    q = jnp.where(om > 0.001, -forget * inv, 0.0)
    gfor = adj * (before + q * igc)
    base = gfor * forget * rg
    grp = (base * (1.0 - rg) * c8v).astype(BF)
    ggp = (adj * scale * igc * (1.0 - ig)).astype(BF)
    pair = jnp.concatenate([grp, ggp], axis=1)
    dw_o[...] += mm_tn(cv, pair)
    gconv = adj * scale * ig + mm_nt(pair, wrg[...])
    ri = ri_i[0].astype(F32)
    gri = cw[0:1] * gconv
    sums = [jnp.sum(ri * gconv, axis=0, keepdims=True)]
    for k in (1, 2, 3):
        z = gconv * m[:, k - 1:k]
        zext[k - 1, 0:rows] = z
        moved = zext[k - 1, k:k + rows]
        zext[k - 1, rows:rows + 8] = z[0:8]
        gri = gri + cw[k:k + 1] * moved
        sums.append(jnp.sum(ri * moved, axis=0, keepdims=True))
    sums.append(jnp.sum(gconv, axis=0, keepdims=True))
    sums.append(jnp.sum(grp.astype(F32), axis=0, keepdims=True))
    sums.append(jnp.sum(ggp.astype(F32), axis=0, keepdims=True))
    sums.append(jnp.sum(base, axis=0, keepdims=True))
    sm_o[...] += jnp.concatenate(sums, axis=0)
    grl = gri.astype(BF)
    gri_o[0] = grl
    part = (mm_nt(gbr, wb[...]) + mm_nt(grl, wi[...])).astype(BF)
    for i, ref in enumerate((n0, n1, n2, n3)):
        @pl.when(r == i)
        def _():
            ref[...] = part


def mlp_core(
    b0, b1, b2, b3, c0, c1, c2, c3, wg, wu, wd,
    n_o, c_o, hid_o, gg_o, gu_o, xs, cs,
):
    i = pl.program_id(0)
    for k, (ref, cref) in enumerate(zip((b0, b1, b2, b3), (c0, c1, c2, c3))):
        @pl.when(i == k)
        def _():
            xs[...] = ref[...]
            cs[...] = cref[...]
    x = xs[...]
    c = cs[...]
    n_o[0] = x
    c_o[0] = c
    ga = mm(x, wg[...])
    ua = mm(x, wu[...])
    gh = mm_nt(c, wd[...])
    gl, slope = gelu_both(ga)
    hid_o[0] = (gl * ua).astype(BF)
    gg_o[0] = (gh * ua * slope).astype(BF)
    gu_o[0] = (gh * gl).astype(BF)


def mlp_back(gg, gu, wg, wu, n0, n1, n2, n3):
    i = pl.program_id(0)
    part = (mm_nt(gg[0], wg[...]) + mm_nt(gu[0], wu[...])).astype(BF)
    for k, ref in enumerate((n3, n2, n1, n0)):
        @pl.when(i == k)
        def _():
            ref[...] = part


def mid_fwd(x, keep, got, far, gain, mid_o, n_o):
    mid = x[...].astype(F32) + (keep[...].astype(F32) + got[...].astype(F32) + far[...].astype(F32))
    inv = lax.rsqrt(jnp.mean(mid * mid, axis=-1, keepdims=True) + EPSILON)
    mid_o[...] = mid
    n_o[...] = (mid * inv * gain[...]).astype(BF)


def norm_back(total, values, gain):
    inv = lax.rsqrt(jnp.mean(values * values, axis=-1, keepdims=True) + EPSILON)
    v = total * gain
    scaled = values * inv
    mean = jnp.mean(v * scaled, axis=-1, keepdims=True)
    grad = inv * (v - scaled * mean)
    return grad, jnp.sum(total * scaled, axis=0, keepdims=True)


def mid_bwd(mid, keep, got, far, gain, cot, gm_o, gb_o, gg_o):
    total = keep[...].astype(F32) + got[...].astype(F32) + far[...].astype(F32)
    grad, gsum = norm_back(total, mid[...], gain[...])
    gm = cot[...].astype(F32) + grad
    gm_o[...] = gm
    gb_o[...] = gm.astype(BF)
    gg_o[...] = gsum


def last_bwd(x, keep, got, far, gain, gm, o, gg_o):
    total = keep[...].astype(F32) + got[...].astype(F32) + far[...].astype(F32)
    grad, gsum = norm_back(total, x[...].astype(F32), gain[...])
    o[...] = gm[...] + grad
    gg_o[...] = gsum


def full(shape):
    return pl.BlockSpec(shape, lambda *_: (0,) * len(shape), pipeline_mode=pl.Buffered(1))


def full_out(shape):
    return pl.BlockSpec(shape, lambda *_: (0,) * len(shape))


def params(**more):
    return pltpu.CompilerParams(vmem_limit_bytes=VMEM_LIMIT, **more)


def cost(flops, bytes_accessed, transcendentals=0):
    return pl.CostEstimate(flops=flops, bytes_accessed=bytes_accessed, transcendentals=transcendentals)


def call_simple(kernel, outs, *args, name):
    total = sum(a.size * a.dtype.itemsize for a in args)
    return pl.pallas_call(
        kernel,
        out_shape=[jax.ShapeDtypeStruct(s, d) for s, d in outs],
        in_specs=[pl.BlockSpec(memory_space=pltpu.VMEM)] * len(args),
        out_specs=[pl.BlockSpec(memory_space=pltpu.VMEM)] * len(outs),
        compiler_params=params(),
        cost_estimate=cost(20 * args[0].size, total * 2),
        name=name,
    )(*args)


CORE = [(i, i ^ 1) for i in range(4)]
FAR = [(i, i ^ 2) for i in range(4)]


def to_core(v):
    return lax.ppermute(v, "ch", CORE)


def to_far(v):
    return lax.ppermute(v, "ch", FAR)


def gather4(own):
    far = to_far(own)
    return own, to_core(own), far, to_core(far)


def scatter4(parts):
    mine, near, far, diag = parts
    got_far = to_core(diag)
    send = (far.astype(F32) + got_far.astype(F32)).astype(BF)
    from_far = to_far(send)
    return mine, to_core(near), from_far


def dyn(g, index, size):
    return lax.dynamic_slice_in_dim(g, index * size, size, 0)


def add_low(a, b):
    return (a.astype(F32) + b.astype(F32)).astype(BF)


def put(total, piece, index):
    return lax.dynamic_update_slice_in_dim(total, piece.astype(total.dtype), index * piece.shape[0], 0)


def sum_rows(g, plan, n_rows):
    if n_rows != 8:
        return lax.psum(g.astype(F32), "rows")
    me = lax.axis_index("rows")
    y, z = me % 2, me // 2
    swap = [(i, i ^ 1) for i in range(8)]
    ring = [(i, (i + 2) % 8) for i in range(8)]
    size = g.shape[0]
    if plan == "y":
        half, blk = size // 2, size // 8
        mine = add_low(dyn(g, y, half), lax.ppermute(dyn(g, 1 - y, half), "rows", swap))
        cur = dyn(mine, (z - 1) % 4, blk)
        for s in range(3):
            cur = add_low(lax.ppermute(cur, "rows", ring), dyn(mine, (z - 2 - s) % 4, blk))
        done = put(jnp.zeros(mine.shape, BF), cur, z)
        for s in range(3):
            cur = lax.ppermute(cur, "rows", ring)
            done = put(done, cur, (z - 1 - s) % 4)
        other = lax.ppermute(done, "rows", swap)
        low = jnp.where(y == 0, done, other)
        high = jnp.where(y == 0, other, done)
        return jnp.concatenate([low, high], 0).astype(F32)
    blk, half = size // 4, size // 8
    cur = dyn(g, (z - 1) % 4, blk)
    for s in range(3):
        cur = add_low(lax.ppermute(cur, "rows", ring), dyn(g, (z - 2 - s) % 4, blk))
    mine = add_low(dyn(cur, y, half), lax.ppermute(dyn(cur, 1 - y, half), "rows", swap))
    other = lax.ppermute(mine, "rows", swap)
    cur = jnp.concatenate([jnp.where(y == 0, mine, other), jnp.where(y == 0, other, mine)], 0)
    total = put(jnp.zeros(g.shape, F32), cur, z)
    for s in range(3):
        cur = lax.ppermute(cur, "rows", ring)
        total = put(total, cur, (z - 1 - s) % 4)
    return total


def block_diag(w):
    h, d, e = w.shape
    rows = [
        jnp.concatenate([w[i] if i == j else jnp.zeros((d, e), w.dtype) for j in range(h)], axis=1)
        for i in range(h)
    ]
    return jnp.concatenate(rows, axis=0)


def body(n_rows, inputs, segment_ids, mixer_gain, branch_weight, input_weight, conv_weight, conv_bias,
         recur_weight, recur_bias, gate_weight, gate_bias, decay_param, out_weight, mlp_gain, mlp_gate,
         mlp_up, mlp_down, cotangent):
    x = inputs[0]
    cot = cotangent[0]
    rows, d = x.shape
    width = branch_weight.shape[1]
    units = mlp_gate.shape[1]
    heads, hd, _ = recur_weight.shape
    seq = segment_ids.shape[1]
    n = seq // rows
    me = lax.axis_index("ch").astype(jnp.int32)[None]
    gain1 = mixer_gain[None]
    gain2 = mlp_gain[None]

    xb = gather4(x)

    ids = segment_ids[0]
    marks = [
        (jnp.pad(ids, (k, 0), constant_values=-1)[:seq] == ids).astype(F32) for k in (1, 2, 3)
    ]
    masks = jnp.pad(jnp.stack(marks, axis=1), ((0, 0), (0, 125))).reshape(n, rows, 128)
    wrg = jnp.concatenate([block_diag(recur_weight), block_diag(gate_weight)], axis=1)
    brg = jnp.concatenate([recur_bias, gate_bias])[None]
    c8 = (-8.0 * jax.nn.softplus(decay_param))[None]
    cb = conv_bias[None]

    def tok(cols):
        return pl.BlockSpec((1, rows, cols), lambda t, me_ref: (t, 0, 0))

    def rel(cols):
        return pl.BlockSpec((1, rows, cols), lambda t, me_ref: (jnp.bitwise_xor(t, me_ref[0]), 0, 0))

    def sds(shape, dtype):
        return jax.ShapeDtypeStruct(shape, dtype)

    fwd = pl.pallas_call(
        mixer_fwd,
        grid_spec=pltpu.PrefetchScalarGridSpec(
            num_scalar_prefetch=1,
            grid=(n,),
            in_specs=[full((rows, d))] * 4 + [
                full((1, d)), full((d, width)), full((d, width)), full((4, width)), full((1, width)),
                full((width, 2 * width)), full((1, 2 * width)), full((1, width)), full((width, d)), tok(128),
            ],
            out_specs=[rel(d), rel(width), rel(width), rel(width), rel(width), rel(width)] + [full_out((rows, d))] * 4,
            scratch_shapes=[
                pltpu.VMEM((rows, d), BF), pltpu.VMEM((rows + 8, width), F32),
                pltpu.VMEM((8, width), F32), pltpu.VMEM((rows + 8, width), F32),
            ],
        ),
        out_shape=[
            sds((n, rows, d), BF), sds((n, rows, width), F32), sds((n, rows, width), BF),
            sds((n, rows, width), BF), sds((n, rows, width), F32), sds((n, rows, width), BF),
        ] + [sds((rows, d), BF)] * 4,
        compiler_params=params(),
        cost_estimate=cost(2 * seq * d * width * 4, 20_000_000, 10 * seq * width),
        name="mixer_fwd",
    )(me, *xb, gain1, branch_weight, input_weight, conv_weight, cb, wrg, brg, c8, out_weight, masks)
    normed_all, br, ri, cv, sp, mix = fwd[:6]

    cotb = gather4(cot)
    pieces = scatter4(fwd[6:])
    mid, normed2 = call_simple(
        mid_fwd, [((rows, d), F32), ((rows, d), BF)], x, *pieces, gain2, name="mid_fwd"
    )
    nb = gather4(normed2)

    def rev(cols):
        return pl.BlockSpec((1, rows, cols), lambda i: (i, 0, 0))

    n2_all, cot_all, hidden, gg, gu = pl.pallas_call(
        mlp_core,
        grid=(n,),
        in_specs=[full((rows, d))] * 8 + [full((d, units)), full((d, units)), full((units, d))],
        out_specs=[rev(d), rev(d), rev(units), rev(units), rev(units)],
        out_shape=[sds((n, rows, d), BF)] * 2 + [sds((n, rows, units), BF)] * 3,
        scratch_shapes=[pltpu.VMEM((rows, d), BF)] * 2,
        compiler_params=params(),
        cost_estimate=cost(6 * seq * d * units, 20_000_000, seq * units),
        name="mlp_core",
    )(*nb, *cotb, mlp_gate, mlp_up, mlp_down)

    def tokens(v):
        return v.reshape(n * rows, v.shape[-1])

    hidden, gg2, gu2 = tokens(hidden), tokens(gg), tokens(gu)
    n2_all, cot_all = tokens(n2_all), tokens(cot_all)
    d_down = mm_tn(hidden, cot_all).astype(BF)
    back = pl.pallas_call(
        mlp_back,
        grid=(n,),
        in_specs=[pl.BlockSpec((1, rows, units), lambda i: (n - 1 - i, 0, 0))] * 2 + [full((d, units))] * 2,
        out_specs=[full_out((rows, d))] * 4,
        out_shape=[sds((rows, d), BF)] * 4,
        compiler_params=params(),
        cost_estimate=cost(4 * seq * d * units, 10_000_000),
        name="mlp_back",
    )(gg, gu, mlp_gate, mlp_up)
    d_gate = mm_tn(n2_all, gg2).astype(BF)
    d_up = mm_tn(n2_all, gu2).astype(BF)
    t_down = sum_rows(d_down, "y", n_rows)
    t_gate = sum_rows(d_gate, "y", n_rows)
    t_up = sum_rows(d_up, "y", n_rows)

    gpieces = scatter4(back)
    gm, gb, gsum2 = call_simple(
        mid_bwd, [((rows, d), F32), ((rows, d), BF), ((1, d), F32)], mid, *gpieces, gain2, cot, name="mid_bwd"
    )
    gbb = gather4(gb)

    def tok_r(cols):
        return pl.BlockSpec((1, rows, cols), lambda s, me_ref: (n - 1 - s, 0, 0))

    def rel_r(cols):
        return pl.BlockSpec((1, rows, cols), lambda s, me_ref: (jnp.bitwise_xor(n - 1 - s, me_ref[0]), 0, 0))

    bwd = pl.pallas_call(
        mixer_bwd,
        grid_spec=pltpu.PrefetchScalarGridSpec(
            num_scalar_prefetch=1,
            grid=(n,),
            in_specs=[full((rows, d))] * 4 + [
                full((d, width)), full((d, width)), full((4, width)),
                full((width, 2 * width)), full((1, 2 * width)), full((1, width)), full((width, d)), tok_r(128),
                rel_r(width), rel_r(width), rel_r(width), rel_r(width),
            ],
            out_specs=[rel_r(d), rel_r(width), rel_r(width)] + [full_out((rows, d))] * 4 + [
                full_out((width, 2 * width)), full_out((8, width))],
            scratch_shapes=[
                pltpu.VMEM((rows, d), BF), pltpu.VMEM((rows + 8, width), F32),
                pltpu.VMEM((8, width), F32), pltpu.VMEM((3, rows + 8, width), F32),
            ],
        ),
        out_shape=[sds((n, rows, d), BF), sds((n, rows, width), BF), sds((n, rows, width), BF)]
        + [sds((rows, d), BF)] * 4 + [sds((width, 2 * width), F32), sds((8, width), F32)],
        compiler_params=params(),
        cost_estimate=cost(2 * seq * d * width * 4, 20_000_000, 10 * seq * width),
        name="mixer_bwd",
    )(me, *gbb, branch_weight, input_weight, conv_weight, wrg, brg, c8, out_weight, masks, br, ri, cv, sp)
    gb_all, gbr, gri = (tokens(v) for v in bwd[:3])
    dw, small = bwd[7], bwd[8]
    normed_all, mix = tokens(normed_all), tokens(mix)
    d_out = mm_tn(mix, gb_all).astype(BF)
    d_branch = mm_tn(normed_all, gbr).astype(BF)
    d_input = mm_tn(normed_all, gri).astype(BF)
    ipieces = scatter4(bwd[3:7])
    input_grad, gsum1 = call_simple(
        last_bwd, [((rows, d), F32), ((1, d), F32)], x, *ipieces, gain1, gm, name="last_bwd"
    )
    mlp_part = mm(hidden, mlp_down).astype(BF)
    mp = [mlp_part[i * rows:(i + 1) * rows] for i in range(n)]
    op = scatter4(mp)
    output = (mid + (op[0].astype(F32) + op[1].astype(F32) + op[2].astype(F32))).astype(BF)

    gains = jnp.concatenate([gsum1, gsum2], axis=0)
    gains = gains + to_core(gains)
    gains = gains + to_far(gains)
    gains = jnp.pad(gains.reshape(-1), (0, 6 * width - 2 * d)).reshape(6, width)
    wide = [dw[i * hd:(i + 1) * hd, j * width + i * hd:j * width + (i + 1) * hd] for i in range(heads) for j in (0, 1)]
    hw = jnp.concatenate(
        [jnp.concatenate(wide[2 * i:2 * i + 2], axis=1) for i in range(heads)], axis=0
    )
    tail = jnp.concatenate([hw, small, gains, jnp.zeros((114, width), F32)], axis=0).astype(BF)
    last = jnp.concatenate([d_branch, d_input, tail], axis=0)
    t_out = sum_rows(d_out, "z", n_rows)
    t_last = sum_rows(last, "z", n_rows)
    t_branch, t_input = t_last[:d], t_last[d:2 * d]
    th = t_last[2 * d:2 * d + heads * hd].reshape(heads, hd, 2 * hd)
    ts = t_last[2 * d + heads * hd:]
    tg = ts[8:14].reshape(-1)
    decay_grad = ts[7] * -8.0 * jax.nn.sigmoid(decay_param)
    return (
        output[None],
        input_grad[None],
        tg[:d],
        t_branch,
        t_input,
        ts[0:4],
        ts[4],
        th[:, :, :hd],
        ts[5],
        th[:, :, hd:],
        ts[6],
        decay_grad,
        t_out,
        tg[d:2 * d],
        t_gate,
        t_up,
        t_down,
    )


def solution(mesh):
    rows, ch = P("rows", "ch", None), P("ch")
    cols, lead = P(None, "ch"), P("ch", None)
    heads = P("ch", None, None)
    return jax.shard_map(
        functools.partial(body, mesh.shape["rows"]),
        mesh=mesh,
        in_specs=(rows, P("rows", None), P(), cols, cols, cols, ch, heads, ch, heads, ch, ch, lead, P(),
                  cols, cols, lead, rows),
        out_specs=(rows, rows, P(), cols, cols, cols, ch, heads, ch, heads, ch, ch, lead, P(), cols, cols, lead),
        check_vma=False,
    )
```

```python
import functools

import jax
import jax.numpy as jnp
from jax import lax
from jax.experimental import pallas as pl
from jax.experimental.pallas import tpu as pltpu
from jax.sharding import PartitionSpec as P

EPSILON = 1e-06
BF = jnp.bfloat16
F32 = jnp.float32
MIB = 1024 * 1024
SCALE = 0.0
Q_FIRST = True
GELU_C = 0.7978845608028654
GELU_A = 0.044715


def mm(a, b):
    return lax.dot_general(a, b, (((1,), (0,)), ((), ())), preferred_element_type=F32)


def mm_nt(a, b):
    return lax.dot_general(a, b, (((1,), (1,)), ((), ())), preferred_element_type=F32)


def mm_tn(a, b):
    return lax.dot_general(a, b, (((0,), (0,)), ((), ())), preferred_element_type=F32)


def sigmoid(v):
    return 0.5 * jnp.tanh(0.5 * v) + 0.5


def gelu_both(v):
    sq = v * v
    th = jnp.tanh(GELU_C * v * (1.0 + GELU_A * sq))
    half = 0.5 * th + 0.5
    slope = half + (0.5 * GELU_C) * v * (1.0 - th * th) * (1.0 + (3.0 * GELU_A) * sq)
    return v * half, slope


def gelu_only(v):
    th = jnp.tanh(GELU_C * v * (1.0 + GELU_A * (v * v)))
    return v * (0.5 * th + 0.5)


def scan_groups(mult, add, start, back):
    rows, cols = mult.shape
    a = mult.reshape(rows // 8, 8, cols)
    d = add.reshape(rows // 8, 8, cols)
    sub = lax.broadcasted_iota(jnp.int32, (1, 8, cols), 1)
    for k in (1, 2, 4):
        ok = sub < 8 - k if back else sub >= k
        turn = 8 - k if back else k
        d = d + a * jnp.where(ok, pltpu.roll(d, turn, 1), 0.0)
        a = a * jnp.where(ok, pltpu.roll(a, turn, 1), 1.0)
    state = start
    got = [None] * (rows // 8)
    order = range(rows // 8)
    for g in reversed(order) if back else order:
        now = d[g] + a[g] * state
        state = now[0:1] if back else now[7:8]
        got[g] = now
    return jnp.concatenate(got, axis=0), state


def gate_values(conv, pre, c8, width):
    rg = sigmoid(pre[:, :width])
    ig = sigmoid(pre[:, width:])
    forget = jnp.exp(c8 * rg)
    om = 1.0 - forget * forget
    top = jnp.maximum(om, 0.001)
    inv = lax.rsqrt(top)
    return rg, ig, forget, om, top * inv, inv


def begin(sem, first, *pairs):
    copies = [pltpu.make_async_copy(src, dst, sem.at[first + k]) for k, (src, dst) in enumerate(pairs)]
    for c in copies:
        c.start()
    return copies


def wait(copies):
    for c in copies:
        c.wait()


def project(x, gain, wb, wi):
    x = x.astype(F32)
    inv = lax.rsqrt(jnp.mean(x * x, axis=-1, keepdims=True) + EPSILON)
    normed = (x * inv * gain).astype(BF)
    return normed, mm(normed, wb), mm(normed, wi)


def mixer_pre(b0, b1, wb_h, wi_h, gain, normed_h, br_h, ri_h, xb, wb, wi, normed_v, br_v, ri_v, sem_in, sem_out):
    first = begin(sem_in, 0, (b0, xb.at[0]), (wb_h, wb), (wi_h, wi))
    second = begin(sem_in, 3, (b1, xb.at[1]))
    for i, ready in enumerate((first, second)):
        wait(ready)
        normed_v[i], br_v[i], ri_v[i] = project(xb[i], gain[...], wb[...], wi[...])
    wait(begin(sem_out, 0, (normed_v, normed_h), (br_v, br_h), (ri_v, ri_h)))


def mixer_fwd(
    me_ref, b2, b3, wb_h, wi_h, br01, ri01, wrg_h, masks_h, wo_h, gain, cw, cb, brg, c8,
    normed_h, br_h, ri_h, cv_h, sp_h, mix_h, p0, p2, p3, p1,
    xb, wb, wi, wrg, masks, wo, normed_v, br_v, ri_s, ri_v, cv_v, sp_v, mix_v, ext, sext, sem_in, sem_out,
):
    n, rows, width = br_v.shape
    first = begin(sem_in, 0, (b2, xb.at[0]), (wb_h, wb), (wi_h, wi))
    second = begin(sem_in, 3, (b3, xb.at[1]))
    later = begin(sem_in, 4, (ri01, ri_s.at[0:2]), (wrg_h, wrg), (masks_h, masks), (br01, br_v.at[0:2]), (wo_h, wo))
    for i, ready in enumerate((first, second)):
        wait(ready)
        normed_v[i], br_v[2 + i], ri_s[2 + i] = project(xb[i], gain[...], wb[...], wi[...])
    out = begin(sem_out, 0, (normed_v, normed_h), (br_v.at[2:4], br_h))
    ext[0:8] = jnp.zeros((8, width), F32)
    wait(later)

    def block(t, first):
        r = jnp.bitwise_xor(t, me_ref[0])
        ri = ri_s[r]
        ri_v[r] = ri.astype(BF)
        ext[8:8 + rows] = ri
        m = masks[t]
        conv = cb[...] + cw[0:1] * ri
        for k in (1, 2, 3):
            conv = conv + cw[k:k + 1] * (ext[8 - k:8 - k + rows] * m[:, k - 1:k])
        ext[0:8] = ext[rows:rows + 8]
        cv = conv.astype(BF)
        cv_v[r] = cv
        cvf = cv.astype(F32)
        pre = mm(cv, wrg[...]) + brg[...]
        rg, ig, forget, om, scale, _ = gate_values(cvf, pre, c8[...], width)
        keep = m[:, 0:1]
        states, last = scan_groups(forget * keep, scale * ig * cvf, first, False)
        sext[8:8 + rows] = states
        sext[7:8] = first
        sp_v[r] = sext[7:7 + rows] * keep
        mix_v[r] = (gelu_only(br_v[r]) * states).astype(BF)
        return last

    lax.fori_loop(0, n, block, jnp.zeros((1, width), F32))
    out += begin(sem_out, 2, (ri_v, ri_h), (cv_v, cv_h), (sp_v, sp_h), (mix_v, mix_h))
    for i, ref in ((3, p3), (1, p1), (2, p2), (0, p0)):
        ref[...] = mm(mix_v[i], wo[...]).astype(BF)
    wait(out)


def mixer_bwd(
    me_ref, y_ref, z_ref, b0, b1, b2, b3, wo_h, br01, br23, cv_h, sp_h, ri_h, wrg_h, masks_h, mix_h, normed01, normed23,
    wb_h, wi_h, cw, brg, c8, gain2,
    n0, n2, n31, pk_o, ps_o, qk_o, qs_o,
    gb, wo, br, cv_v, sp, ri_v, wrg, masks, mix, normed, wb, wi,
    gm_s, pair_s, gbr_v, gri_v, p_v, last_v, sm_v, aext, zext, sem_in, sem_out,
):
    n, rows, width = br.shape
    d = gb.shape[2]
    first_in = begin(sem_in, 0, (wo_h, wo), (b0, gb.at[0]), (b1, gb.at[1]), (b2, gb.at[2]), (b3, gb.at[3]))
    next_in = begin(sem_in, 5, (br01, br.at[0:2]), (br23, br.at[2:4]), (cv_h, cv_v), (sp_h, sp), (ri_h, ri_v),
                    (wrg_h, wrg), (masks_h, masks))
    last_in = begin(sem_in, 12, (mix_h, mix), (normed01, normed.at[0:2]), (normed23, normed.at[2:4]), (wb_h, wb),
                    (wi_h, wi))
    wait(first_in)
    for i in range(n):
        gm_s[i] = mm_nt(gb[i], wo[...])
    aext[rows:rows + 8] = jnp.zeros((8, width), F32)
    zext[:, rows:rows + 8] = jnp.zeros((3, 8, width), F32)
    sm_v[...] = jnp.zeros(sm_v.shape, F32)
    wait(next_in)

    def block(step, after):
        t = n - 1 - step
        r = jnp.bitwise_xor(t, me_ref[0])
        gmix = gm_s[r]
        gl, slope = gelu_both(br[r])
        cv = cv_v[r]
        cvf = cv.astype(F32)
        c8v = c8[...]
        pre = mm(cv, wrg[...]) + brg[...]
        rg, ig, forget, om, scale, inv = gate_values(cvf, pre, c8v, width)
        m = masks[t]
        before = sp[r]
        igc = ig * cvf
        states = forget * before + scale * igc
        gbr_v[r] = (gmix * states * slope).astype(BF)
        aext[0:rows] = forget * m[:, 0:1]
        later = aext[1:1 + rows]
        aext[rows:rows + 8] = aext[0:8]
        adj, head = scan_groups(later, gmix * gl, after, True)
        q = jnp.where(om > 0.001, -forget * inv, 0.0)
        gfor = adj * (before + q * igc)
        base = gfor * forget * rg
        grp = (base * (1.0 - rg) * c8v).astype(BF)
        ggp = (adj * scale * igc * (1.0 - ig)).astype(BF)
        pair = jnp.concatenate([grp, ggp], axis=1)
        pair_s[r] = pair
        gconv = adj * scale * ig + mm_nt(pair, wrg[...])
        ri = ri_v[r].astype(F32)
        gri = cw[0:1] * gconv
        sums = [jnp.sum(ri * gconv, axis=0, keepdims=True)]
        for k in (1, 2, 3):
            z = gconv * m[:, k - 1:k]
            zext[k - 1, 0:rows] = z
            moved = zext[k - 1, k:k + rows]
            zext[k - 1, rows:rows + 8] = z[0:8]
            gri = gri + cw[k:k + 1] * moved
            sums.append(jnp.sum(ri * moved, axis=0, keepdims=True))
        sums.append(jnp.sum(gconv, axis=0, keepdims=True))
        sums.append(jnp.sum(grp.astype(F32), axis=0, keepdims=True))
        sums.append(jnp.sum(ggp.astype(F32), axis=0, keepdims=True))
        sums.append(jnp.sum(base, axis=0, keepdims=True))
        sm_v[...] += jnp.concatenate(sums, axis=0)
        gri_v[r] = gri.astype(BF)
        return head

    lax.fori_loop(0, n, block, jnp.zeros((1, width), F32))
    wait(last_in)
    out = []
    gain1 = jnp.zeros((1, d), F32)
    for k, (i, ref) in enumerate(((3, n31.at[0]), (1, n31.at[1]), (2, n2), (0, n0))):
        part = mm_nt(gbr_v[i], wb[...]) + mm_nt(gri_v[i], wi[...])
        p_v[i] = part.astype(BF)
        out += begin(sem_out, k, (p_v.at[i], ref))
        gain1 = gain1 + jnp.sum(part * normed[i].astype(F32), axis=0, keepdims=True)

    def flat(ref):
        return ref[...].reshape(n * rows, ref.shape[2])

    def as_rows(v):
        v = jnp.concatenate([v, jnp.zeros((1, 3 * width - d), F32)], axis=1)
        return [v[:, i * width:(i + 1) * width] for i in range(3)]

    for k, g in ((0, gbr_v), (1, gri_v)):
        last_v[k, 0:d] = mm_tn(flat(normed), flat(g)).astype(BF)
    dw = mm_tn(flat(cv_v), flat(pair_s))
    hd = width // 2
    left = lax.broadcasted_iota(jnp.int32, (hd, width), 1) < hd
    rest = last_v.shape[1] - d - hd - d // 2
    few = [sm_v[...]] + as_rows(gain1) + as_rows(gain2[...])
    tails = (jnp.concatenate(few + [jnp.zeros((rest - 14, width), F32)], axis=0), jnp.zeros((rest, width), F32))
    d_out = mm_tn(flat(gb), flat(mix)).astype(BF)
    for k in (0, 1):
        mine = dw[:, k * width:(k + 1) * width]
        last_v[k, d:d + hd] = jnp.where(left, mine[:hd], mine[hd:]).astype(BF)
        last_v[k, d + hd:d + hd + rest] = tails[k].astype(BF)
        last_v[k, d + hd + rest:] = d_out[k * (d // 2):(k + 1) * (d // 2)]
    cut = last_v.shape[1] // 2
    low, high = last_v.at[:, 0:cut], last_v.at[:, cut:2 * cut]
    for part in (0, 1):
        here, there = (low, high) if part == 0 else (high, low)

        @pl.when(y_ref[0] == part)
        def _():
            wait(begin(sem_out, 4, (here.at[0], pk_o), (there.at[0], ps_o)))

        @pl.when(z_ref[0] == part)
        def _():
            wait(begin(sem_out, 6, (here.at[1], qk_o), (there.at[1], qs_o)))
    wait(out)


def mlp_blocks(xb, cot, wg, wu, wd, hid, gg, gu, p_v, ready, base):
    for i in range(xb.shape[0]):
        wait(ready[i])
        x = xb[i]
        ga = mm(x, wg[...])
        if i == 0:
            wait(ready[-1][:1])
        ua = mm(x, wu[...])
        if i == 0:
            wait(ready[-1][1:])
        gh = mm_nt(cot[base + i], wd[...])
        gl, slope = gelu_both(ga)
        hid[base + i] = (gl * ua).astype(BF)
        gg[i] = (gh * ua * slope).astype(BF)
        gu[i] = (gh * gl).astype(BF)
    for i in reversed(range(xb.shape[0])):
        p_v[i] = (mm_nt(gg[i], wg[...]) + mm_nt(gu[i], wu[...])).astype(BF)


def mlp_pre(
    b0, b1, c0, c1, wg_h, wu_h, wd_h, hid_h, gg_h, gu_h, n0, n1,
    xb, cot, wg, wu, wd, hid, gg, gu, p_v, sem_in, sem_out,
):
    first = begin(sem_in, 0, (b0, xb.at[0]), (wg_h, wg))
    then = begin(sem_in, 2, (wu_h, wu), (c0, cot.at[0]), (wd_h, wd))
    second = begin(sem_in, 5, (b1, xb.at[1]), (c1, cot.at[1]))
    mlp_blocks(xb, cot, wg, wu, wd, hid, gg, gu, p_v, (first, second, then), 0)
    wait(begin(sem_out, 0, (hid, hid_h), (gg, gg_h), (gu, gu_h), (p_v.at[1], n1), (p_v.at[0], n0)))


def mlp_main(
    y_ref, b2, b3, c0, c1, c2, c3, hid01, n1, wg_h, wu_h, wd_h, hid_h, gg_h, gu_h, n2, n31, dk_o, ds_o,
    xb, cot, wg, wu, wd, hid, gg, gu, p_v, dd, sem_in, sem_out,
):
    rows, units = hid.shape[1:]
    first = begin(sem_in, 0, (b2, xb.at[0]), (wg_h, wg))
    then = begin(sem_in, 2, (wu_h, wu), (c2, cot.at[2]), (wd_h, wd))
    second = begin(sem_in, 5, (b3, xb.at[1]), (c3, cot.at[3]))
    last = begin(sem_in, 7, (c0, cot.at[0]), (c1, cot.at[1]), (hid01, hid.at[0:2]), (n1, n31.at[1]))
    mlp_blocks(xb, cot, wg, wu, wd, hid, gg, gu, p_v, (first, second, then), 2)
    n31[0] = p_v[1]
    n2[...] = p_v[0]
    out = begin(sem_out, 0, (hid.at[2:4], hid_h), (gg, gg_h), (gu, gu_h))
    wait(last)
    call_ = cot[...].reshape(4 * rows, cot.shape[2])
    hall = hid[...].reshape(4 * rows, units)
    half = units // 2
    for part in (0, 1):
        dd[part] = mm_tn(hall[:, part * half:(part + 1) * half], call_).astype(BF)
    for part in (0, 1):
        @pl.when(y_ref[0] == part)
        def _():
            wait(begin(sem_out, 5, (dd.at[part], dk_o), (dd.at[1 - part], ds_o)))
    wait(out)


def mlp_post(
    y_ref, z_ref, b0, b1, b2, b3, gg01, gg23, gu01, gu23, hid01, hid23, wd_h, gk_o, gs_o, uk_o, us_o, m0, m2, m31,
    xb, gg, gu, hid, wd, dg, du, p_v, sem_in, sem_out,
):
    n, rows, units = hid.shape
    first = begin(sem_in, 0, (b0, xb.at[0]), (b1, xb.at[1]), (b2, xb.at[2]), (b3, xb.at[3]),
                  (gg01, gg.at[0:2]), (gg23, gg.at[2:4]))
    second = begin(sem_in, 6, (gu01, gu.at[0:2]), (gu23, gu.at[2:4]))
    third = begin(sem_in, 8, (hid01, hid.at[0:2]), (hid23, hid.at[2:4]), (wd_h, wd))

    def flat(ref):
        return ref[...].reshape(n * rows, ref.shape[2])

    wait(first)
    xall = flat(xb)
    half = dg.shape[1]
    for part in (0, 1):
        dg[part] = mm_tn(xall[:, part * half:(part + 1) * half], flat(gg)).astype(BF)
    wait(second)
    for part in (0, 1):
        du[part] = mm_tn(xall[:, part * half:(part + 1) * half], flat(gu)).astype(BF)
    for part in (0, 1):
        @pl.when(y_ref[0] == part)
        def _():
            begin(sem_out, 4, (dg.at[part], gk_o), (dg.at[1 - part], gs_o))

        @pl.when(z_ref[0] == part)
        def _():
            begin(sem_out, 6, (du.at[part], uk_o), (du.at[1 - part], us_o))
    out = []
    wait(third)
    for k, (i, ref) in enumerate(((3, m31.at[0]), (1, m31.at[1]), (2, m2), (0, m0))):
        p_v[i] = mm(hid[i], wd[...]).astype(BF)
        out += begin(sem_out, k, (p_v.at[i], ref))
    wait(out)
    wait([pltpu.make_async_copy(v.at[0], o, sem_out.at[4 + k])
          for k, (v, o) in enumerate(((dg, gk_o), (dg, gs_o), (du, uk_o), (du, us_o)))])


def add_two(a, b, got_a, got_b, send_o, own_o):
    send_o[...] = plus(a[...], got_a[...]).astype(BF)
    own_o[...] = plus(b[...], got_b[...]).astype(BF)


def add_pair(a, b, got, send_o, own_o):
    send_o[...] = plus(a[...], got[0]).astype(BF)
    own_o[...] = plus(b[...], got[1]).astype(BF)


def mid_fwd(x, own, far, gain, mid_o, n_o):
    mid = x[...].astype(F32) + plus(own[...], far[...])
    inv = lax.rsqrt(jnp.mean(mid * mid, axis=-1, keepdims=True) + EPSILON)
    mid_o[...] = mid
    n_o[...] = (mid * inv * gain[...]).astype(BF)


def norm_back(total, values, gain):
    inv = lax.rsqrt(jnp.mean(values * values, axis=-1, keepdims=True) + EPSILON)
    v = total * gain
    scaled = values * inv
    mean = jnp.mean(v * scaled, axis=-1, keepdims=True)
    grad = inv * (v - scaled * mean)
    return grad, jnp.sum(total * scaled, axis=0, keepdims=True)


def mid_bwd(mid, own, far, gain, cot, gm_o, gb_o, gg_o):
    grad, gsum = norm_back(plus(own[...], far[...]), mid[...], gain[...])
    gm = cot[...].astype(F32) + grad
    gm_o[...] = gm
    gb_o[...] = gm.astype(BF)
    gg_o[...] = gsum


def last_bwd(x, own, far, gain, gm, o):
    grad, _ = norm_back(plus(own[...], far[...]), x[...].astype(F32), gain[...])
    o[...] = gm[...] + grad


def cost(us):
    return pl.CostEstimate(flops=1 + int(us * 1.15e9), bytes_accessed=0, transcendentals=0)


HBM, VMEM, SMEM = pltpu.HBM, pltpu.VMEM, pltpu.SMEM


def call(kernel, outs, *args, name, us, mib, places, out, scratch=()):
    spec = {"h": HBM, "v": VMEM, "s": SMEM, "a": pl.ANY}
    args = [
        pltpu.with_memory_space_constraint(a, VMEM if p == "v" else HBM) if p in "hv" else a
        for p, a in zip(places, args, strict=True)
    ]
    return pl.pallas_call(
        kernel,
        out_shape=[(VMEM if p == "v" else HBM)(*o) for p, o in zip(out, outs, strict=True)],
        in_specs=[pl.BlockSpec(memory_space=spec[p]) if p in spec else pl.BlockSpec() for p in places],
        out_specs=[pl.BlockSpec(memory_space=spec[p]) if p in spec else pl.BlockSpec() for p in out],
        scratch_shapes=list(scratch),
        compiler_params=pltpu.CompilerParams(vmem_limit_bytes=mib * MIB),
        cost_estimate=cost(us),
        name=name,
    )(*args)


CORE = [(i, i ^ 1) for i in range(4)]
FAR = [(i, i ^ 2) for i in range(4)]


def to_core(v):
    return lax.ppermute(v, "ch", CORE)


def to_far(v):
    return lax.ppermute(v, "ch", FAR)


class Order:
    def __init__(self):
        self.last = None

    def run(self, work, *values):
        if self.last is not None:
            values = lax.optimization_barrier((*values, *self.last))[:len(values)]
        got = work(*values)
        self.last = tuple(got) if isinstance(got, (tuple, list)) else (got,)
        return got

    def gate(self, value):
        return lax.optimization_barrier((value, *self.last))[0]

    def take(self, value):
        return self.run(lambda v: (v,), value)[0]


def dyn(g, index, size):
    return lax.dynamic_slice_in_dim(g, index * size, size, 0)


def plus(a, b):
    return a.astype(F32) + b.astype(F32)


def add_low(a, b):
    return plus(a, b).astype(BF)


def put(total, piece, index):
    return lax.dynamic_update_slice_in_dim(total, piece.astype(total.dtype), index * piece.shape[0], 0)


Y = [(i, i ^ 1) for i in range(8)]
Z1 = [(i, i ^ 2) for i in range(8)]
Z2 = [(i, i ^ 4) for i in range(8)]
def both(low, a, b):
    return jnp.concatenate([jnp.where(low, a, b), jnp.where(low, b, a)], 0)


def sum_rows_plain(keep, send, ends):
    return ends(lax.psum(jnp.concatenate([keep, send], 0).astype(F32), "rows"))
    yield


INWARD = [(0, 2), (1, 3), (6, 4), (7, 5)]
MIDDLE = [(2, 4), (3, 5), (4, 2), (5, 3)]
OUTWARD = [(2, 0), (3, 1), (4, 6), (5, 7)]


def send_on(value, pairs, order):
    if (yield "ready"):
        value = order.gate(value)
    got = lax.ppermute(value, "rows", pairs)
    yield "sent"
    return order.take(got)


def sum_rows_halves(keep, send, order, way, ends):
    me = lax.axis_index("rows")
    y, z = (Y, me % 2), (Z1, (me // 2) % 2)
    stages = ((y, z) if way == "y" else (z, y)) + ((Z2, me // 4),)
    got = yield from send_on(send, stages[0][0], order)
    yield "came"
    for pairs, bit in stages[1:]:
        half = keep.shape[0] // 2

        def split(a, b, bit=bit, half=half):
            return (add_low(dyn(a, 1 - bit, half), dyn(b, 1 - bit, half)), add_low(dyn(a, bit, half), dyn(b, bit, half)))

        send, keep = order.run(split, keep, got)
        got = yield from send_on(send, pairs, order)
        yield "came"
    cur = order.run(add_low, keep, got)
    for pairs, bit in stages[::-1]:
        got = yield from send_on(cur, pairs, order)
        yield "came"
        if pairs is stages[0][0]:
            return order.run(lambda a, b: ends(both(bit == 0, a, b)), cur, got)
        cur = order.run(lambda a, b, bit=bit: both(bit == 0, a, b), cur, got)


def sum_rows_line(keep, send, order, ends):
    me = lax.axis_index("rows")
    y, z = me % 2, me // 2
    inner = (z == 1) | (z == 2)
    got = yield from send_on(send, Y, order)
    yield "came"
    cur = order.run(add_low, keep, got)
    for pairs in (INWARD, MIDDLE):
        got = yield from send_on(cur, pairs, order)
        yield "came"
        cur = order.run(add_low, cur, got)
    got = yield from send_on(cur, OUTWARD, order)
    yield "came"
    cur = order.run(lambda a, b: jnp.where(inner, a, b), cur, got)
    got = yield from send_on(cur, Y, order)
    yield "came"
    return order.run(lambda a, b: ends(both(y == 0, a, b)), cur, got)


class Chain:
    def __init__(self, steps):
        self.steps, self.value, self.state, self.held = steps, None, None, False
        self.go()

    def step(self, first=False):
        try:
            self.state = self.steps.send(None if self.state is None else self.held)
            self.held = False
        except StopIteration as end:
            self.state, self.value = "done", end.value

    def to(self, state):
        if self.state == "done":
            return
        self.step()
        while self.state not in (state, "done"):
            self.step()
        self.held = state == "ready"

    def come(self):
        if self.state == "sent":
            self.to("came")

    def go(self):
        self.to("sent")

    def finish(self):
        while self.state != "done":
            self.go()
        return self.value


def block_diag(w):
    h, d, e = w.shape
    rows = [
        jnp.concatenate([w[i] if i == j else jnp.zeros((d, e), w.dtype) for j in range(h)], axis=1)
        for i in range(h)
    ]
    return jnp.concatenate(rows, axis=0)


def body(n_rows, inputs, segment_ids, mixer_gain, branch_weight, input_weight, conv_weight, conv_bias,
         recur_weight, recur_bias, gate_weight, gate_bias, decay_param, out_weight, mlp_gain, mlp_gate,
         mlp_up, mlp_down, cotangent):
    x = inputs[0]
    cot = cotangent[0]
    rows, d = x.shape
    width = branch_weight.shape[1]
    units = mlp_gate.shape[1]
    heads, hd, _ = recur_weight.shape
    seq = segment_ids.shape[1]
    n = seq // rows
    me = lax.axis_index("ch").astype(jnp.int32)[None]
    gain1 = mixer_gain[None]
    gain2 = mlp_gain[None]
    order = Order()
    row = lax.axis_index("rows").astype(jnp.int32)[None]
    y_half = row % 2 if n_rows == 8 else jnp.zeros((1,), jnp.int32)
    z_half = (row // 2) % 2 if n_rows == 8 else jnp.zeros((1,), jnp.int32)

    def total(keep, send, way, ends):
        if n_rows != 8:
            return Chain(sum_rows_plain(keep, send, ends))
        if way == "line":
            return Chain(sum_rows_line(keep, send, order, ends))
        return Chain(sum_rows_halves(keep, send, order, way, ends))

    x_far, x_near = to_far(x), to_core(x)

    def tables(ids, rw, gw, rb, gb_, dp):
        marks = [
            (jnp.pad(ids, (k, 0), constant_values=-1)[:seq] == ids).astype(F32) for k in (1, 2, 3)
        ]
        masks = jnp.pad(jnp.stack(marks, axis=1), ((0, 0), (0, 125))).reshape(n, rows, 128)
        wrg = jnp.concatenate([block_diag(rw), block_diag(gw)], axis=1)
        return masks, wrg, jnp.concatenate([rb, gb_])[None], (-8.0 * jax.nn.softplus(dp))[None]

    masks, wrg, brg, c8 = order.run(
        tables, segment_ids[0], recur_weight, gate_weight, recur_bias, gate_bias, decay_param
    )
    cb = conv_bias[None]
    blk, narrow, wide = (rows, d), (n, rows, width), (n, rows, units)
    four, two = (n, rows, d), (2, rows, d)
    narrow2, wide2 = (2, rows, width), (2, rows, units)
    dma = pltpu.SemaphoreType.DMA
    normed01, br01, ri01 = order.run(
        functools.partial(
            call, mixer_pre, [(two, BF), (narrow2, F32), (narrow2, F32)], name="mixer_pre", us=0, mib=20,
            places="aahhi", out="hhh", scratch=[
                VMEM(two, BF), VMEM((d, width), BF), VMEM((d, width), BF), VMEM(two, BF), VMEM(narrow2, F32),
                VMEM(narrow2, F32), dma((4,)), dma((3,)),
            ]),
        x, x_near, branch_weight, input_weight, gain1)
    x_far = order.take(x_far)
    x_diag = to_core(x_far)
    cot_far = to_far(cot)
    x_diag = order.take(x_diag)
    fwd = order.run(
        functools.partial(
            call, mixer_fwd,
            [(two, BF), (narrow2, F32), (narrow, BF), (narrow, BF), (narrow, F32), (narrow, BF)] + [(blk, BF)] * 4,
            name="mixer_fwd", us=0, mib=30, places="saahhhhhhhiiiii", out="h" * 6 + "vvvv", scratch=[
                VMEM(two, BF), VMEM((d, width), BF), VMEM((d, width), BF), VMEM((width, 2 * width), BF),
                VMEM((n, rows, 128), F32), VMEM((width, d), BF), VMEM(two, BF), VMEM(narrow, F32),
                VMEM(narrow, F32), VMEM(narrow, BF), VMEM(narrow, BF), VMEM(narrow, F32), VMEM(narrow, BF),
                VMEM((rows + 8, width), F32), VMEM((rows + 8, width), F32), dma((9,)), dma((6,)),
            ]),
        me, x_far, x_diag, branch_weight, input_weight, br01, ri01, wrg, masks, out_weight, gain1, conv_weight, cb,
        brg, c8)
    normed23, br23, ri, cv, sp, mix = fwd[:6]
    cot_far = order.take(cot_far)

    def near_half(own, far, pair):
        got = to_core(pair)
        return order.run(
            functools.partial(call, add_pair, [(blk, BF)] * 2, name="add_pair", us=0, mib=6, places="iii", out="vv"),
            far, own, got)

    send, own = order.run(
        functools.partial(call, add_two, [(blk, BF)] * 2, name="add_two", us=0, mib=6, places="vvii", out="vv"),
        fwd[7], fwd[6], to_core(fwd[8]), to_core(fwd[9]))
    far = to_far(send)
    cot_near, cot_diag = to_core(cot), to_core(cot_far)
    cot_near = order.take(cot_near)
    cot_diag = order.take(cot_diag)
    mid, normed2 = order.run(functools.partial(
        call, mid_fwd, [(blk, F32), (blk, BF)], name="mid_fwd", us=0, mib=8, places="ivvi", out="iv"),
        x, own, far, gain2)
    n_far, n_near = to_far(normed2), to_core(normed2)
    n_near = order.take(n_near)
    mlp_scratch = [
        VMEM((d, units), BF), VMEM((d, units), BF), VMEM((units, d), BF)]
    hid01, gg01, gu01, g0, g1 = order.run(
        functools.partial(
            call, mlp_pre, [(wide2, BF)] * 3 + [(blk, BF)] * 2, name="mlp_pre", us=0, mib=30, places="aahhhhh",
            out="h" * 5, scratch=[VMEM(two, BF), VMEM(two, BF)] + mlp_scratch + [VMEM(wide2, BF)] * 3 + [
                VMEM(two, BF), dma((7,)), dma((5,))]),
        normed2, n_near, cot, cot_near, mlp_gate, mlp_up, mlp_down)
    n_far = order.take(n_far)
    n_diag = order.take(to_core(n_far))
    hid23, gg23, gu23, g2, g31, down_keep, down_send = order.run(
        functools.partial(
            call, mlp_main, [(wide2, BF)] * 3 + [(blk, BF), (two, BF)] + [((units // 2, d), BF)] * 2, name="mlp_main",
            us=0, mib=26, places="saahhhhhhhhh", out="hhhvvhh",
            scratch=[VMEM(two, BF), VMEM(four, BF)] + mlp_scratch + [VMEM(wide, BF), VMEM(wide2, BF), VMEM(wide2, BF)] + [
                VMEM(two, BF), VMEM((2, units // 2, d), BF), dma((11,)), dma((7,))]),
        y_half, n_far, n_diag, cot, cot_near, cot_far, cot_diag, hid01, g1, mlp_gate, mlp_up, mlp_down)
    s_down = total(down_keep, down_send, "line", lambda v: v.astype(F32))
    g_send, g_own = near_half(g0, g2, g31)
    from_far = to_far(g_send)
    post = order.run(
        functools.partial(
            call, mlp_post, [((d // 2, units), BF)] * 4 + [(blk, BF), (blk, BF), (two, BF)], name="mlp_post", us=0,
            mib=26, places="ssaaaahhhhhhh", out="h" * 7, scratch=[
                VMEM(four, BF), VMEM(wide, BF), VMEM(wide, BF), VMEM(wide, BF), VMEM((units, d), BF),
                VMEM((2, d // 2, units), BF), VMEM((2, d // 2, units), BF), VMEM(four, BF), dma((11,)), dma((8,)),
            ]),
        y_half, z_half, normed2, n_near, n_far, n_diag, gg01, gg23, gu01, gu23, hid01, hid23, mlp_down)
    s_gate = total(post[0], post[1], "line", lambda v: v.astype(F32))
    s_up = total(post[2], post[3], "z", lambda v: v.astype(F32))
    s_down.go()
    gm, gb, gsum2 = order.run(functools.partial(
        call, mid_bwd, [(blk, F32), (blk, BF), ((1, d), F32)], name="mid_bwd", us=10, mib=8, places="ivvii", out="ivi"),
        mid, g_own, from_far, gain2, cot)
    g_near, g_far = to_core(gb), to_far(gb)
    s_up.go()
    s_gate.go()
    g_far = order.take(g_far)
    g_diag = to_core(g_far)
    g_near = order.take(g_near)
    g_diag = order.take(g_diag)
    s_down.go()

    last_rows = d + hd + 64 + d // 2
    bwd = order.run(
        functools.partial(
            call, mixer_bwd, [(blk, BF), (blk, BF), (two, BF)] + [((last_rows // 2, width), BF)] * 4,
            name="mixer_bwd", us=0, mib=38, places="sss" + "a" * 4 + "h" * 13 + "iiii", out="h" * 7, scratch=[
                VMEM(four, BF), VMEM((width, d), BF), VMEM(narrow, F32), VMEM(narrow, BF), VMEM(narrow, F32),
                VMEM(narrow, BF), VMEM((width, 2 * width), BF), VMEM((n, rows, 128), F32), VMEM(narrow, BF),
                VMEM(four, BF), VMEM((d, width), BF), VMEM((d, width), BF),
                VMEM(narrow, F32), VMEM((n, rows, 2 * width), BF), VMEM(narrow, BF), VMEM(narrow, BF), VMEM(four, BF),
                VMEM((2, last_rows, width), BF), VMEM((8, width), F32),
                VMEM((rows + 8, width), F32), VMEM((3, rows + 8, width), F32), dma((17,)), dma((8,)),
            ]),
        me, y_half, y_half if Q_FIRST else z_half, gb, g_near, g_far, g_diag, out_weight, br01, br23, cv, sp, ri, wrg, masks, mix, normed01,
        normed23, branch_weight, input_weight, conv_weight, brg, c8, gsum2)
    for s in (s_up, s_gate, s_down):
        s.come()

    def heads_of(v):
        return jnp.stack([v[:, i * hd:(i + 1) * hd] for i in range(heads)], axis=0).astype(F32)

    def ends(v):
        wide = v[:d].astype(F32)
        return wide, heads_of(v[d:d + hd]), v[d + hd:d + hd + 14].astype(F32), v[-(d // 2):]

    s_p = total(bwd[3], bwd[4], "line", ends)
    s_q = total(bwd[5], bwd[6], "line", ends)
    def sum_ch(parts, finish):
        own, far, pair = (order.gate(v) for v in parts)
        got = to_core(pair)
        yield "sent"
        got = order.take(got)
        yield "came"
        send, own = order.run(
            functools.partial(call, add_pair, [(blk, BF)] * 2, name="add_pair", us=0, mib=6, places="iii", out="vv"),
            far, own, got)
        far = to_far(send)
        yield "sent"
        far = order.take(far)
        yield "came"
        return order.run(finish, own, far)

    def last(own, far):
        return call(
            last_bwd, [(blk, F32)], x, own, far, gain1, gm, name="last_bwd", us=0, mib=8, places="ivvii", out="i")[0]

    queue = [s_up, s_gate, s_down, s_p, s_q]
    later = [lambda: Chain(sum_ch(bwd[:3], last)),
             lambda: Chain(sum_ch(post[4:], lambda own, far: (mid + plus(own, far)).astype(BF)))]
    others = []
    while queue:
        chain = queue.pop(0)
        chain.go()
        if chain.state != "done":
            queue.append(chain)
        elif later:
            queue.append(later.pop(0)())
            others.append(queue[-1])
    input_grad, output = (c.value for c in others)
    t_p = s_p.finish()
    ts = t_p[2]
    gains = jnp.stack([ts[8:11].reshape(-1)[:d], ts[11:14].reshape(-1)[:d]])
    near = to_core(gains)
    gains = order.run(jnp.add, gains, near)
    far = to_far(gains)
    t_q = s_q.finish()
    t_down, t_gate, t_up = (s.finish() for s in (s_down, s_gate, s_up))
    gains = order.run(jnp.add, gains, far)
    t_out = order.run(lambda a, b: jnp.concatenate([a, b], axis=0).T.astype(F32), t_p[3], t_q[3])
    decay_grad = ts[7] * -8.0 * jax.nn.sigmoid(decay_param)
    return (
        output[None],
        input_grad[None],
        gains[0] / mixer_gain,
        t_p[0],
        t_q[0],
        ts[0:4],
        ts[4],
        t_p[1],
        ts[5],
        t_q[1],
        ts[6],
        decay_grad,
        t_out,
        gains[1],
        t_gate,
        t_up,
        t_down,
    )


def solution(mesh):
    rows, ch = P("rows", "ch", None), P("ch")
    cols, lead = P(None, "ch"), P("ch", None)
    heads = P("ch", None, None)
    return jax.shard_map(
        functools.partial(body, mesh.shape["rows"]),
        mesh=mesh,
        in_specs=(rows, P("rows", None), P(), cols, cols, cols, ch, heads, ch, heads, ch, ch, lead, P(),
                  cols, cols, lead, rows),
        out_specs=(rows, rows, P(), cols, cols, cols, ch, heads, ch, heads, ch, ch, lead, P(), cols, cols, lead),
        check_vma=False,
    )
```

```python
import functools

import jax
import jax.numpy as jnp
from jax import lax
from jax.experimental import pallas as pl
from jax.experimental.pallas import tpu as pltpu
from jax.sharding import PartitionSpec as P

EPSILON = 1e-06
BF = jnp.bfloat16
F32 = jnp.float32
MIB = 1024 * 1024
KINDS = {"d": "line", "g": "line", "u": "z", "p": "line", "q": "line"}
LATE = 2
PLAN_AFTER = ("u", "g", "d", "p", "i", "q")
PLAN = ("d", "rf", "u", "g", "gf", "d", "m", "u", "g", "d", "p", "q")
GELU_C = 0.7978845608028654
GELU_A = 0.044715


def mm(a, b):
    return lax.dot_general(a, b, (((1,), (0,)), ((), ())), preferred_element_type=F32)


def mm_nt(a, b):
    return lax.dot_general(a, b, (((1,), (1,)), ((), ())), preferred_element_type=F32)


def mm_tn(a, b):
    return lax.dot_general(a, b, (((0,), (0,)), ((), ())), preferred_element_type=F32)


def sigmoid(v):
    return 0.5 * jnp.tanh(0.5 * v) + 0.5


def gelu_both(v):
    sq = v * v
    th = jnp.tanh(GELU_C * v * (1.0 + GELU_A * sq))
    half = 0.5 * th + 0.5
    slope = half + (0.5 * GELU_C) * v * (1.0 - th * th) * (1.0 + (3.0 * GELU_A) * sq)
    return v * half, slope


def gelu_only(v):
    th = jnp.tanh(GELU_C * v * (1.0 + GELU_A * (v * v)))
    return v * (0.5 * th + 0.5)


def scan_groups(mult, add, start, back):
    rows, cols = mult.shape
    a = mult.reshape(rows // 8, 8, cols)
    d = add.reshape(rows // 8, 8, cols)
    sub = lax.broadcasted_iota(jnp.int32, (1, 8, cols), 1)
    for k in (1, 2, 4):
        ok = sub < 8 - k if back else sub >= k
        turn = 8 - k if back else k
        d = d + a * jnp.where(ok, pltpu.roll(d, turn, 1), 0.0)
        a = a * jnp.where(ok, pltpu.roll(a, turn, 1), 1.0)
    state = start
    got = [None] * (rows // 8)
    order = range(rows // 8)
    for g in reversed(order) if back else order:
        now = d[g] + a[g] * state
        state = now[0:1] if back else now[7:8]
        got[g] = now
    return jnp.concatenate(got, axis=0), state


def gate_values(conv, pre, c8, width):
    rg = sigmoid(pre[:, :width])
    ig = sigmoid(pre[:, width:])
    forget = jnp.exp(c8 * rg)
    om = 1.0 - forget * forget
    top = jnp.maximum(om, 0.001)
    inv = lax.rsqrt(top)
    return rg, ig, forget, om, top * inv, inv


def begin(sem, first, *pairs):
    copies = [pltpu.make_async_copy(src, dst, sem.at[first + k]) for k, (src, dst) in enumerate(pairs)]
    for c in copies:
        c.start()
    return copies


def wait(copies):
    for c in copies:
        c.wait()


def project(x, gain, wb, wi):
    x = x.astype(F32)
    inv = lax.rsqrt(jnp.mean(x * x, axis=-1, keepdims=True) + EPSILON)
    normed = (x * inv * gain).astype(BF)
    return normed, mm(normed, wb), mm(normed, wi)


def mixer_pre(b0, b1, wb_h, wi_h, gain, normed_h, br_h, ri_h, xb, wb, wi, normed_v, br_v, ri_v, sem_in, sem_out):
    first = begin(sem_in, 0, (b0, xb.at[0]), (wb_h, wb), (wi_h, wi))
    second = begin(sem_in, 3, (b1, xb.at[1]))
    for i, ready in enumerate((first, second)):
        wait(ready)
        normed_v[i], br_v[i], ri_v[i] = project(xb[i], gain[...], wb[...], wi[...])
    wait(begin(sem_out, 0, (normed_v, normed_h), (br_v, br_h), (ri_v, ri_h)))


def mixer_fwd(
    me_ref, b2, b3, wb_h, wi_h, br01, ri01, wrg_h, masks_h, wo_h, gain, cw, cb, brg, c8,
    normed_h, br_h, ri_h, cv_h, sp_h, mix_h, p0, p2, p3, p1,
    xb, wb, wi, wrg, masks, wo, normed_v, br_v, ri_s, ri_v, cv_v, sp_v, mix_v, ext, sext, sem_in, sem_out,
):
    n, rows, width = br_v.shape
    first = begin(sem_in, 0, (b2, xb.at[0]), (wb_h, wb), (wi_h, wi))
    second = begin(sem_in, 3, (b3, xb.at[1]))
    later = begin(sem_in, 4, (ri01, ri_s.at[0:2]), (wrg_h, wrg), (masks_h, masks), (br01, br_v.at[0:2]), (wo_h, wo))
    for i, ready in enumerate((first, second)):
        wait(ready)
        normed_v[i], br_v[2 + i], ri_s[2 + i] = project(xb[i], gain[...], wb[...], wi[...])
    out = begin(sem_out, 0, (normed_v, normed_h), (br_v.at[2:4], br_h))
    ext[0:8] = jnp.zeros((8, width), F32)
    wait(later)

    def block(t, first):
        r = jnp.bitwise_xor(t, me_ref[0])
        ri = ri_s[r]
        ri_v[r] = ri.astype(BF)
        ext[8:8 + rows] = ri
        m = masks[t]
        conv = cb[...] + cw[0:1] * ri
        for k in (1, 2, 3):
            conv = conv + cw[k:k + 1] * (ext[8 - k:8 - k + rows] * m[:, k - 1:k])
        ext[0:8] = ext[rows:rows + 8]
        cv = conv.astype(BF)
        cv_v[r] = cv
        cvf = cv.astype(F32)
        pre = mm(cv, wrg[...]) + brg[...]
        rg, ig, forget, om, scale, _ = gate_values(cvf, pre, c8[...], width)
        keep = m[:, 0:1]
        states, last = scan_groups(forget * keep, scale * ig * cvf, first, False)
        sext[8:8 + rows] = states
        sext[7:8] = first
        sp_v[r] = sext[7:7 + rows] * keep
        mix_v[r] = (gelu_only(br_v[r]) * states).astype(BF)
        return last

    lax.fori_loop(0, n, block, jnp.zeros((1, width), F32))
    out += begin(sem_out, 2, (ri_v, ri_h), (cv_v, cv_h), (sp_v, sp_h), (mix_v, mix_h))
    for i, ref in ((3, p3), (1, p1), (2, p2), (0, p0)):
        ref[...] = mm(mix_v[i], wo[...]).astype(BF)
    wait(out)


def mixer_mid(
    me_ref, br01, br23, cv_h, sp_h, wrg_h, masks_h, brg, c8,
    a1_h, gl_h, later_h, f1_h, f2_h, f3_h, f4_h,
    br, cv, sp, wrg, masks, a1, gl, later, f1, f2, f3, f4, aext, sem_in, sem_out,
):
    n, rows, width = br.shape
    wait(begin(sem_in, 0, (br01, br.at[0:2]), (br23, br.at[2:4]), (cv_h, cv), (wrg_h, wrg), (masks_h, masks), (sp_h, sp)))
    aext[rows:rows + 8] = jnp.zeros((8, width), F32)

    def block(step, _):
        t = n - 1 - step
        r = jnp.bitwise_xor(t, me_ref[0])
        gelu, slope = gelu_both(br[r])
        cvb = cv[r]
        cvf = cvb.astype(F32)
        c8v = c8[...]
        pre = mm(cvb, wrg[...]) + brg[...]
        rg, ig, forget, om, scale, inv = gate_values(cvf, pre, c8v, width)
        m = masks[t]
        before = sp[r]
        igc = ig * cvf
        gl[r] = gelu.astype(BF)
        a1[r] = ((forget * before + scale * igc) * slope).astype(BF)
        aext[0:rows] = forget * m[:, 0:1]
        later[r] = aext[1:1 + rows]
        aext[rows:rows + 8] = aext[0:8]
        q = jnp.where(om > 0.001, -forget * inv, 0.0)
        base = (before + q * igc) * forget * rg
        f1[r] = base.astype(BF)
        f2[r] = (base * (1.0 - rg) * c8v).astype(BF)
        f3[r] = (scale * igc * (1.0 - ig)).astype(BF)
        f4[r] = (scale * ig).astype(BF)
        return 0

    lax.fori_loop(0, n, block, 0)
    wait(begin(sem_out, 0, (a1, a1_h), (gl, gl_h), (later, later_h), (f1, f1_h), (f2, f2_h), (f3, f3_h), (f4, f4_h)))


def flat(ref):
    return ref[...].reshape(ref.shape[0] * ref.shape[1], ref.shape[2])


def mixer_out(
    y_ref, b0, b1, b2, b3, wo_h, a1_h, gl_h, normed01, normed23, mix_h,
    gs_h, gbr_h, keep_o, send_o,
    gb, wo, a1, gl, normed, mix, gs, gbr, pair, sem_in, sem_out,
):
    n = gb.shape[0]
    first = begin(sem_in, 0, (wo_h, wo), (b0, gb.at[0]), (b1, gb.at[1]), (b2, gb.at[2]), (b3, gb.at[3]))
    then = begin(sem_in, 5, (a1_h, a1), (gl_h, gl))
    last = begin(sem_in, 7, (normed01, normed.at[0:2]), (normed23, normed.at[2:4]), (mix_h, mix))
    wait(first)
    for i in range(n):
        gmix = mm_nt(gb[i], wo[...])
        if i == 0:
            wait(then)
        gbr[i] = (gmix * a1[i].astype(F32)).astype(BF)
        gs[i] = gmix * gl[i].astype(F32)
    out = begin(sem_out, 0, (gs, gs_h), (gbr, gbr_h))
    wait(last)
    pair[0] = mm_tn(flat(normed), flat(gbr)).astype(BF)
    pair[1] = mm_tn(flat(gb), flat(mix)).astype(BF)
    for part in (0, 1):
        @pl.when(y_ref[0] == part)
        def _():
            wait(begin(sem_out, 2, (pair.at[part], keep_o), (pair.at[1 - part], send_o)))
    wait(out)


def mixer_bwd(
    me_ref, y_ref, gs_h, later_h, f1_h, f2_h, f3_h, f4_h, ri_h, cv_h, wrg_h, masks_h, gbr_h, normed01, normed23,
    wb_h, wi_h, cw, gain2,
    n0, n2, n31, keep_o, send_o,
    gs, later, f1, f2, f3, f4, ri_v, cv_v, wrg, masks, gbr, normed, wb, wi,
    pair_s, gri_v, p_v, last_v, sm_v, zext, sem_block, sem_in, sem_out,
):
    n, rows, width = gs.shape
    d = normed.shape[2]
    early = begin(sem_in, 0, (wrg_h, wrg), (masks_h, masks))
    blocks = ((gs_h, gs), (later_h, later), (f1_h, f1), (f2_h, f2), (f3_h, f3), (f4_h, f4), (ri_h, ri_v), (cv_h, cv_v))

    def pulls(step):
        r = jnp.bitwise_xor(n - 1 - step, me_ref[0])
        return [pltpu.make_async_copy(src.at[r], dst.at[r], sem_block.at[k, step])
                for k, (src, dst) in enumerate(blocks)]

    for step in range(n):
        for c in pulls(step):
            c.start()
    late = begin(sem_in, 2, (gbr_h, gbr), (normed01, normed.at[0:2]), (normed23, normed.at[2:4]), (wb_h, wb), (wi_h, wi))
    zext[:, rows:rows + 8] = jnp.zeros((3, 8, width), F32)
    sm_v[...] = jnp.zeros(sm_v.shape, F32)
    wait(early)

    def block(step, after):
        wait(pulls(step))
        t = n - 1 - step
        r = jnp.bitwise_xor(t, me_ref[0])
        m = masks[t]
        adj, head = scan_groups(later[r], gs[r], after, True)
        grp = (adj * f2[r].astype(F32)).astype(BF)
        ggp = (adj * f3[r].astype(F32)).astype(BF)
        pair = jnp.concatenate([grp, ggp], axis=1)
        pair_s[r] = pair
        gconv = adj * f4[r].astype(F32) + mm_nt(pair, wrg[...])
        ri = ri_v[r].astype(F32)
        gri = cw[0:1] * gconv
        sums = [jnp.sum(ri * gconv, axis=0, keepdims=True)]
        for k in (1, 2, 3):
            z = gconv * m[:, k - 1:k]
            zext[k - 1, 0:rows] = z
            moved = zext[k - 1, k:k + rows]
            zext[k - 1, rows:rows + 8] = z[0:8]
            gri = gri + cw[k:k + 1] * moved
            sums.append(jnp.sum(ri * moved, axis=0, keepdims=True))
        sums.append(jnp.sum(gconv, axis=0, keepdims=True))
        sums.append(jnp.sum(grp.astype(F32), axis=0, keepdims=True))
        sums.append(jnp.sum(ggp.astype(F32), axis=0, keepdims=True))
        sums.append(jnp.sum(adj * f1[r].astype(F32), axis=0, keepdims=True))
        sm_v[...] += jnp.concatenate(sums, axis=0)
        gri_v[r] = gri.astype(BF)
        return head

    lax.fori_loop(0, n, block, jnp.zeros((1, width), F32))
    wait(late)
    out = []
    gain1 = jnp.zeros((1, d), F32)
    for k, (i, ref) in enumerate(((3, n31.at[0]), (1, n31.at[1]), (2, n2), (0, n0))):
        part = mm_nt(gbr[i], wb[...]) + mm_nt(gri_v[i], wi[...])
        p_v[i] = part.astype(BF)
        out += begin(sem_out, k, (p_v.at[i], ref))
        gain1 = gain1 + jnp.sum(part * normed[i].astype(F32), axis=0, keepdims=True)

    def as_rows(v):
        v = jnp.concatenate([v, jnp.zeros((1, 3 * width - d), F32)], axis=1)
        return [v[:, i * width:(i + 1) * width] for i in range(3)]

    last_v[0:d] = mm_tn(flat(normed), flat(gri_v)).astype(BF)
    dw = mm_tn(flat(cv_v), flat(pair_s))
    hd = width // 2
    left = lax.broadcasted_iota(jnp.int32, (hd, width), 1) < hd
    for k in (0, 1):
        mine = dw[:, k * width:(k + 1) * width]
        last_v[d + k * hd:d + (k + 1) * hd] = jnp.where(left, mine[:hd], mine[hd:]).astype(BF)
    rest = last_v.shape[0] - d - 2 * hd
    few = [sm_v[...]] + as_rows(gain1) + as_rows(gain2[...]) + [jnp.zeros((rest - 14, width), F32)]
    last_v[d + 2 * hd:] = jnp.concatenate(few, axis=0).astype(BF)
    cut = last_v.shape[0] // 2
    halves = last_v.at[0:cut], last_v.at[cut:2 * cut]
    for part in (0, 1):
        @pl.when(y_ref[0] == part)
        def _():
            wait(begin(sem_out, 4, (halves[part], keep_o), (halves[1 - part], send_o)))
    wait(out)


def ends_branch(y_ref, cur, got, branch_o, out_o):
    for part in (0, 1):
        @pl.when(y_ref[0] == part)
        def _():
            pair = (cur, got) if part == 0 else (got, cur)
            branch_o[...] = pair[0][...].astype(F32)
            out_o[...] = pair[1][...].astype(F32).T


def ends_input(y_ref, cur, got, input_o, recur_o, gate_o, few_o, gains_o, whole):
    d, hd = input_o.shape[0], recur_o.shape[1]
    cut = whole.shape[0] // 2
    for part in (0, 1):
        @pl.when(y_ref[0] == part)
        def _():
            whole[part * cut:(part + 1) * cut] = cur[...]
            whole[(1 - part) * cut:(2 - part) * cut] = got[...]
    input_o[...] = whole[0:d].astype(F32)
    for k, ref in enumerate((recur_o, gate_o)):
        both_heads = whole[d + k * hd:d + (k + 1) * hd].astype(F32)
        for i in range(recur_o.shape[0]):
            ref[i] = both_heads[:, i * hd:(i + 1) * hd]
    few = whole[d + 2 * hd:d + 2 * hd + 16].astype(F32)
    few_o[...] = few[0:8]
    for k in (0, 1):
        at = 8 + 3 * k
        gains_o[k:k + 1] = jnp.concatenate([few[at + i:at + i + 1] for i in range(3)], axis=1)[:, :gains_o.shape[1]]


def mlp_blocks(xb, cot, wg, wu, wd, hid, gg, gu, p_v, ready, base):
    for i in range(xb.shape[0]):
        wait(ready[i])
        x = xb[i]
        ga = mm(x, wg[...])
        if i == 0:
            wait(ready[-1][:1])
        ua = mm(x, wu[...])
        if i == 0:
            wait(ready[-1][1:])
        gh = mm_nt(cot[base + i], wd[...])
        gl, slope = gelu_both(ga)
        hid[base + i] = (gl * ua).astype(BF)
        gg[i] = (gh * ua * slope).astype(BF)
        gu[i] = (gh * gl).astype(BF)
    for i in reversed(range(xb.shape[0])):
        p_v[i] = (mm_nt(gg[i], wg[...]) + mm_nt(gu[i], wu[...])).astype(BF)


def mlp_pre(
    b0, b1, c0, c1, wg_h, wu_h, wd_h, hid_h, gg_h, gu_h, n0, n1,
    xb, cot, wg, wu, wd, hid, gg, gu, p_v, sem_in, sem_out,
):
    first = begin(sem_in, 0, (b0, xb.at[0]), (wg_h, wg))
    then = begin(sem_in, 2, (wu_h, wu), (c0, cot.at[0]), (wd_h, wd))
    second = begin(sem_in, 5, (b1, xb.at[1]), (c1, cot.at[1]))
    mlp_blocks(xb, cot, wg, wu, wd, hid, gg, gu, p_v, (first, second, then), 0)
    wait(begin(sem_out, 0, (hid, hid_h), (gg, gg_h), (gu, gu_h), (p_v.at[1], n1), (p_v.at[0], n0)))


def mlp_main(
    y_ref, b2, b3, c0, c1, c2, c3, hid01, n1, wg_h, wu_h, wd_h, hid_h, gg_h, gu_h, n2, n31, dk_o, ds_o,
    xb, cot, wg, wu, wd, hid, gg, gu, p_v, dd, sem_in, sem_out,
):
    rows, units = hid.shape[1:]
    first = begin(sem_in, 0, (b2, xb.at[0]), (wg_h, wg))
    then = begin(sem_in, 2, (wu_h, wu), (c2, cot.at[2]), (wd_h, wd))
    second = begin(sem_in, 5, (b3, xb.at[1]), (c3, cot.at[3]))
    last = begin(sem_in, 7, (c0, cot.at[0]), (c1, cot.at[1]), (hid01, hid.at[0:2]), (n1, n31.at[1]))
    mlp_blocks(xb, cot, wg, wu, wd, hid, gg, gu, p_v, (first, second, then), 2)
    n31[0] = p_v[1]
    n2[...] = p_v[0]
    out = begin(sem_out, 0, (hid.at[2:4], hid_h), (gg, gg_h), (gu, gu_h))
    wait(last)
    call_ = cot[...].reshape(4 * rows, cot.shape[2])
    hall = hid[...].reshape(4 * rows, units)
    half = units // 2
    for part in (0, 1):
        dd[part] = mm_tn(hall[:, part * half:(part + 1) * half], call_).astype(BF)
    for part in (0, 1):
        @pl.when(y_ref[0] == part)
        def _():
            wait(begin(sem_out, 5, (dd.at[part], dk_o), (dd.at[1 - part], ds_o)))
    wait(out)


def mlp_post(
    y_ref, z_ref, b0, b1, b2, b3, gg01, gg23, gu01, gu23, hid01, hid23, wd_h, gk_o, gs_o, uk_o, us_o, m0, m2, m31,
    xb, gg, gu, hid, wd, dg, du, p_v, sem_in, sem_out,
):
    n, rows, units = hid.shape
    first = begin(sem_in, 0, (b0, xb.at[0]), (b1, xb.at[1]), (b2, xb.at[2]), (b3, xb.at[3]),
                  (gg01, gg.at[0:2]), (gg23, gg.at[2:4]))
    second = begin(sem_in, 6, (gu01, gu.at[0:2]), (gu23, gu.at[2:4]))
    third = begin(sem_in, 8, (hid01, hid.at[0:2]), (hid23, hid.at[2:4]), (wd_h, wd))

    def flat(ref):
        return ref[...].reshape(n * rows, ref.shape[2])

    wait(first)
    xall = flat(xb)
    half = dg.shape[1]
    for part in (0, 1):
        dg[part] = mm_tn(xall[:, part * half:(part + 1) * half], flat(gg)).astype(BF)
    wait(second)
    for part in (0, 1):
        du[part] = mm_tn(xall[:, part * half:(part + 1) * half], flat(gu)).astype(BF)
    for part in (0, 1):
        @pl.when(y_ref[0] == part)
        def _():
            begin(sem_out, 4, (dg.at[part], gk_o), (dg.at[1 - part], gs_o))

        @pl.when(z_ref[0] == part)
        def _():
            begin(sem_out, 6, (du.at[part], uk_o), (du.at[1 - part], us_o))
    out = []
    wait(third)
    for k, (i, ref) in enumerate(((3, m31.at[0]), (1, m31.at[1]), (2, m2), (0, m0))):
        p_v[i] = mm(hid[i], wd[...]).astype(BF)
        out += begin(sem_out, k, (p_v.at[i], ref))
    wait(out)
    wait([pltpu.make_async_copy(v.at[0], o, sem_out.at[4 + k])
          for k, (v, o) in enumerate(((dg, gk_o), (dg, gs_o), (du, uk_o), (du, us_o)))])


def add_two(a, b, got_a, got_b, send_o, own_o):
    send_o[...] = plus(a[...], got_a[...]).astype(BF)
    own_o[...] = plus(b[...], got_b[...]).astype(BF)


def add_both(i2, i0, o2, o0, got_i, got_o, send_o, own_i, own_o):
    send_o[0] = plus(i2[...], got_i[0]).astype(BF)
    own_i[...] = plus(i0[...], got_i[1]).astype(BF)
    send_o[1] = plus(o2[...], got_o[0]).astype(BF)
    own_o[...] = plus(o0[...], got_o[1]).astype(BF)


def add_pair(a, b, got, send_o, own_o):
    send_o[...] = plus(a[...], got[0]).astype(BF)
    own_o[...] = plus(b[...], got[1]).astype(BF)


def mid_fwd(x, own, far, gain, mid_o, n_o):
    mid = x[...].astype(F32) + plus(own[...], far[...])
    inv = lax.rsqrt(jnp.mean(mid * mid, axis=-1, keepdims=True) + EPSILON)
    mid_o[...] = mid
    n_o[...] = (mid * inv * gain[...]).astype(BF)


def norm_back(total, values, gain):
    inv = lax.rsqrt(jnp.mean(values * values, axis=-1, keepdims=True) + EPSILON)
    v = total * gain
    scaled = values * inv
    mean = jnp.mean(v * scaled, axis=-1, keepdims=True)
    grad = inv * (v - scaled * mean)
    return grad, jnp.sum(total * scaled, axis=0, keepdims=True)


def mid_bwd(mid, own, far, gain, cot, gm_o, gb_o, gg_o):
    grad, gsum = norm_back(plus(own[...], far[...]), mid[...], gain[...])
    gm = cot[...].astype(F32) + grad
    gm_o[...] = gm
    gb_o[...] = gm.astype(BF)
    gg_o[...] = gsum


def last_bwd(x, mid, own_i, own_o, far, gain, gm, o, out_o):
    grad, _ = norm_back(plus(own_i[...], far[0]), x[...].astype(F32), gain[...])
    o[...] = gm[...] + grad
    out_o[...] = (mid[...] + plus(own_o[...], far[1])).astype(BF)


def cost(us):
    return pl.CostEstimate(flops=1 + int(us * 1.15e9), bytes_accessed=0, transcendentals=0)


HBM, VMEM, SMEM = pltpu.HBM, pltpu.VMEM, pltpu.SMEM


def call(kernel, outs, *args, name, us, mib, places, out, scratch=()):
    spec = {"h": HBM, "v": VMEM, "s": SMEM, "a": pl.ANY}
    args = [
        pltpu.with_memory_space_constraint(a, VMEM if p == "v" else HBM) if p in "hv" else a
        for p, a in zip(places, args, strict=True)
    ]
    return pl.pallas_call(
        kernel,
        out_shape=[(VMEM if p == "v" else HBM)(*o) for p, o in zip(out, outs, strict=True)],
        in_specs=[pl.BlockSpec(memory_space=spec[p]) if p in spec else pl.BlockSpec() for p in places],
        out_specs=[pl.BlockSpec(memory_space=spec[p]) if p in spec else pl.BlockSpec() for p in out],
        scratch_shapes=list(scratch),
        compiler_params=pltpu.CompilerParams(vmem_limit_bytes=mib * MIB),
        cost_estimate=cost(us),
        name=name,
    )(*args)


CORE = [(i, i ^ 1) for i in range(4)]
FAR = [(i, i ^ 2) for i in range(4)]


def to_core(v):
    return lax.ppermute(v, "ch", CORE)


def to_far(v):
    return lax.ppermute(v, "ch", FAR)


class Order:
    def __init__(self):
        self.last = None

    def run(self, work, *values):
        if self.last is not None:
            values = lax.optimization_barrier((*values, *self.last))[:len(values)]
        got = work(*values)
        self.last = tuple(got) if isinstance(got, (tuple, list)) else (got,)
        return got

    def gate(self, value):
        return lax.optimization_barrier((value, *self.last))[0]

    def take(self, value):
        return self.run(lambda v: (v,), value)[0]


def dyn(g, index, size):
    return lax.dynamic_slice_in_dim(g, index * size, size, 0)


def plus(a, b):
    return a.astype(F32) + b.astype(F32)


def add_low(a, b):
    return plus(a, b).astype(BF)


def put(total, piece, index):
    return lax.dynamic_update_slice_in_dim(total, piece.astype(total.dtype), index * piece.shape[0], 0)


Y = [(i, i ^ 1) for i in range(8)]
Z1 = [(i, i ^ 2) for i in range(8)]
Z2 = [(i, i ^ 4) for i in range(8)]
def both(low, a, b):
    return jnp.concatenate([jnp.where(low, a, b), jnp.where(low, b, a)], 0)


def sum_rows_plain(keep, send, ends):
    yield "sent"
    return ends(*(lax.psum(v.astype(F32), "rows").astype(BF) for v in (keep, send)))


INWARD = [(0, 2), (1, 3), (6, 4), (7, 5)]
MIDDLE = [(2, 4), (3, 5), (4, 2), (5, 3)]
OUTWARD = [(2, 0), (3, 1), (4, 6), (5, 7)]


def send_on(value, pairs, order):
    if (yield "ready"):
        value = order.gate(value)
    got = lax.ppermute(value, "rows", pairs)
    yield "sent"
    return order.take(got)


def sum_rows_halves(keep, send, order, way, ends):
    me = lax.axis_index("rows")
    y, z = (Y, me % 2), (Z1, (me // 2) % 2)
    stages = ((y, z) if way == "y" else (z, y)) + ((Z2, me // 4),)
    got = yield from send_on(send, stages[0][0], order)
    yield "came"
    for pairs, bit in stages[1:]:
        half = keep.shape[0] // 2

        def split(a, b, bit=bit, half=half):
            return (add_low(dyn(a, 1 - bit, half), dyn(b, 1 - bit, half)), add_low(dyn(a, bit, half), dyn(b, bit, half)))

        send, keep = order.run(split, keep, got)
        got = yield from send_on(send, pairs, order)
        yield "came"
    cur = order.run(add_low, keep, got)
    for pairs, bit in stages[::-1]:
        got = yield from send_on(cur, pairs, order)
        yield "came"
        if pairs is stages[0][0]:
            return order.run(ends, cur, got)
        cur = order.run(lambda a, b, bit=bit: both(bit == 0, a, b), cur, got)


def sum_rows_line(keep, send, order, ends):
    me = lax.axis_index("rows")
    y, z = me % 2, me // 2
    inner = (z == 1) | (z == 2)
    got = yield from send_on(send, Y, order)
    yield "came"
    cur = order.run(add_low, keep, got)
    for pairs in (INWARD, MIDDLE):
        got = yield from send_on(cur, pairs, order)
        yield "came"
        cur = order.run(add_low, cur, got)
    got = yield from send_on(cur, OUTWARD, order)
    yield "came"
    cur = order.run(lambda a, b: jnp.where(inner, a, b), cur, got)
    got = yield from send_on(cur, Y, order)
    yield "came"
    return order.run(ends, cur, got)


class Chain:
    def __init__(self, steps):
        self.steps, self.value, self.state, self.held = steps, None, None, False
        self.go()

    def step(self, first=False):
        try:
            self.state = self.steps.send(None if self.state is None else self.held)
            self.held = False
        except StopIteration as end:
            self.state, self.value = "done", end.value

    def to(self, state):
        if self.state == "done":
            return
        self.step()
        while self.state not in (state, "done"):
            self.step()
        self.held = state == "ready"

    def come(self):
        if self.state == "sent":
            self.to("came")

    def go(self):
        self.to("sent")

    def finish(self):
        while self.state != "done":
            self.go()
        return self.value


def block_diag(w):
    h, d, e = w.shape
    rows = [
        jnp.concatenate([w[i] if i == j else jnp.zeros((d, e), w.dtype) for j in range(h)], axis=1)
        for i in range(h)
    ]
    return jnp.concatenate(rows, axis=0)


def body(n_rows, inputs, segment_ids, mixer_gain, branch_weight, input_weight, conv_weight, conv_bias,
         recur_weight, recur_bias, gate_weight, gate_bias, decay_param, out_weight, mlp_gain, mlp_gate,
         mlp_up, mlp_down, cotangent):
    x = inputs[0]
    cot = cotangent[0]
    rows, d = x.shape
    width = branch_weight.shape[1]
    units = mlp_gate.shape[1]
    heads, hd, _ = recur_weight.shape
    seq = segment_ids.shape[1]
    n = seq // rows
    me = lax.axis_index("ch").astype(jnp.int32)[None]
    gain1 = mixer_gain[None]
    gain2 = mlp_gain[None]
    order = Order()
    row = lax.axis_index("rows").astype(jnp.int32)[None]
    y_half = row % 2 if n_rows == 8 else jnp.zeros((1,), jnp.int32)
    z_half = (row // 2) % 2 if n_rows == 8 else jnp.zeros((1,), jnp.int32)

    split = {k: z_half if v == "z" else y_half for k, v in KINDS.items()}

    def total(keep, send, way, ends):
        if n_rows != 8:
            return Chain(sum_rows_plain(keep, send, ends))
        if way == "line":
            return Chain(sum_rows_line(keep, send, order, ends))
        return Chain(sum_rows_halves(keep, send, order, way, ends))

    x_far, x_near = to_far(x), to_core(x)

    def tables(ids, rw, gw, rb, gb_, dp):
        marks = [
            (jnp.pad(ids, (k, 0), constant_values=-1)[:seq] == ids).astype(F32) for k in (1, 2, 3)
        ]
        masks = jnp.pad(jnp.stack(marks, axis=1), ((0, 0), (0, 125))).reshape(n, rows, 128)
        wrg = jnp.concatenate([block_diag(rw), block_diag(gw)], axis=1)
        return masks, wrg, jnp.concatenate([rb, gb_])[None], (-8.0 * jax.nn.softplus(dp))[None]

    masks, wrg, brg, c8 = order.run(
        tables, segment_ids[0], recur_weight, gate_weight, recur_bias, gate_bias, decay_param
    )
    cb = conv_bias[None]
    blk, narrow, wide = (rows, d), (n, rows, width), (n, rows, units)
    four, two = (n, rows, d), (2, rows, d)
    narrow2, wide2 = (2, rows, width), (2, rows, units)
    dma = pltpu.SemaphoreType.DMA
    normed01, br01, ri01 = order.run(
        functools.partial(
            call, mixer_pre, [(two, BF), (narrow2, F32), (narrow2, F32)], name="mixer_pre", us=0, mib=20,
            places="aahhi", out="hhh", scratch=[
                VMEM(two, BF), VMEM((d, width), BF), VMEM((d, width), BF), VMEM(two, BF), VMEM(narrow2, F32),
                VMEM(narrow2, F32), dma((4,)), dma((3,)),
            ]),
        x, x_near, branch_weight, input_weight, gain1)
    x_far = order.take(x_far)
    x_diag = to_core(x_far)
    cot_far = to_far(cot)
    x_diag = order.take(x_diag)
    fwd = order.run(
        functools.partial(
            call, mixer_fwd,
            [(two, BF), (narrow2, F32), (narrow, BF), (narrow, BF), (narrow, F32), (narrow, BF)] + [(blk, BF)] * 4,
            name="mixer_fwd", us=0, mib=30, places="saahhhhhhhiiiii", out="h" * 6 + "vvvv", scratch=[
                VMEM(two, BF), VMEM((d, width), BF), VMEM((d, width), BF), VMEM((width, 2 * width), BF),
                VMEM((n, rows, 128), F32), VMEM((width, d), BF), VMEM(two, BF), VMEM(narrow, F32),
                VMEM(narrow, F32), VMEM(narrow, BF), VMEM(narrow, BF), VMEM(narrow, F32), VMEM(narrow, BF),
                VMEM((rows + 8, width), F32), VMEM((rows + 8, width), F32), dma((9,)), dma((6,)),
            ]),
        me, x_far, x_diag, branch_weight, input_weight, br01, ri01, wrg, masks, out_weight, gain1, conv_weight, cb,
        brg, c8)
    normed23, br23, ri, cv, sp, mix = fwd[:6]
    cot_far = order.take(cot_far)

    def near_half(own, far, pair):
        got = to_core(pair)
        return order.run(
            functools.partial(call, add_pair, [(blk, BF)] * 2, name="add_pair", us=0, mib=6, places="iii", out="vv"),
            far, own, got)

    send, own = order.run(
        functools.partial(call, add_two, [(blk, BF)] * 2, name="add_two", us=0, mib=6, places="vvii", out="vv"),
        fwd[7], fwd[6], to_core(fwd[8]), to_core(fwd[9]))
    far = to_far(send)
    cot_near, cot_diag = to_core(cot), to_core(cot_far)
    cot_near = order.take(cot_near)
    cot_diag = order.take(cot_diag)
    a1, gl, later, *fs = order.run(
        functools.partial(
            call, mixer_mid, [(narrow, BF), (narrow, BF), (narrow, F32)] + [(narrow, BF)] * 4, name="mixer_mid", us=0,
            mib=30, places="s" + "h" * 6 + "ii", out="h" * 7, scratch=[
                VMEM(narrow, F32), VMEM(narrow, BF), VMEM(narrow, F32), VMEM((width, 2 * width), BF),
                VMEM((n, rows, 128), F32), VMEM(narrow, BF), VMEM(narrow, BF), VMEM(narrow, F32)]
            + [VMEM(narrow, BF)] * 4 + [VMEM((rows + 8, width), F32), dma((6,)), dma((7,))]),
        me, br01, br23, cv, sp, wrg, masks, brg, c8)
    mid, normed2 = order.run(functools.partial(
        call, mid_fwd, [(blk, F32), (blk, BF)], name="mid_fwd", us=0, mib=8, places="ivvi", out="iv"),
        x, own, far, gain2)
    n_far, n_near = to_far(normed2), to_core(normed2)
    n_near = order.take(n_near)
    mlp_scratch = [
        VMEM((d, units), BF), VMEM((d, units), BF), VMEM((units, d), BF)]
    hid01, gg01, gu01, g0, g1 = order.run(
        functools.partial(
            call, mlp_pre, [(wide2, BF)] * 3 + [(blk, BF)] * 2, name="mlp_pre", us=0, mib=30, places="aahhhhh",
            out="h" * 5, scratch=[VMEM(two, BF), VMEM(two, BF)] + mlp_scratch + [VMEM(wide2, BF)] * 3 + [
                VMEM(two, BF), dma((7,)), dma((5,))]),
        normed2, n_near, cot, cot_near, mlp_gate, mlp_up, mlp_down)
    n_far = order.take(n_far)
    n_diag = order.take(to_core(n_far))
    hid23, gg23, gu23, g2, g31, down_keep, down_send = order.run(
        functools.partial(
            call, mlp_main, [(wide2, BF)] * 3 + [(blk, BF), (two, BF)] + [((units // 2, d), BF)] * 2, name="mlp_main",
            us=0, mib=26, places="saahhhhhhhhh", out="hhhvvhh",
            scratch=[VMEM(two, BF), VMEM(four, BF)] + mlp_scratch + [VMEM(wide, BF), VMEM(wide2, BF), VMEM(wide2, BF)] + [
                VMEM(two, BF), VMEM((2, units // 2, d), BF), dma((11,)), dma((7,))]),
        split["d"], n_far, n_diag, cot, cot_near, cot_far, cot_diag, hid01, g1, mlp_gate, mlp_up, mlp_down)
    y_low, z_low = y_half[0] == 0, z_half[0] == 0

    def wide_ends(low, a, b):
        return both(low, a, b).astype(F32)

    def ends_of(kind):
        return functools.partial(wide_ends, y_low if split[kind] is y_half else z_low)

    s_down = total(down_keep, down_send, KINDS["d"], ends_of("d"))
    g_send, g_own = near_half(g0, g2, g31)
    from_far = to_far(g_send)
    post = order.run(
        functools.partial(
            call, mlp_post, [((d // 2, units), BF)] * 4 + [(blk, BF), (blk, BF), (two, BF)], name="mlp_post", us=0,
            mib=26, places="ssaaaahhhhhhh", out="h" * 7, scratch=[
                VMEM(four, BF), VMEM(wide, BF), VMEM(wide, BF), VMEM(wide, BF), VMEM((units, d), BF),
                VMEM((2, d // 2, units), BF), VMEM((2, d // 2, units), BF), VMEM(four, BF), dma((11,)), dma((8,)),
            ]),
        split["g"], split["u"], normed2, n_near, n_far, n_diag, gg01, gg23, gu01, gu23, hid01, hid23, mlp_down)
    s_gate = total(post[0], post[1], KINDS["g"], ends_of("g"))
    s_up = total(post[2], post[3], KINDS["u"], ends_of("u"))
    chains = {"d": s_down, "g": s_gate, "u": s_up}
    live = {}

    def at_rf():
        gm, gb, gsum2 = order.run(functools.partial(
            call, mid_bwd, [(blk, F32), (blk, BF), ((1, d), F32)], name="mid_bwd", us=10, mib=8, places="ivvii", out="ivi"),
            mid, g_own, from_far, gain2, cot)
        g_near, g_far = to_core(gb), to_far(gb)
        live.update(gm=gm, gb=gb, gsum2=gsum2, g_near=g_near, g_far=g_far)

    def at_gf():
        gb = live["gb"]
        g_far = order.take(live["g_far"])
        g_diag = to_core(g_far)
        g_near = order.take(live["g_near"])
        g_diag = order.take(g_diag)
        gs, gbr, p_keep, p_send = order.run(
            functools.partial(
                call, mixer_out, [(narrow, F32), (narrow, BF)] + [((d, width), BF)] * 2, name="mixer_out", us=0, mib=30,
                places="shhaa" + "h" * 6, out="h" * 4, scratch=[
                    VMEM(four, BF), VMEM((width, d), BF), VMEM(narrow, BF), VMEM(narrow, BF), VMEM(four, BF),
                    VMEM(narrow, BF), VMEM(narrow, F32), VMEM(narrow, BF), VMEM((2, d, width), BF), dma((10,)), dma((4,))]),
            split["p"], gb, g_near, g_far, g_diag, out_weight, a1, gl, normed01, normed23, mix)
        chains["p"] = total(p_keep, p_send, KINDS["p"], functools.partial(
            call, ends_branch, [((d, width), F32), ((width, d), F32)], split["p"], name="ends_branch", us=0, mib=16,
            places="sii", out="ii"))
        live.update(gs=gs, gbr=gbr)

    def at_m():
        last_rows = d + 2 * hd + 64
        bwd = order.run(
            functools.partial(
                call, mixer_bwd, [(blk, BF), (blk, BF), (two, BF)] + [((last_rows // 2, width), BF)] * 2,
                name="mixer_bwd", us=0, mib=36, places="ss" + "h" * 15 + "ii", out="h" * 5, scratch=[
                    VMEM(narrow, F32), VMEM(narrow, F32)] + [VMEM(narrow, BF)] * 6 + [
                    VMEM((width, 2 * width), BF), VMEM((n, rows, 128), F32), VMEM(narrow, BF), VMEM(four, BF),
                    VMEM((d, width), BF), VMEM((d, width), BF), VMEM((n, rows, 2 * width), BF), VMEM(narrow, BF),
                    VMEM(four, BF), VMEM((last_rows, width), BF), VMEM((8, width), F32), VMEM((3, rows + 8, width), F32),
                    dma((8, n)), dma((8,)), dma((6,)),
                ]),
            me, split["q"], live["gs"], later, *fs, ri, cv, wrg, masks, live["gbr"], normed01, normed23, branch_weight, input_weight,
            conv_weight, live["gsum2"])
        chains["q"] = total(bwd[3], bwd[4], KINDS["q"], functools.partial(
            call, ends_input, [((d, width), F32), ((heads, hd, hd), F32), ((heads, hd, hd), F32), ((8, width), F32),
             ((2, d), F32)], split["q"], name="ends_input", us=0, mib=16, places="sii", out="iiiii", scratch=[VMEM((last_rows, width), BF)]))

        live.update(bwd=bwd)

    def sum_ch(n0, n2, pair):
        got_i, got_o = to_core(order.gate(pair)), to_core(order.gate(post[6]))
        yield "sent"
        got_i, got_o = order.run(lambda a, b: (a, b), got_i, got_o)
        yield "came"
        send, own_i, own_o = order.run(
            functools.partial(
                call, add_both, [(two, BF), (blk, BF), (blk, BF)], name="add_both", us=0, mib=14, places="iiiiii", out="uuu"),
            n2, n0, post[5], post[4], got_i, got_o)
        far = to_far(send)
        yield "sent"
        far = order.take(far)
        yield "came"
        return order.run(
            functools.partial(
                call, last_bwd, [(blk, F32), (blk, BF)], name="last_bwd", us=0, mib=14, places="iiiiiii", out="ii"),
            x, mid, own_i, own_o, far, gain1, live["gm"])

    events = {"rf": at_rf, "gf": at_gf, "m": at_m}

    def turn(what):
        if what in events:
            events[what]()
            return
        chain = chains[what]
        chain.go()
        ended = sum(c.state == "done" for c in chains.values())
        if "bwd" in live and "i" not in chains and ended >= LATE:
            chains["i"] = Chain(sum_ch(*live["bwd"][:3]))

    for what in PLAN:
        turn(what)
    while any(c.state != "done" for c in chains.values()):
        for what in PLAN_AFTER:
            if what in chains:
                turn(what)
    input_grad, output = chains["i"].value
    t_branch, t_out = chains["p"].value
    t_input, t_recur, t_gate_w, ts, gains = chains["q"].value
    t_down, t_gate, t_up = (s.value for s in (s_down, s_gate, s_up))
    gains = order.run(jnp.add, gains, to_core(gains))
    gains = order.run(jnp.add, gains, to_far(gains))
    decay_grad = ts[7] * -8.0 * jax.nn.sigmoid(decay_param)
    return (
        output[None],
        input_grad[None],
        gains[0] / mixer_gain,
        t_branch,
        t_input,
        ts[0:4],
        ts[4],
        t_recur,
        ts[5],
        t_gate_w,
        ts[6],
        decay_grad,
        t_out,
        gains[1],
        t_gate,
        t_up,
        t_down,
    )


def solution(mesh):
    rows, ch = P("rows", "ch", None), P("ch")
    cols, lead = P(None, "ch"), P("ch", None)
    heads = P("ch", None, None)
    return jax.shard_map(
        functools.partial(body, mesh.shape["rows"]),
        mesh=mesh,
        in_specs=(rows, P("rows", None), P(), cols, cols, cols, ch, heads, ch, heads, ch, ch, lead, P(),
                  cols, cols, lead, rows),
        out_specs=(rows, rows, P(), cols, cols, cols, ch, heads, ch, heads, ch, ch, lead, P(), cols, cols, lead),
        check_vma=False,
    )
```

```python
import functools

import jax
import jax.numpy as jnp
from jax import lax
from jax.experimental import pallas as pl
from jax.experimental.pallas import tpu as pltpu
from jax.sharding import PartitionSpec as P

EPSILON = 1e-06
BF = jnp.bfloat16
F32 = jnp.float32
MIB = 1024 * 1024
KINDS = {"d": "line", "g": "line", "u": "z", "p": "line", "q": "line"}
PLAN_AFTER = ("u", "g", "d", "p", "i", "q", "c")
PLAN = ("d", "rf", "u", "g", "gf", "d", "m", "u", "g", "d", "p", "q")
GELU_C = 0.7978845608028654
GELU_A = 0.044715


def mm(a, b):
    return lax.dot_general(a, b, (((1,), (0,)), ((), ())), preferred_element_type=F32)


def mm_nt(a, b):
    return lax.dot_general(a, b, (((1,), (1,)), ((), ())), preferred_element_type=F32)


def mm_tn(a, b):
    return lax.dot_general(a, b, (((0,), (0,)), ((), ())), preferred_element_type=F32)


def sigmoid(v):
    return 0.5 * jnp.tanh(0.5 * v) + 0.5


def gelu_both(v):
    sq = v * v
    th = jnp.tanh(GELU_C * v * (1.0 + GELU_A * sq))
    half = 0.5 * th + 0.5
    slope = half + (0.5 * GELU_C) * v * (1.0 - th * th) * (1.0 + (3.0 * GELU_A) * sq)
    return v * half, slope


def gelu_only(v):
    th = jnp.tanh(GELU_C * v * (1.0 + GELU_A * (v * v)))
    return v * (0.5 * th + 0.5)


def scan_groups(mult, add, start, back):
    rows, cols = mult.shape
    a = mult.reshape(rows // 8, 8, cols)
    d = add.reshape(rows // 8, 8, cols)
    sub = lax.broadcasted_iota(jnp.int32, (1, 8, cols), 1)
    for k in (1, 2, 4):
        ok = sub < 8 - k if back else sub >= k
        turn = 8 - k if back else k
        d = d + a * jnp.where(ok, pltpu.roll(d, turn, 1), 0.0)
        a = a * jnp.where(ok, pltpu.roll(a, turn, 1), 1.0)
    state = start
    got = [None] * (rows // 8)
    order = range(rows // 8)
    for g in reversed(order) if back else order:
        now = d[g] + a[g] * state
        state = now[0:1] if back else now[7:8]
        got[g] = now
    return jnp.concatenate(got, axis=0), state


def gate_values(conv, pre, c8, width):
    rg = sigmoid(pre[:, :width])
    ig = sigmoid(pre[:, width:])
    forget = jnp.exp(c8 * rg)
    om = 1.0 - forget * forget
    top = jnp.maximum(om, 0.001)
    inv = lax.rsqrt(top)
    return rg, ig, forget, om, top * inv, inv


def begin(sem, first, *pairs):
    copies = [pltpu.make_async_copy(src, dst, sem.at[first + k]) for k, (src, dst) in enumerate(pairs)]
    for c in copies:
        c.start()
    return copies


def wait(copies):
    for c in copies:
        c.wait()


def project(x, gain, wb, wi):
    x = x.astype(F32)
    inv = lax.rsqrt(jnp.mean(x * x, axis=-1, keepdims=True) + EPSILON)
    normed = (x * inv * gain).astype(BF)
    return normed, mm(normed, wb), mm(normed, wi)


def mixer_pre(b0, b1, wb_h, wi_h, gain, normed_h, br_h, ri_h, xb, wb, wi, normed_v, br_v, ri_v, sem_in, sem_out):
    first = begin(sem_in, 0, (b0, xb.at[0]), (wb_h, wb), (wi_h, wi))
    second = begin(sem_in, 3, (b1, xb.at[1]))
    for i, ready in enumerate((first, second)):
        wait(ready)
        normed_v[i], br_v[i], ri_v[i] = project(xb[i], gain[...], wb[...], wi[...])
    wait(begin(sem_out, 0, (normed_v, normed_h), (br_v, br_h), (ri_v, ri_h)))


def mixer_fwd(
    me_ref, b2, b3, wb_h, wi_h, br01, ri01, wrg_h, masks_h, wo_h, gain, cw, cb, brg, c8,
    normed_h, br_h, ri_h, cv_h, sp_h, mix_h, p0, p2, p3, p1,
    xb, wb, wi, wrg, masks, wo, normed_v, br_v, ri_s, ri_v, cv_v, sp_v, mix_v, ext, sext, sem_in, sem_out,
):
    n, rows, width = br_v.shape
    first = begin(sem_in, 0, (b2, xb.at[0]), (wb_h, wb), (wi_h, wi))
    second = begin(sem_in, 3, (b3, xb.at[1]))
    later = begin(sem_in, 4, (ri01, ri_s.at[0:2]), (wrg_h, wrg), (masks_h, masks), (br01, br_v.at[0:2]), (wo_h, wo))
    for i, ready in enumerate((first, second)):
        wait(ready)
        normed_v[i], br_v[2 + i], ri_s[2 + i] = project(xb[i], gain[...], wb[...], wi[...])
    out = begin(sem_out, 0, (normed_v, normed_h), (br_v.at[2:4], br_h))
    ext[0:8] = jnp.zeros((8, width), F32)
    wait(later)

    def block(t, first):
        r = jnp.bitwise_xor(t, me_ref[0])
        ri = ri_s[r]
        ri_v[r] = ri.astype(BF)
        ext[8:8 + rows] = ri
        m = masks[t]
        conv = cb[...] + cw[0:1] * ri
        for k in (1, 2, 3):
            conv = conv + cw[k:k + 1] * (ext[8 - k:8 - k + rows] * m[:, k - 1:k])
        ext[0:8] = ext[rows:rows + 8]
        cv = conv.astype(BF)
        cv_v[r] = cv
        cvf = cv.astype(F32)
        pre = mm(cv, wrg[...]) + brg[...]
        rg, ig, forget, om, scale, _ = gate_values(cvf, pre, c8[...], width)
        keep = m[:, 0:1]
        states, last = scan_groups(forget * keep, scale * ig * cvf, first, False)
        sext[8:8 + rows] = states
        sext[7:8] = first
        sp_v[r] = sext[7:7 + rows] * keep
        mix_v[r] = (gelu_only(br_v[r]) * states).astype(BF)
        return last

    lax.fori_loop(0, n, block, jnp.zeros((1, width), F32))
    out += begin(sem_out, 2, (ri_v, ri_h), (cv_v, cv_h), (sp_v, sp_h), (mix_v, mix_h))
    for i, ref in ((3, p3), (1, p1), (2, p2), (0, p0)):
        ref[...] = mm(mix_v[i], wo[...]).astype(BF)
    wait(out)


def mixer_mid(
    me_ref, br01, br23, cv_h, sp_h, wrg_h, masks_h, brg, c8,
    a1_h, gl_h, later_h, f1_h, f2_h, f3_h, f4_h,
    br, cv, sp, wrg, masks, a1, gl, later, f1, f2, f3, f4, aext, sem_in, sem_out,
):
    n, rows, width = br.shape
    wait(begin(sem_in, 0, (br01, br.at[0:2]), (br23, br.at[2:4]), (cv_h, cv), (wrg_h, wrg), (masks_h, masks), (sp_h, sp)))
    aext[rows:rows + 8] = jnp.zeros((8, width), F32)

    def block(step, _):
        t = n - 1 - step
        r = jnp.bitwise_xor(t, me_ref[0])
        gelu, slope = gelu_both(br[r])
        cvb = cv[r]
        cvf = cvb.astype(F32)
        c8v = c8[...]
        pre = mm(cvb, wrg[...]) + brg[...]
        rg, ig, forget, om, scale, inv = gate_values(cvf, pre, c8v, width)
        m = masks[t]
        before = sp[r]
        igc = ig * cvf
        gl[r] = gelu.astype(BF)
        a1[r] = ((forget * before + scale * igc) * slope).astype(BF)
        aext[0:rows] = forget * m[:, 0:1]
        later[r] = aext[1:1 + rows]
        aext[rows:rows + 8] = aext[0:8]
        q = jnp.where(om > 0.001, -forget * inv, 0.0)
        base = (before + q * igc) * forget * rg
        f1[r] = base.astype(BF)
        f2[r] = (base * (1.0 - rg) * c8v).astype(BF)
        f3[r] = (scale * igc * (1.0 - ig)).astype(BF)
        f4[r] = (scale * ig).astype(BF)
        return 0

    lax.fori_loop(0, n, block, 0)
    wait(begin(sem_out, 0, (a1, a1_h), (gl, gl_h), (later, later_h), (f1, f1_h), (f2, f2_h), (f3, f3_h), (f4, f4_h)))


def flat(ref):
    return ref[...].reshape(ref.shape[0] * ref.shape[1], ref.shape[2])


def mixer_out(
    y_ref, b0, b1, b2, b3, wo_h, a1_h, gl_h, normed01, normed23, mix_h,
    gs_h, gbr_h, keep_o, send_o,
    gb, wo, a1, gl, normed, mix, gs, gbr, pair, sem_in, sem_out,
):
    n = gb.shape[0]
    first = begin(sem_in, 0, (wo_h, wo), (b0, gb.at[0]), (b1, gb.at[1]), (b2, gb.at[2]), (b3, gb.at[3]))
    then = begin(sem_in, 5, (a1_h, a1), (gl_h, gl))
    last = begin(sem_in, 7, (normed01, normed.at[0:2]), (normed23, normed.at[2:4]), (mix_h, mix))
    wait(first)
    for i in range(n):
        gmix = mm_nt(gb[i], wo[...])
        if i == 0:
            wait(then)
        gbr[i] = (gmix * a1[i].astype(F32)).astype(BF)
        gs[i] = gmix * gl[i].astype(F32)
    out = begin(sem_out, 0, (gs, gs_h), (gbr, gbr_h))
    wait(last)
    pair[0] = mm_tn(flat(normed), flat(gbr)).astype(BF)
    pair[1] = mm_tn(flat(gb), flat(mix)).astype(BF)
    for part in (0, 1):
        @pl.when(y_ref[0] == part)
        def _():
            wait(begin(sem_out, 2, (pair.at[part], keep_o), (pair.at[1 - part], send_o)))
    wait(out)


def mixer_bwd(
    me_ref, y_ref, gs_h, later_h, f1_h, f2_h, f3_h, f4_h, ri_h, cv_h, wrg_h, masks_h, gbr_h, normed01, normed23,
    wb_h, wi_h, cw, gain2,
    n0, n2, n31, keep_o, send_o,
    gs, later, f1, f2, f3, f4, ri_v, cv_v, wrg, masks, gbr, normed, wb, wi,
    pair_s, gri_v, p_v, last_v, sm_v, zext, sem_block, sem_in, sem_out,
):
    n, rows, width = gs.shape
    d = normed.shape[2]
    early = begin(sem_in, 0, (wrg_h, wrg), (masks_h, masks))
    blocks = ((gs_h, gs), (later_h, later), (f1_h, f1), (f2_h, f2), (f3_h, f3), (f4_h, f4), (ri_h, ri_v), (cv_h, cv_v))

    def pulls(step):
        r = jnp.bitwise_xor(n - 1 - step, me_ref[0])
        return [pltpu.make_async_copy(src.at[r], dst.at[r], sem_block.at[k, step])
                for k, (src, dst) in enumerate(blocks)]

    for step in range(n):
        for c in pulls(step):
            c.start()
    late = begin(sem_in, 2, (gbr_h, gbr), (normed01, normed.at[0:2]), (normed23, normed.at[2:4]), (wb_h, wb), (wi_h, wi))
    zext[:, rows:rows + 8] = jnp.zeros((3, 8, width), F32)
    sm_v[...] = jnp.zeros(sm_v.shape, F32)
    wait(early)

    def block(step, after):
        wait(pulls(step))
        t = n - 1 - step
        r = jnp.bitwise_xor(t, me_ref[0])
        m = masks[t]
        adj, head = scan_groups(later[r], gs[r], after, True)
        grp = (adj * f2[r].astype(F32)).astype(BF)
        ggp = (adj * f3[r].astype(F32)).astype(BF)
        pair = jnp.concatenate([grp, ggp], axis=1)
        pair_s[r] = pair
        gconv = adj * f4[r].astype(F32) + mm_nt(pair, wrg[...])
        ri = ri_v[r].astype(F32)
        gri = cw[0:1] * gconv
        sums = [jnp.sum(ri * gconv, axis=0, keepdims=True)]
        for k in (1, 2, 3):
            z = gconv * m[:, k - 1:k]
            zext[k - 1, 0:rows] = z
            moved = zext[k - 1, k:k + rows]
            zext[k - 1, rows:rows + 8] = z[0:8]
            gri = gri + cw[k:k + 1] * moved
            sums.append(jnp.sum(ri * moved, axis=0, keepdims=True))
        sums.append(jnp.sum(gconv, axis=0, keepdims=True))
        sums.append(jnp.sum(grp.astype(F32), axis=0, keepdims=True))
        sums.append(jnp.sum(ggp.astype(F32), axis=0, keepdims=True))
        sums.append(jnp.sum(adj * f1[r].astype(F32), axis=0, keepdims=True))
        sm_v[...] += jnp.concatenate(sums, axis=0)
        gri_v[r] = gri.astype(BF)
        return head

    lax.fori_loop(0, n, block, jnp.zeros((1, width), F32))
    wait(late)
    out = []
    gain1 = jnp.zeros((1, d), F32)
    for k, (i, ref) in enumerate(((3, n31.at[0]), (1, n31.at[1]), (2, n2), (0, n0))):
        part = mm_nt(gbr[i], wb[...]) + mm_nt(gri_v[i], wi[...])
        p_v[i] = part.astype(BF)
        out += begin(sem_out, k, (p_v.at[i], ref))
        gain1 = gain1 + jnp.sum(part * normed[i].astype(F32), axis=0, keepdims=True)

    def as_rows(v):
        v = jnp.concatenate([v, jnp.zeros((1, 3 * width - d), F32)], axis=1)
        return [v[:, i * width:(i + 1) * width] for i in range(3)]

    last_v[0:d] = mm_tn(flat(normed), flat(gri_v)).astype(BF)
    dw = mm_tn(flat(cv_v), flat(pair_s))
    hd = width // 2
    left = lax.broadcasted_iota(jnp.int32, (hd, width), 1) < hd
    for k in (0, 1):
        mine = dw[:, k * width:(k + 1) * width]
        last_v[d + k * hd:d + (k + 1) * hd] = jnp.where(left, mine[:hd], mine[hd:]).astype(BF)
    rest = last_v.shape[0] - d - 2 * hd
    few = [sm_v[...]] + as_rows(gain1) + as_rows(gain2[...]) + [jnp.zeros((rest - 14, width), F32)]
    last_v[d + 2 * hd:] = jnp.concatenate(few, axis=0).astype(BF)
    cut = last_v.shape[0] // 2
    halves = last_v.at[0:cut], last_v.at[cut:2 * cut]
    for part in (0, 1):
        @pl.when(y_ref[0] == part)
        def _():
            wait(begin(sem_out, 4, (halves[part], keep_o), (halves[1 - part], send_o)))
    wait(out)


def ends_branch(y_ref, cur, got, branch_o, out_o):
    for part in (0, 1):
        @pl.when(y_ref[0] == part)
        def _():
            pair = (cur, got) if part == 0 else (got, cur)
            branch_o[...] = pair[0][...].astype(F32)
            out_o[...] = pair[1][...].astype(F32).T


def ends_input(y_ref, cur, got, input_o, recur_o, gate_o, few_o, gains_o, whole):
    d, hd = input_o.shape[0], recur_o.shape[1]
    cut = whole.shape[0] // 2
    for part in (0, 1):
        @pl.when(y_ref[0] == part)
        def _():
            whole[part * cut:(part + 1) * cut] = cur[...]
            whole[(1 - part) * cut:(2 - part) * cut] = got[...]
    input_o[...] = whole[0:d].astype(F32)
    for k, ref in enumerate((recur_o, gate_o)):
        both_heads = whole[d + k * hd:d + (k + 1) * hd].astype(F32)
        for i in range(recur_o.shape[0]):
            ref[i] = both_heads[:, i * hd:(i + 1) * hd]
    few = whole[d + 2 * hd:d + 2 * hd + 16].astype(F32)
    few_o[...] = few[0:8]
    for k in (0, 1):
        at = 8 + 3 * k
        gains_o[k:k + 1] = jnp.concatenate([few[at + i:at + i + 1] for i in range(3)], axis=1)[:, :gains_o.shape[1]]


def mlp_blocks(xb, cot, wg, wu, wd, hid, gg, gu, p_v, ready, base):
    for i in range(xb.shape[0]):
        wait(ready[i])
        x = xb[i]
        ga = mm(x, wg[...])
        if i == 0:
            wait(ready[-1][:1])
        ua = mm(x, wu[...])
        if i == 0:
            wait(ready[-1][1:])
        gh = mm_nt(cot[base + i], wd[...])
        gl, slope = gelu_both(ga)
        hid[base + i] = (gl * ua).astype(BF)
        gg[i] = (gh * ua * slope).astype(BF)
        gu[i] = (gh * gl).astype(BF)
    for i in reversed(range(xb.shape[0])):
        p_v[i] = (mm_nt(gg[i], wg[...]) + mm_nt(gu[i], wu[...])).astype(BF)


def mlp_pre(
    b0, b1, c0, c1, wg_h, wu_h, wd_h, hid_h, gg_h, gu_h, n0, n1,
    xb, cot, wg, wu, wd, hid, gg, gu, p_v, sem_in, sem_out,
):
    first = begin(sem_in, 0, (b0, xb.at[0]), (wg_h, wg))
    then = begin(sem_in, 2, (wu_h, wu), (c0, cot.at[0]), (wd_h, wd))
    second = begin(sem_in, 5, (b1, xb.at[1]), (c1, cot.at[1]))
    mlp_blocks(xb, cot, wg, wu, wd, hid, gg, gu, p_v, (first, second, then), 0)
    wait(begin(sem_out, 0, (hid, hid_h), (gg, gg_h), (gu, gu_h), (p_v.at[1], n1), (p_v.at[0], n0)))


def mlp_main(
    y_ref, b2, b3, c0, c1, c2, c3, hid01, n1, wg_h, wu_h, wd_h, hid_h, gg_h, gu_h, n2, n31, dk_o, ds_o,
    xb, cot, wg, wu, wd, hid, gg, gu, p_v, dd, sem_in, sem_out,
):
    rows, units = hid.shape[1:]
    first = begin(sem_in, 0, (b2, xb.at[0]), (wg_h, wg))
    then = begin(sem_in, 2, (wu_h, wu), (c2, cot.at[2]), (wd_h, wd))
    second = begin(sem_in, 5, (b3, xb.at[1]), (c3, cot.at[3]))
    last = begin(sem_in, 7, (c0, cot.at[0]), (c1, cot.at[1]), (hid01, hid.at[0:2]), (n1, n31.at[1]))
    mlp_blocks(xb, cot, wg, wu, wd, hid, gg, gu, p_v, (first, second, then), 2)
    n31[0] = p_v[1]
    n2[...] = p_v[0]
    out = begin(sem_out, 0, (hid.at[2:4], hid_h), (gg, gg_h), (gu, gu_h))
    wait(last)
    call_ = cot[...].reshape(4 * rows, cot.shape[2])
    hall = hid[...].reshape(4 * rows, units)
    half = units // 2
    for part in (0, 1):
        dd[part] = mm_tn(hall[:, part * half:(part + 1) * half], call_).astype(BF)
    for part in (0, 1):
        @pl.when(y_ref[0] == part)
        def _():
            wait(begin(sem_out, 5, (dd.at[part], dk_o), (dd.at[1 - part], ds_o)))
    wait(out)


def mlp_post(
    y_ref, z_ref, b0, b1, b2, b3, gg01, gg23, gu01, gu23, hid01, hid23, wd_h, gk_o, gs_o, uk_o, us_o, m0, m2, m31,
    xb, gg, gu, hid, wd, dg, du, p_v, sem_in, sem_out,
):
    n, rows, units = hid.shape
    first = begin(sem_in, 0, (b0, xb.at[0]), (b1, xb.at[1]), (b2, xb.at[2]), (b3, xb.at[3]),
                  (gg01, gg.at[0:2]), (gg23, gg.at[2:4]))
    second = begin(sem_in, 6, (gu01, gu.at[0:2]), (gu23, gu.at[2:4]))
    third = begin(sem_in, 8, (hid01, hid.at[0:2]), (hid23, hid.at[2:4]), (wd_h, wd))

    def flat(ref):
        return ref[...].reshape(n * rows, ref.shape[2])

    wait(first)
    xall = flat(xb)
    half = dg.shape[1]
    for part in (0, 1):
        dg[part] = mm_tn(xall[:, part * half:(part + 1) * half], flat(gg)).astype(BF)
    wait(second)
    for part in (0, 1):
        du[part] = mm_tn(xall[:, part * half:(part + 1) * half], flat(gu)).astype(BF)
    for part in (0, 1):
        @pl.when(y_ref[0] == part)
        def _():
            begin(sem_out, 4, (dg.at[part], gk_o), (dg.at[1 - part], gs_o))

        @pl.when(z_ref[0] == part)
        def _():
            begin(sem_out, 6, (du.at[part], uk_o), (du.at[1 - part], us_o))
    out = []
    wait(third)
    for k, (i, ref) in enumerate(((3, m31.at[0]), (1, m31.at[1]), (2, m2), (0, m0))):
        p_v[i] = mm(hid[i], wd[...]).astype(BF)
        out += begin(sem_out, k, (p_v.at[i], ref))
    wait(out)
    wait([pltpu.make_async_copy(v.at[0], o, sem_out.at[4 + k])
          for k, (v, o) in enumerate(((dg, gk_o), (dg, gs_o), (du, uk_o), (du, us_o)))])


def add_two(a, b, got_a, got_b, send_o, own_o):
    send_o[...] = plus(a[...], got_a[...]).astype(BF)
    own_o[...] = plus(b[...], got_b[...]).astype(BF)


def add_both(i2, i0, o2, o0, got_i, got_o, send_o, own_i, own_o):
    send_o[0] = plus(i2[...], got_i[0]).astype(BF)
    own_i[...] = plus(i0[...], got_i[1]).astype(BF)
    send_o[1] = plus(o2[...], got_o[0]).astype(BF)
    own_o[...] = plus(o0[...], got_o[1]).astype(BF)


def add_pair(a, b, got, send_o, own_o):
    send_o[...] = plus(a[...], got[0]).astype(BF)
    own_o[...] = plus(b[...], got[1]).astype(BF)


def mid_fwd(x, own, far, gain, mid_o, n_o):
    mid = x[...].astype(F32) + plus(own[...], far[...])
    inv = lax.rsqrt(jnp.mean(mid * mid, axis=-1, keepdims=True) + EPSILON)
    mid_o[...] = mid
    n_o[...] = (mid * inv * gain[...]).astype(BF)


def norm_back(total, values, gain):
    inv = lax.rsqrt(jnp.mean(values * values, axis=-1, keepdims=True) + EPSILON)
    v = total * gain
    scaled = values * inv
    mean = jnp.mean(v * scaled, axis=-1, keepdims=True)
    grad = inv * (v - scaled * mean)
    return grad, jnp.sum(total * scaled, axis=0, keepdims=True)


def mid_bwd(mid, own, far, gain, cot, gm_o, gb_o, gg_o):
    grad, gsum = norm_back(plus(own[...], far[...]), mid[...], gain[...])
    gm = cot[...].astype(F32) + grad
    gm_o[...] = gm
    gb_o[...] = gm.astype(BF)
    gg_o[...] = gsum


def last_bwd(x, mid, own_i, own_o, far, gain, gm, o, out_o):
    grad, _ = norm_back(plus(own_i[...], far[0]), x[...].astype(F32), gain[...])
    o[...] = gm[...] + grad
    out_o[...] = (mid[...] + plus(own_o[...], far[1])).astype(BF)


def cost(us):
    return pl.CostEstimate(flops=1 + int(us * 1.15e9), bytes_accessed=0, transcendentals=0)


HBM, VMEM, SMEM = pltpu.HBM, pltpu.VMEM, pltpu.SMEM


def call(kernel, outs, *args, name, us, mib, places, out, scratch=()):
    spec = {"h": HBM, "v": VMEM, "s": SMEM, "a": pl.ANY}
    args = [
        pltpu.with_memory_space_constraint(a, VMEM if p == "v" else HBM) if p in "hv" else a
        for p, a in zip(places, args, strict=True)
    ]
    return pl.pallas_call(
        kernel,
        out_shape=[(VMEM if p == "v" else HBM)(*o) for p, o in zip(out, outs, strict=True)],
        in_specs=[pl.BlockSpec(memory_space=spec[p]) if p in spec else pl.BlockSpec() for p in places],
        out_specs=[pl.BlockSpec(memory_space=spec[p]) if p in spec else pl.BlockSpec() for p in out],
        scratch_shapes=list(scratch),
        compiler_params=pltpu.CompilerParams(vmem_limit_bytes=mib * MIB),
        cost_estimate=cost(us),
        name=name,
    )(*args)


CORE = [(i, i ^ 1) for i in range(4)]
FAR = [(i, i ^ 2) for i in range(4)]


def to_core(v):
    return lax.ppermute(v, "ch", CORE)


def to_far(v):
    return lax.ppermute(v, "ch", FAR)


class Order:
    def __init__(self):
        self.last = None

    def run(self, work, *values):
        if self.last is not None:
            values = lax.optimization_barrier((*values, *self.last))[:len(values)]
        got = work(*values)
        self.last = tuple(got) if isinstance(got, (tuple, list)) else (got,)
        return got

    def gate(self, value):
        return lax.optimization_barrier((value, *self.last))[0]

    def take(self, value):
        return self.run(lambda v: (v,), value)[0]


def dyn(g, index, size):
    return lax.dynamic_slice_in_dim(g, index * size, size, 0)


def plus(a, b):
    return a.astype(F32) + b.astype(F32)


def add_low(a, b):
    return plus(a, b).astype(BF)


def put(total, piece, index):
    return lax.dynamic_update_slice_in_dim(total, piece.astype(total.dtype), index * piece.shape[0], 0)


Y = [(i, i ^ 1) for i in range(8)]
Z1 = [(i, i ^ 2) for i in range(8)]
Z2 = [(i, i ^ 4) for i in range(8)]
def both(low, a, b):
    return jnp.concatenate([jnp.where(low, a, b), jnp.where(low, b, a)], 0)


def sum_rows_plain(keep, send, ends):
    yield "sent"
    return ends(*(lax.psum(v.astype(F32), "rows").astype(BF) for v in (keep, send)))


INWARD = [(0, 2), (1, 3), (6, 4), (7, 5)]
MIDDLE = [(2, 4), (3, 5), (4, 2), (5, 3)]
OUTWARD = [(2, 0), (3, 1), (4, 6), (5, 7)]


def send_on(value, pairs, order):
    if (yield "ready"):
        value = order.gate(value)
    got = lax.ppermute(value, "rows", pairs)
    yield "sent"
    return order.take(got)


def sum_rows_halves(keep, send, order, way, ends):
    me = lax.axis_index("rows")
    y, z = (Y, me % 2), (Z1, (me // 2) % 2)
    stages = ((y, z) if way == "y" else (z, y)) + ((Z2, me // 4),)
    got = yield from send_on(send, stages[0][0], order)
    yield "came"
    for pairs, bit in stages[1:]:
        half = keep.shape[0] // 2

        def split(a, b, bit=bit, half=half):
            return (add_low(dyn(a, 1 - bit, half), dyn(b, 1 - bit, half)), add_low(dyn(a, bit, half), dyn(b, bit, half)))

        send, keep = order.run(split, keep, got)
        got = yield from send_on(send, pairs, order)
        yield "came"
    cur = order.run(add_low, keep, got)
    for pairs, bit in stages[::-1]:
        got = yield from send_on(cur, pairs, order)
        yield "came"
        if pairs is stages[0][0]:
            return order.run(ends, cur, got)
        cur = order.run(lambda a, b, bit=bit: both(bit == 0, a, b), cur, got)


def sum_rows_line(keep, send, order, ends):
    me = lax.axis_index("rows")
    y, z = me % 2, me // 2
    inner = (z == 1) | (z == 2)
    got = yield from send_on(send, Y, order)
    yield "came"
    cur = order.run(add_low, keep, got)
    for pairs in (INWARD, MIDDLE):
        got = yield from send_on(cur, pairs, order)
        yield "came"
        cur = order.run(add_low, cur, got)
    got = yield from send_on(cur, OUTWARD, order)
    yield "came"
    cur = order.run(lambda a, b: jnp.where(inner, a, b), cur, got)
    got = yield from send_on(cur, Y, order)
    yield "came"
    return order.run(ends, cur, got)


class Chain:
    def __init__(self, steps):
        self.steps, self.value, self.state, self.held = steps, None, None, False
        self.go()

    def step(self, first=False):
        try:
            self.state = self.steps.send(None if self.state is None else self.held)
            self.held = False
        except StopIteration as end:
            self.state, self.value = "done", end.value

    def to(self, state):
        if self.state == "done":
            return
        self.step()
        while self.state not in (state, "done"):
            self.step()
        self.held = state == "ready"

    def come(self):
        if self.state == "sent":
            self.to("came")

    def go(self):
        self.to("sent")

    def finish(self):
        while self.state != "done":
            self.go()
        return self.value


def block_diag(w):
    h, d, e = w.shape
    rows = [
        jnp.concatenate([w[i] if i == j else jnp.zeros((d, e), w.dtype) for j in range(h)], axis=1)
        for i in range(h)
    ]
    return jnp.concatenate(rows, axis=0)


def body(n_rows, inputs, segment_ids, mixer_gain, branch_weight, input_weight, conv_weight, conv_bias,
         recur_weight, recur_bias, gate_weight, gate_bias, decay_param, out_weight, mlp_gain, mlp_gate,
         mlp_up, mlp_down, cotangent):
    x = inputs[0]
    cot = cotangent[0]
    rows, d = x.shape
    width = branch_weight.shape[1]
    units = mlp_gate.shape[1]
    heads, hd, _ = recur_weight.shape
    seq = segment_ids.shape[1]
    n = seq // rows
    me = lax.axis_index("ch").astype(jnp.int32)[None]
    gain1 = mixer_gain[None]
    gain2 = mlp_gain[None]
    order = Order()
    row = lax.axis_index("rows").astype(jnp.int32)[None]
    y_half = row % 2 if n_rows == 8 else jnp.zeros((1,), jnp.int32)
    z_half = (row // 2) % 2 if n_rows == 8 else jnp.zeros((1,), jnp.int32)

    split = {k: z_half if v == "z" else y_half for k, v in KINDS.items()}

    def total(keep, send, way, ends):
        if n_rows != 8:
            return Chain(sum_rows_plain(keep, send, ends))
        if way == "line":
            return Chain(sum_rows_line(keep, send, order, ends))
        return Chain(sum_rows_halves(keep, send, order, way, ends))

    x_far, x_near = to_far(x), to_core(x)

    def tables(ids, rw, gw, rb, gb_, dp):
        marks = [
            (jnp.pad(ids, (k, 0), constant_values=-1)[:seq] == ids).astype(F32) for k in (1, 2, 3)
        ]
        masks = jnp.pad(jnp.stack(marks, axis=1), ((0, 0), (0, 125))).reshape(n, rows, 128)
        wrg = jnp.concatenate([block_diag(rw), block_diag(gw)], axis=1)
        return masks, wrg, jnp.concatenate([rb, gb_])[None], (-8.0 * jax.nn.softplus(dp))[None]

    masks, wrg, brg, c8 = order.run(
        tables, segment_ids[0], recur_weight, gate_weight, recur_bias, gate_bias, decay_param
    )
    cb = conv_bias[None]
    blk, narrow, wide = (rows, d), (n, rows, width), (n, rows, units)
    four, two = (n, rows, d), (2, rows, d)
    narrow2, wide2 = (2, rows, width), (2, rows, units)
    dma = pltpu.SemaphoreType.DMA
    normed01, br01, ri01 = order.run(
        functools.partial(
            call, mixer_pre, [(two, BF), (narrow2, F32), (narrow2, F32)], name="mixer_pre", us=0, mib=20,
            places="aahhi", out="hhh", scratch=[
                VMEM(two, BF), VMEM((d, width), BF), VMEM((d, width), BF), VMEM(two, BF), VMEM(narrow2, F32),
                VMEM(narrow2, F32), dma((4,)), dma((3,)),
            ]),
        x, x_near, branch_weight, input_weight, gain1)
    x_far = order.take(x_far)
    x_diag = to_core(x_far)
    cot_far = to_far(cot)
    x_diag = order.take(x_diag)
    fwd = order.run(
        functools.partial(
            call, mixer_fwd,
            [(two, BF), (narrow2, F32), (narrow, BF), (narrow, BF), (narrow, F32), (narrow, BF)] + [(blk, BF)] * 4,
            name="mixer_fwd", us=0, mib=30, places="saahhhhhhhiiiii", out="h" * 6 + "vvvv", scratch=[
                VMEM(two, BF), VMEM((d, width), BF), VMEM((d, width), BF), VMEM((width, 2 * width), BF),
                VMEM((n, rows, 128), F32), VMEM((width, d), BF), VMEM(two, BF), VMEM(narrow, F32),
                VMEM(narrow, F32), VMEM(narrow, BF), VMEM(narrow, BF), VMEM(narrow, F32), VMEM(narrow, BF),
                VMEM((rows + 8, width), F32), VMEM((rows + 8, width), F32), dma((9,)), dma((6,)),
            ]),
        me, x_far, x_diag, branch_weight, input_weight, br01, ri01, wrg, masks, out_weight, gain1, conv_weight, cb,
        brg, c8)
    normed23, br23, ri, cv, sp, mix = fwd[:6]
    cot_far = order.take(cot_far)

    def near_half(own, far, pair):
        got = to_core(pair)
        return order.run(
            functools.partial(call, add_pair, [(blk, BF)] * 2, name="add_pair", us=0, mib=6, places="iii", out="vv"),
            far, own, got)

    send, own = order.run(
        functools.partial(call, add_two, [(blk, BF)] * 2, name="add_two", us=0, mib=6, places="vvii", out="vv"),
        fwd[7], fwd[6], to_core(fwd[8]), to_core(fwd[9]))
    far = to_far(send)
    cot_near, cot_diag = to_core(cot), to_core(cot_far)
    cot_near = order.take(cot_near)
    cot_diag = order.take(cot_diag)
    a1, gl, later, *fs = order.run(
        functools.partial(
            call, mixer_mid, [(narrow, BF), (narrow, BF), (narrow, F32)] + [(narrow, BF)] * 4, name="mixer_mid", us=0,
            mib=30, places="s" + "h" * 6 + "ii", out="h" * 7, scratch=[
                VMEM(narrow, F32), VMEM(narrow, BF), VMEM(narrow, F32), VMEM((width, 2 * width), BF),
                VMEM((n, rows, 128), F32), VMEM(narrow, BF), VMEM(narrow, BF), VMEM(narrow, F32)]
            + [VMEM(narrow, BF)] * 4 + [VMEM((rows + 8, width), F32), dma((6,)), dma((7,))]),
        me, br01, br23, cv, sp, wrg, masks, brg, c8)
    mid, normed2 = order.run(functools.partial(
        call, mid_fwd, [(blk, F32), (blk, BF)], name="mid_fwd", us=0, mib=8, places="ivvi", out="iv"),
        x, own, far, gain2)
    n_far, n_near = to_far(normed2), to_core(normed2)
    n_near = order.take(n_near)
    mlp_scratch = [
        VMEM((d, units), BF), VMEM((d, units), BF), VMEM((units, d), BF)]
    hid01, gg01, gu01, g0, g1 = order.run(
        functools.partial(
            call, mlp_pre, [(wide2, BF)] * 3 + [(blk, BF)] * 2, name="mlp_pre", us=0, mib=30, places="aahhhhh",
            out="h" * 5, scratch=[VMEM(two, BF), VMEM(two, BF)] + mlp_scratch + [VMEM(wide2, BF)] * 3 + [
                VMEM(two, BF), dma((7,)), dma((5,))]),
        normed2, n_near, cot, cot_near, mlp_gate, mlp_up, mlp_down)
    n_far = order.take(n_far)
    n_diag = order.take(to_core(n_far))
    hid23, gg23, gu23, g2, g31, down_keep, down_send = order.run(
        functools.partial(
            call, mlp_main, [(wide2, BF)] * 3 + [(blk, BF), (two, BF)] + [((units // 2, d), BF)] * 2, name="mlp_main",
            us=0, mib=26, places="saahhhhhhhhh", out="hhhvvhh",
            scratch=[VMEM(two, BF), VMEM(four, BF)] + mlp_scratch + [VMEM(wide, BF), VMEM(wide2, BF), VMEM(wide2, BF)] + [
                VMEM(two, BF), VMEM((2, units // 2, d), BF), dma((11,)), dma((7,))]),
        split["d"], n_far, n_diag, cot, cot_near, cot_far, cot_diag, hid01, g1, mlp_gate, mlp_up, mlp_down)
    y_low, z_low = y_half[0] == 0, z_half[0] == 0

    def wide_ends(low, a, b):
        return both(low, a, b).astype(F32)

    def ends_of(kind):
        return functools.partial(wide_ends, y_low if split[kind] is y_half else z_low)

    s_down = total(down_keep, down_send, KINDS["d"], ends_of("d"))
    g_send, g_own = near_half(g0, g2, g31)
    from_far = to_far(g_send)
    post = order.run(
        functools.partial(
            call, mlp_post, [((d // 2, units), BF)] * 4 + [(blk, BF), (blk, BF), (two, BF)], name="mlp_post", us=0,
            mib=26, places="ssaaaahhhhhhh", out="h" * 7, scratch=[
                VMEM(four, BF), VMEM(wide, BF), VMEM(wide, BF), VMEM(wide, BF), VMEM((units, d), BF),
                VMEM((2, d // 2, units), BF), VMEM((2, d // 2, units), BF), VMEM(four, BF), dma((11,)), dma((8,)),
            ]),
        split["g"], split["u"], normed2, n_near, n_far, n_diag, gg01, gg23, gu01, gu23, hid01, hid23, mlp_down)
    s_gate = total(post[0], post[1], KINDS["g"], ends_of("g"))
    s_up = total(post[2], post[3], KINDS["u"], ends_of("u"))
    chains = {"d": s_down, "g": s_gate, "u": s_up}
    live = {}

    def at_rf():
        gm, gb, gsum2 = order.run(functools.partial(
            call, mid_bwd, [(blk, F32), (blk, BF), ((1, d), F32)], name="mid_bwd", us=10, mib=8, places="ivvii", out="ivi"),
            mid, g_own, from_far, gain2, cot)
        g_near, g_far = to_core(gb), to_far(gb)
        live.update(gm=gm, gb=gb, gsum2=gsum2, g_near=g_near, g_far=g_far)

    def at_gf():
        gb = live["gb"]
        g_far = order.take(live["g_far"])
        g_diag = to_core(g_far)
        g_near = order.take(live["g_near"])
        g_diag = order.take(g_diag)
        gs, gbr, p_keep, p_send = order.run(
            functools.partial(
                call, mixer_out, [(narrow, F32), (narrow, BF)] + [((d, width), BF)] * 2, name="mixer_out", us=0, mib=30,
                places="shhaa" + "h" * 6, out="h" * 4, scratch=[
                    VMEM(four, BF), VMEM((width, d), BF), VMEM(narrow, BF), VMEM(narrow, BF), VMEM(four, BF),
                    VMEM(narrow, BF), VMEM(narrow, F32), VMEM(narrow, BF), VMEM((2, d, width), BF), dma((10,)), dma((4,))]),
            split["p"], gb, g_near, g_far, g_diag, out_weight, a1, gl, normed01, normed23, mix)
        chains["p"] = total(p_keep, p_send, KINDS["p"], functools.partial(
            call, ends_branch, [((d, width), F32), ((width, d), F32)], split["p"], name="ends_branch", us=0, mib=16,
            places="sii", out="ii"))
        live.update(gs=gs, gbr=gbr)

    def at_m():
        last_rows = d + 2 * hd + 64
        bwd = order.run(
            functools.partial(
                call, mixer_bwd, [(blk, BF), (blk, BF), (two, BF)] + [((last_rows // 2, width), BF)] * 2,
                name="mixer_bwd", us=0, mib=36, places="ss" + "h" * 15 + "ii", out="h" * 5, scratch=[
                    VMEM(narrow, F32), VMEM(narrow, F32)] + [VMEM(narrow, BF)] * 6 + [
                    VMEM((width, 2 * width), BF), VMEM((n, rows, 128), F32), VMEM(narrow, BF), VMEM(four, BF),
                    VMEM((d, width), BF), VMEM((d, width), BF), VMEM((n, rows, 2 * width), BF), VMEM(narrow, BF),
                    VMEM(four, BF), VMEM((last_rows, width), BF), VMEM((8, width), F32), VMEM((3, rows + 8, width), F32),
                    dma((8, n)), dma((8,)), dma((6,)),
                ]),
            me, split["q"], live["gs"], later, *fs, ri, cv, wrg, masks, live["gbr"], normed01, normed23, branch_weight, input_weight,
            conv_weight, live["gsum2"])
        chains["q"] = total(bwd[3], bwd[4], KINDS["q"], functools.partial(
            call, ends_input, [((d, width), F32), ((heads, hd, hd), F32), ((heads, hd, hd), F32), ((8, width), F32),
             ((2, d), F32)], split["q"], name="ends_input", us=0, mib=16, places="sii", out="iiiii", scratch=[VMEM((last_rows, width), BF)]))

        live.update(bwd=bwd)

    def sum_ch(n0, n2, pair):
        got_i, got_o = to_core(order.gate(pair)), to_core(order.gate(post[6]))
        yield "sent"
        got_i, got_o = order.run(lambda a, b: (a, b), got_i, got_o)
        yield "came"
        send, own_i, own_o = order.run(
            functools.partial(
                call, add_both, [(two, BF), (blk, BF), (blk, BF)], name="add_both", us=0, mib=14, places="iiiiii", out="uuu"),
            n2, n0, post[5], post[4], got_i, got_o)
        far = to_far(send)
        yield "sent"
        far = order.take(far)
        yield "came"
        return order.run(
            functools.partial(
                call, last_bwd, [(blk, F32), (blk, BF)], name="last_bwd", us=0, mib=14, places="iiiiiii", out="ii"),
            x, mid, own_i, own_o, far, gain1, live["gm"])

    events = {"rf": at_rf, "gf": at_gf, "m": at_m}

    def turn(what):
        if what in events:
            events[what]()
            return
        if what == "c":
            if "bwd" in live and "i" not in chains and chains["d"].state == "done":
                chains["i"] = Chain(sum_ch(*live["bwd"][:3]))
            return
        chains[what].go()

    for what in PLAN:
        turn(what)
    while "i" not in chains or any(c.state != "done" for c in chains.values()):
        for what in PLAN_AFTER:
            if what in chains or what == "c":
                turn(what)
    input_grad, output = chains["i"].value
    t_branch, t_out = chains["p"].value
    t_input, t_recur, t_gate_w, ts, gains = chains["q"].value
    t_down, t_gate, t_up = (s.value for s in (s_down, s_gate, s_up))
    gains = order.run(jnp.add, gains, to_core(gains))
    gains = order.run(jnp.add, gains, to_far(gains))
    decay_grad = ts[7] * -8.0 * jax.nn.sigmoid(decay_param)
    return (
        output[None],
        input_grad[None],
        gains[0] / mixer_gain,
        t_branch,
        t_input,
        ts[0:4],
        ts[4],
        t_recur,
        ts[5],
        t_gate_w,
        ts[6],
        decay_grad,
        t_out,
        gains[1],
        t_gate,
        t_up,
        t_down,
    )


def solution(mesh):
    rows, ch = P("rows", "ch", None), P("ch")
    cols, lead = P(None, "ch"), P("ch", None)
    heads = P("ch", None, None)
    return jax.shard_map(
        functools.partial(body, mesh.shape["rows"]),
        mesh=mesh,
        in_specs=(rows, P("rows", None), P(), cols, cols, cols, ch, heads, ch, heads, ch, ch, lead, P(),
                  cols, cols, lead, rows),
        out_specs=(rows, rows, P(), cols, cols, cols, ch, heads, ch, heads, ch, ch, lead, P(), cols, cols, lead),
        check_vma=False,
    )
```

```python
import functools

import jax
import jax.numpy as jnp
from jax import lax
from jax.experimental import pallas as pl
from jax.experimental.pallas import tpu as pltpu
from jax.sharding import PartitionSpec as P

EPSILON = 1e-06
BF = jnp.bfloat16
F32 = jnp.float32
MIB = 1024 * 1024
KINDS = {"d": "line", "g": "line", "u": "z", "p": "line", "q": "line"}
PLAN_AFTER = ("u", "g", "d", "p", "q", "i", "c")
PLAN = ("d", "rf", "u", "g", "gf", "d", "m", "u", "g", "d", "p", "q")
GELU_C = 0.7978845608028654
GELU_A = 0.044715


def mm(a, b):
    return lax.dot_general(a, b, (((1,), (0,)), ((), ())), preferred_element_type=F32)


def mm_nt(a, b):
    return lax.dot_general(a, b, (((1,), (1,)), ((), ())), preferred_element_type=F32)


def mm_tn(a, b):
    return lax.dot_general(a, b, (((0,), (0,)), ((), ())), preferred_element_type=F32)


def sigmoid(v):
    return 0.5 * jnp.tanh(0.5 * v) + 0.5


def gelu_both(v):
    sq = v * v
    th = jnp.tanh(GELU_C * v * (1.0 + GELU_A * sq))
    half = 0.5 * th + 0.5
    slope = half + (0.5 * GELU_C) * v * (1.0 - th * th) * (1.0 + (3.0 * GELU_A) * sq)
    return v * half, slope


def gelu_only(v):
    th = jnp.tanh(GELU_C * v * (1.0 + GELU_A * (v * v)))
    return v * (0.5 * th + 0.5)


def scan_groups(mult, add, start, back):
    rows, cols = mult.shape
    a = mult.reshape(rows // 8, 8, cols)
    d = add.reshape(rows // 8, 8, cols)
    sub = lax.broadcasted_iota(jnp.int32, (1, 8, cols), 1)
    for k in (1, 2, 4):
        ok = sub < 8 - k if back else sub >= k
        turn = 8 - k if back else k
        d = d + a * jnp.where(ok, pltpu.roll(d, turn, 1), 0.0)
        a = a * jnp.where(ok, pltpu.roll(a, turn, 1), 1.0)
    state = start
    got = [None] * (rows // 8)
    order = range(rows // 8)
    for g in reversed(order) if back else order:
        now = d[g] + a[g] * state
        state = now[0:1] if back else now[7:8]
        got[g] = now
    return jnp.concatenate(got, axis=0), state


def gate_values(conv, pre, c8, width):
    rg = sigmoid(pre[:, :width])
    ig = sigmoid(pre[:, width:])
    forget = jnp.exp(c8 * rg)
    om = 1.0 - forget * forget
    top = jnp.maximum(om, 0.001)
    inv = lax.rsqrt(top)
    return rg, ig, forget, om, top * inv, inv


def begin(sem, first, *pairs):
    copies = [pltpu.make_async_copy(src, dst, sem.at[first + k]) for k, (src, dst) in enumerate(pairs)]
    for c in copies:
        c.start()
    return copies


def wait(copies):
    for c in copies:
        c.wait()


def project(x, gain, wb, wi):
    x = x.astype(F32)
    inv = lax.rsqrt(jnp.mean(x * x, axis=-1, keepdims=True) + EPSILON)
    normed = (x * inv * gain).astype(BF)
    return normed, mm(normed, wb), mm(normed, wi)


def mixer_pre(b0, b1, wb_h, wi_h, gain, normed_h, br_h, ri_h, xb, wb, wi, normed_v, br_v, ri_v, sem_in, sem_out):
    first = begin(sem_in, 0, (b0, xb.at[0]), (wb_h, wb), (wi_h, wi))
    second = begin(sem_in, 3, (b1, xb.at[1]))
    for i, ready in enumerate((first, second)):
        wait(ready)
        normed_v[i], br_v[i], ri_v[i] = project(xb[i], gain[...], wb[...], wi[...])
    wait(begin(sem_out, 0, (normed_v, normed_h), (br_v, br_h), (ri_v, ri_h)))


def mixer_fwd(
    me_ref, b2, b3, wb_h, wi_h, br01, ri01, wrg_h, masks_h, wo_h, gain, cw, cb, brg, c8,
    normed_h, br_h, ri_h, cv_h, sp_h, mix_h, p0, p2, p3, p1,
    xb, wb, wi, wrg, masks, wo, normed_v, br_v, ri_s, ri_v, cv_v, sp_v, mix_v, ext, sext, sem_in, sem_out,
):
    n, rows, width = br_v.shape
    first = begin(sem_in, 0, (b2, xb.at[0]), (wb_h, wb), (wi_h, wi))
    second = begin(sem_in, 3, (b3, xb.at[1]))
    later = begin(sem_in, 4, (ri01, ri_s.at[0:2]), (wrg_h, wrg), (masks_h, masks), (br01, br_v.at[0:2]), (wo_h, wo))
    for i, ready in enumerate((first, second)):
        wait(ready)
        normed_v[i], br_v[2 + i], ri_s[2 + i] = project(xb[i], gain[...], wb[...], wi[...])
    out = begin(sem_out, 0, (normed_v, normed_h), (br_v.at[2:4], br_h))
    ext[0:8] = jnp.zeros((8, width), F32)
    wait(later)

    def block(t, first):
        r = jnp.bitwise_xor(t, me_ref[0])
        ri = ri_s[r]
        ri_v[r] = ri.astype(BF)
        ext[8:8 + rows] = ri
        m = masks[t]
        conv = cb[...] + cw[0:1] * ri
        for k in (1, 2, 3):
            conv = conv + cw[k:k + 1] * (ext[8 - k:8 - k + rows] * m[:, k - 1:k])
        ext[0:8] = ext[rows:rows + 8]
        cv = conv.astype(BF)
        cv_v[r] = cv
        cvf = cv.astype(F32)
        pre = mm(cv, wrg[...]) + brg[...]
        rg, ig, forget, om, scale, _ = gate_values(cvf, pre, c8[...], width)
        keep = m[:, 0:1]
        states, last = scan_groups(forget * keep, scale * ig * cvf, first, False)
        sext[8:8 + rows] = states
        sext[7:8] = first
        sp_v[r] = sext[7:7 + rows] * keep
        mix_v[r] = (gelu_only(br_v[r]) * states).astype(BF)
        return last

    lax.fori_loop(0, n, block, jnp.zeros((1, width), F32))
    out += begin(sem_out, 2, (ri_v, ri_h), (cv_v, cv_h), (sp_v, sp_h), (mix_v, mix_h))
    for i, ref in ((3, p3), (1, p1), (2, p2), (0, p0)):
        ref[...] = mm(mix_v[i], wo[...]).astype(BF)
    wait(out)


def mixer_mid(
    me_ref, br01, br23, cv_h, sp_h, wrg_h, masks_h, brg, c8,
    a1_h, gl_h, later_h, f1_h, f2_h, f3_h, f4_h,
    br, cv, sp, wrg, masks, a1, gl, later, f1, f2, f3, f4, aext, sem_in, sem_out,
):
    n, rows, width = br.shape
    wait(begin(sem_in, 0, (br01, br.at[0:2]), (br23, br.at[2:4]), (cv_h, cv), (wrg_h, wrg), (masks_h, masks), (sp_h, sp)))
    aext[rows:rows + 8] = jnp.zeros((8, width), F32)

    def block(step, _):
        t = n - 1 - step
        r = jnp.bitwise_xor(t, me_ref[0])
        gelu, slope = gelu_both(br[r])
        cvb = cv[r]
        cvf = cvb.astype(F32)
        c8v = c8[...]
        pre = mm(cvb, wrg[...]) + brg[...]
        rg, ig, forget, om, scale, inv = gate_values(cvf, pre, c8v, width)
        m = masks[t]
        before = sp[r]
        igc = ig * cvf
        gl[r] = gelu.astype(BF)
        a1[r] = ((forget * before + scale * igc) * slope).astype(BF)
        aext[0:rows] = forget * m[:, 0:1]
        later[r] = aext[1:1 + rows]
        aext[rows:rows + 8] = aext[0:8]
        q = jnp.where(om > 0.001, -forget * inv, 0.0)
        base = (before + q * igc) * forget * rg
        f1[r] = base.astype(BF)
        f2[r] = (base * (1.0 - rg) * c8v).astype(BF)
        f3[r] = (scale * igc * (1.0 - ig)).astype(BF)
        f4[r] = (scale * ig).astype(BF)
        return 0

    lax.fori_loop(0, n, block, 0)
    wait(begin(sem_out, 0, (a1, a1_h), (gl, gl_h), (later, later_h), (f1, f1_h), (f2, f2_h), (f3, f3_h), (f4, f4_h)))


def flat(ref):
    return ref[...].reshape(ref.shape[0] * ref.shape[1], ref.shape[2])


def mixer_out(
    y_ref, b0, b1, b2, b3, wo_h, a1_h, gl_h, normed01, normed23, mix_h,
    gs_h, gbr_h, keep_o, send_o,
    gb, wo, a1, gl, normed, mix, gs, gbr, pair, sem_in, sem_out,
):
    n = gb.shape[0]
    first = begin(sem_in, 0, (wo_h, wo), (b0, gb.at[0]), (b1, gb.at[1]), (b2, gb.at[2]), (b3, gb.at[3]))
    then = begin(sem_in, 5, (a1_h, a1), (gl_h, gl))
    last = begin(sem_in, 7, (normed01, normed.at[0:2]), (normed23, normed.at[2:4]), (mix_h, mix))
    wait(first)
    for i in range(n):
        gmix = mm_nt(gb[i], wo[...])
        if i == 0:
            wait(then)
        gbr[i] = (gmix * a1[i].astype(F32)).astype(BF)
        gs[i] = gmix * gl[i].astype(F32)
    out = begin(sem_out, 0, (gs, gs_h), (gbr, gbr_h))
    wait(last)
    pair[0] = mm_tn(flat(normed), flat(gbr)).astype(BF)
    pair[1] = mm_tn(flat(gb), flat(mix)).astype(BF)
    for part in (0, 1):
        @pl.when(y_ref[0] == part)
        def _():
            wait(begin(sem_out, 2, (pair.at[part], keep_o), (pair.at[1 - part], send_o)))
    wait(out)


def mixer_bwd(
    me_ref, y_ref, gs_h, later_h, f1_h, f2_h, f3_h, f4_h, ri_h, cv_h, wrg_h, masks_h, gbr_h, normed01, normed23,
    wb_h, wi_h, cw, gain2,
    n0, n2, n31, keep_o, send_o,
    gs, later, f1, f2, f3, f4, ri_v, cv_v, wrg, masks, gbr, normed, wb, wi,
    pair_s, gri_v, p_v, last_v, sm_v, zext, sem_block, sem_in, sem_out,
):
    n, rows, width = gs.shape
    d = normed.shape[2]
    early = begin(sem_in, 0, (wrg_h, wrg), (masks_h, masks))
    blocks = ((gs_h, gs), (later_h, later), (f1_h, f1), (f2_h, f2), (f3_h, f3), (f4_h, f4), (ri_h, ri_v), (cv_h, cv_v))

    def pulls(step):
        r = jnp.bitwise_xor(n - 1 - step, me_ref[0])
        return [pltpu.make_async_copy(src.at[r], dst.at[r], sem_block.at[k, step])
                for k, (src, dst) in enumerate(blocks)]

    for step in range(n):
        for c in pulls(step):
            c.start()
    late = begin(sem_in, 2, (gbr_h, gbr), (normed01, normed.at[0:2]), (normed23, normed.at[2:4]), (wb_h, wb), (wi_h, wi))
    zext[:, rows:rows + 8] = jnp.zeros((3, 8, width), F32)
    sm_v[...] = jnp.zeros(sm_v.shape, F32)
    wait(early)

    def block(step, after):
        wait(pulls(step))
        t = n - 1 - step
        r = jnp.bitwise_xor(t, me_ref[0])
        m = masks[t]
        adj, head = scan_groups(later[r], gs[r], after, True)
        grp = (adj * f2[r].astype(F32)).astype(BF)
        ggp = (adj * f3[r].astype(F32)).astype(BF)
        pair = jnp.concatenate([grp, ggp], axis=1)
        pair_s[r] = pair
        gconv = adj * f4[r].astype(F32) + mm_nt(pair, wrg[...])
        ri = ri_v[r].astype(F32)
        gri = cw[0:1] * gconv
        sums = [jnp.sum(ri * gconv, axis=0, keepdims=True)]
        for k in (1, 2, 3):
            z = gconv * m[:, k - 1:k]
            zext[k - 1, 0:rows] = z
            moved = zext[k - 1, k:k + rows]
            zext[k - 1, rows:rows + 8] = z[0:8]
            gri = gri + cw[k:k + 1] * moved
            sums.append(jnp.sum(ri * moved, axis=0, keepdims=True))
        sums.append(jnp.sum(gconv, axis=0, keepdims=True))
        sums.append(jnp.sum(grp.astype(F32), axis=0, keepdims=True))
        sums.append(jnp.sum(ggp.astype(F32), axis=0, keepdims=True))
        sums.append(jnp.sum(adj * f1[r].astype(F32), axis=0, keepdims=True))
        sm_v[...] += jnp.concatenate(sums, axis=0)
        gri_v[r] = gri.astype(BF)
        return head

    lax.fori_loop(0, n, block, jnp.zeros((1, width), F32))
    wait(late)
    out = []
    gain1 = jnp.zeros((1, d), F32)
    for k, (i, ref) in enumerate(((3, n31.at[0]), (1, n31.at[1]), (2, n2), (0, n0))):
        part = mm_nt(gbr[i], wb[...]) + mm_nt(gri_v[i], wi[...])
        p_v[i] = part.astype(BF)
        out += begin(sem_out, k, (p_v.at[i], ref))
        gain1 = gain1 + jnp.sum(part * normed[i].astype(F32), axis=0, keepdims=True)

    def as_rows(v):
        v = jnp.concatenate([v, jnp.zeros((1, 3 * width - d), F32)], axis=1)
        return [v[:, i * width:(i + 1) * width] for i in range(3)]

    last_v[0:d] = mm_tn(flat(normed), flat(gri_v)).astype(BF)
    dw = mm_tn(flat(cv_v), flat(pair_s))
    hd = width // 2
    left = lax.broadcasted_iota(jnp.int32, (hd, width), 1) < hd
    for k in (0, 1):
        mine = dw[:, k * width:(k + 1) * width]
        last_v[d + k * hd:d + (k + 1) * hd] = jnp.where(left, mine[:hd], mine[hd:]).astype(BF)
    rest = last_v.shape[0] - d - 2 * hd
    few = [sm_v[...]] + as_rows(gain1) + as_rows(gain2[...]) + [jnp.zeros((rest - 14, width), F32)]
    last_v[d + 2 * hd:] = jnp.concatenate(few, axis=0).astype(BF)
    cut = last_v.shape[0] // 2
    halves = last_v.at[0:cut], last_v.at[cut:2 * cut]
    for part in (0, 1):
        @pl.when(y_ref[0] == part)
        def _():
            wait(begin(sem_out, 4, (halves[part], keep_o), (halves[1 - part], send_o)))
    wait(out)


def ends_branch(y_ref, cur, got, branch_o, out_o):
    for part in (0, 1):
        @pl.when(y_ref[0] == part)
        def _():
            pair = (cur, got) if part == 0 else (got, cur)
            branch_o[...] = pair[0][...].astype(F32)
            out_o[...] = pair[1][...].astype(F32).T


def ends_input(y_ref, cur, got, input_o, recur_o, gate_o, few_o, gains_o, whole):
    d, hd = input_o.shape[0], recur_o.shape[1]
    cut = whole.shape[0] // 2
    for part in (0, 1):
        @pl.when(y_ref[0] == part)
        def _():
            whole[part * cut:(part + 1) * cut] = cur[...]
            whole[(1 - part) * cut:(2 - part) * cut] = got[...]
    input_o[...] = whole[0:d].astype(F32)
    for k, ref in enumerate((recur_o, gate_o)):
        both_heads = whole[d + k * hd:d + (k + 1) * hd].astype(F32)
        for i in range(recur_o.shape[0]):
            ref[i] = both_heads[:, i * hd:(i + 1) * hd]
    few = whole[d + 2 * hd:d + 2 * hd + 16].astype(F32)
    few_o[...] = few[0:8]
    for k in (0, 1):
        at = 8 + 3 * k
        gains_o[k:k + 1] = jnp.concatenate([few[at + i:at + i + 1] for i in range(3)], axis=1)[:, :gains_o.shape[1]]


def mlp_blocks(xb, cot, wg, wu, wd, hid, gg, gu, p_v, ready, base):
    for i in range(xb.shape[0]):
        wait(ready[i])
        x = xb[i]
        ga = mm(x, wg[...])
        if i == 0:
            wait(ready[-1][:1])
        ua = mm(x, wu[...])
        if i == 0:
            wait(ready[-1][1:])
        gh = mm_nt(cot[base + i], wd[...])
        gl, slope = gelu_both(ga)
        hid[base + i] = (gl * ua).astype(BF)
        gg[i] = (gh * ua * slope).astype(BF)
        gu[i] = (gh * gl).astype(BF)
    for i in reversed(range(xb.shape[0])):
        p_v[i] = (mm_nt(gg[i], wg[...]) + mm_nt(gu[i], wu[...])).astype(BF)


def mlp_pre(
    b0, b1, c0, c1, wg_h, wu_h, wd_h, hid_h, gg_h, gu_h, n0, n1,
    xb, cot, wg, wu, wd, hid, gg, gu, p_v, sem_in, sem_out,
):
    first = begin(sem_in, 0, (b0, xb.at[0]), (wg_h, wg))
    then = begin(sem_in, 2, (wu_h, wu), (c0, cot.at[0]), (wd_h, wd))
    second = begin(sem_in, 5, (b1, xb.at[1]), (c1, cot.at[1]))
    mlp_blocks(xb, cot, wg, wu, wd, hid, gg, gu, p_v, (first, second, then), 0)
    wait(begin(sem_out, 0, (hid, hid_h), (gg, gg_h), (gu, gu_h), (p_v.at[1], n1), (p_v.at[0], n0)))


def mlp_main(
    y_ref, b2, b3, c0, c1, c2, c3, hid01, n1, wg_h, wu_h, wd_h, hid_h, gg_h, gu_h, n2, n31, dk_o, ds_o,
    xb, cot, wg, wu, wd, hid, gg, gu, p_v, dd, sem_in, sem_out,
):
    rows, units = hid.shape[1:]
    first = begin(sem_in, 0, (b2, xb.at[0]), (wg_h, wg))
    then = begin(sem_in, 2, (wu_h, wu), (c2, cot.at[2]), (wd_h, wd))
    second = begin(sem_in, 5, (b3, xb.at[1]), (c3, cot.at[3]))
    last = begin(sem_in, 7, (c0, cot.at[0]), (c1, cot.at[1]), (hid01, hid.at[0:2]), (n1, n31.at[1]))
    mlp_blocks(xb, cot, wg, wu, wd, hid, gg, gu, p_v, (first, second, then), 2)
    n31[0] = p_v[1]
    n2[...] = p_v[0]
    out = begin(sem_out, 0, (hid.at[2:4], hid_h), (gg, gg_h), (gu, gu_h))
    wait(last)
    call_ = cot[...].reshape(4 * rows, cot.shape[2])
    hall = hid[...].reshape(4 * rows, units)
    half = units // 2
    for part in (0, 1):
        dd[part] = mm_tn(hall[:, part * half:(part + 1) * half], call_).astype(BF)
    for part in (0, 1):
        @pl.when(y_ref[0] == part)
        def _():
            wait(begin(sem_out, 5, (dd.at[part], dk_o), (dd.at[1 - part], ds_o)))
    wait(out)


def mlp_post(
    y_ref, z_ref, b0, b1, b2, b3, gg01, gg23, gu01, gu23, hid01, hid23, wd_h, gk_o, gs_o, uk_o, us_o, m0, m2, m31,
    xb, gg, gu, hid, wd, dg, du, p_v, sem_in, sem_out,
):
    n, rows, units = hid.shape
    first = begin(sem_in, 0, (b0, xb.at[0]), (b1, xb.at[1]), (b2, xb.at[2]), (b3, xb.at[3]),
                  (gg01, gg.at[0:2]), (gg23, gg.at[2:4]))
    second = begin(sem_in, 6, (gu01, gu.at[0:2]), (gu23, gu.at[2:4]))
    third = begin(sem_in, 8, (hid01, hid.at[0:2]), (hid23, hid.at[2:4]), (wd_h, wd))

    def flat(ref):
        return ref[...].reshape(n * rows, ref.shape[2])

    wait(first)
    xall = flat(xb)
    half = dg.shape[1]
    for part in (0, 1):
        dg[part] = mm_tn(xall[:, part * half:(part + 1) * half], flat(gg)).astype(BF)
    wait(second)
    for part in (0, 1):
        du[part] = mm_tn(xall[:, part * half:(part + 1) * half], flat(gu)).astype(BF)
    for part in (0, 1):
        @pl.when(y_ref[0] == part)
        def _():
            begin(sem_out, 4, (dg.at[part], gk_o), (dg.at[1 - part], gs_o))

        @pl.when(z_ref[0] == part)
        def _():
            begin(sem_out, 6, (du.at[part], uk_o), (du.at[1 - part], us_o))
    out = []
    wait(third)
    for k, (i, ref) in enumerate(((3, m31.at[0]), (1, m31.at[1]), (2, m2), (0, m0))):
        p_v[i] = mm(hid[i], wd[...]).astype(BF)
        out += begin(sem_out, k, (p_v.at[i], ref))
    wait(out)
    wait([pltpu.make_async_copy(v.at[0], o, sem_out.at[4 + k])
          for k, (v, o) in enumerate(((dg, gk_o), (dg, gs_o), (du, uk_o), (du, us_o)))])


def add_two(a, b, got_a, got_b, send_o, own_o):
    send_o[...] = plus(a[...], got_a[...]).astype(BF)
    own_o[...] = plus(b[...], got_b[...]).astype(BF)


def add_both(i2, i0, o2, o0, got_i, got_o, send_o, own_i, own_o):
    send_o[0] = plus(i2[...], got_i[0]).astype(BF)
    own_i[...] = plus(i0[...], got_i[1]).astype(BF)
    send_o[1] = plus(o2[...], got_o[0]).astype(BF)
    own_o[...] = plus(o0[...], got_o[1]).astype(BF)


def add_pair(a, b, got, send_o, own_o):
    send_o[...] = plus(a[...], got[0]).astype(BF)
    own_o[...] = plus(b[...], got[1]).astype(BF)


def mid_fwd(x, own, far, gain, mid_o, n_o):
    mid = x[...].astype(F32) + plus(own[...], far[...])
    inv = lax.rsqrt(jnp.mean(mid * mid, axis=-1, keepdims=True) + EPSILON)
    mid_o[...] = mid
    n_o[...] = (mid * inv * gain[...]).astype(BF)


def norm_back(total, values, gain):
    inv = lax.rsqrt(jnp.mean(values * values, axis=-1, keepdims=True) + EPSILON)
    v = total * gain
    scaled = values * inv
    mean = jnp.mean(v * scaled, axis=-1, keepdims=True)
    grad = inv * (v - scaled * mean)
    return grad, jnp.sum(total * scaled, axis=0, keepdims=True)


def mid_bwd(mid, own, far, gain, cot, gm_o, gb_o, gg_o):
    grad, gsum = norm_back(plus(own[...], far[...]), mid[...], gain[...])
    gm = cot[...].astype(F32) + grad
    gm_o[...] = gm
    gb_o[...] = gm.astype(BF)
    gg_o[...] = gsum


def last_bwd(x, mid, own_i, own_o, far, gain, gm, o, out_o):
    grad, _ = norm_back(plus(own_i[...], far[0]), x[...].astype(F32), gain[...])
    o[...] = gm[...] + grad
    out_o[...] = (mid[...] + plus(own_o[...], far[1])).astype(BF)


def cost(us):
    return pl.CostEstimate(flops=1 + int(us * 1.15e9), bytes_accessed=0, transcendentals=0)


HBM, VMEM, SMEM = pltpu.HBM, pltpu.VMEM, pltpu.SMEM


def call(kernel, outs, *args, name, us, mib, places, out, scratch=()):
    spec = {"h": HBM, "v": VMEM, "s": SMEM, "a": pl.ANY}
    args = [
        pltpu.with_memory_space_constraint(a, VMEM if p == "v" else HBM) if p in "hv" else a
        for p, a in zip(places, args, strict=True)
    ]
    return pl.pallas_call(
        kernel,
        out_shape=[(VMEM if p == "v" else HBM)(*o) for p, o in zip(out, outs, strict=True)],
        in_specs=[pl.BlockSpec(memory_space=spec[p]) if p in spec else pl.BlockSpec() for p in places],
        out_specs=[pl.BlockSpec(memory_space=spec[p]) if p in spec else pl.BlockSpec() for p in out],
        scratch_shapes=list(scratch),
        compiler_params=pltpu.CompilerParams(vmem_limit_bytes=mib * MIB),
        cost_estimate=cost(us),
        name=name,
    )(*args)


CORE = [(i, i ^ 1) for i in range(4)]
FAR = [(i, i ^ 2) for i in range(4)]


def to_core(v):
    return lax.ppermute(v, "ch", CORE)


def to_far(v):
    return lax.ppermute(v, "ch", FAR)


class Order:
    def __init__(self):
        self.last = None

    def run(self, work, *values):
        if self.last is not None:
            values = lax.optimization_barrier((*values, *self.last))[:len(values)]
        got = work(*values)
        self.last = tuple(got) if isinstance(got, (tuple, list)) else (got,)
        return got

    def gate(self, value):
        return lax.optimization_barrier((value, *self.last))[0]

    def take(self, value):
        return self.run(lambda v: (v,), value)[0]


def dyn(g, index, size):
    return lax.dynamic_slice_in_dim(g, index * size, size, 0)


def plus(a, b):
    return a.astype(F32) + b.astype(F32)


def add_low(a, b):
    return plus(a, b).astype(BF)


def put(total, piece, index):
    return lax.dynamic_update_slice_in_dim(total, piece.astype(total.dtype), index * piece.shape[0], 0)


Y = [(i, i ^ 1) for i in range(8)]
Z1 = [(i, i ^ 2) for i in range(8)]
Z2 = [(i, i ^ 4) for i in range(8)]
def both(low, a, b):
    return jnp.concatenate([jnp.where(low, a, b), jnp.where(low, b, a)], 0)


def sum_rows_plain(keep, send, ends):
    yield "sent"
    return ends(*(lax.psum(v.astype(F32), "rows").astype(BF) for v in (keep, send)))


INWARD = [(0, 2), (1, 3), (6, 4), (7, 5)]
MIDDLE = [(2, 4), (3, 5), (4, 2), (5, 3)]
OUTWARD = [(2, 0), (3, 1), (4, 6), (5, 7)]


def send_on(value, pairs, order):
    if (yield "ready"):
        value = order.gate(value)
    got = lax.ppermute(value, "rows", pairs)
    yield "sent"
    return order.take(got)


def sum_rows_halves(keep, send, order, way, ends):
    me = lax.axis_index("rows")
    y, z = (Y, me % 2), (Z1, (me // 2) % 2)
    stages = ((y, z) if way == "y" else (z, y)) + ((Z2, me // 4),)
    got = yield from send_on(send, stages[0][0], order)
    yield "came"
    for pairs, bit in stages[1:]:
        half = keep.shape[0] // 2

        def split(a, b, bit=bit, half=half):
            return (add_low(dyn(a, 1 - bit, half), dyn(b, 1 - bit, half)), add_low(dyn(a, bit, half), dyn(b, bit, half)))

        send, keep = order.run(split, keep, got)
        got = yield from send_on(send, pairs, order)
        yield "came"
    cur = order.run(add_low, keep, got)
    for pairs, bit in stages[::-1]:
        got = yield from send_on(cur, pairs, order)
        yield "came"
        if pairs is stages[0][0]:
            return order.run(ends, cur, got)
        cur = order.run(lambda a, b, bit=bit: both(bit == 0, a, b), cur, got)


def sum_rows_line(keep, send, order, ends):
    me = lax.axis_index("rows")
    y, z = me % 2, me // 2
    inner = (z == 1) | (z == 2)
    got = yield from send_on(send, Y, order)
    yield "came"
    cur = order.run(add_low, keep, got)
    for pairs in (INWARD, MIDDLE):
        got = yield from send_on(cur, pairs, order)
        yield "came"
        cur = order.run(add_low, cur, got)
    got = yield from send_on(cur, OUTWARD, order)
    yield "came"
    cur = order.run(lambda a, b: jnp.where(inner, a, b), cur, got)
    got = yield from send_on(cur, Y, order)
    yield "came"
    return order.run(ends, cur, got)


class Chain:
    def __init__(self, steps):
        self.steps, self.value, self.state, self.held = steps, None, None, False
        self.go()

    def step(self, first=False):
        try:
            self.state = self.steps.send(None if self.state is None else self.held)
            self.held = False
        except StopIteration as end:
            self.state, self.value = "done", end.value

    def to(self, state):
        if self.state == "done":
            return
        self.step()
        while self.state not in (state, "done"):
            self.step()
        self.held = state == "ready"

    def come(self):
        if self.state == "sent":
            self.to("came")

    def go(self):
        self.to("sent")

    def finish(self):
        while self.state != "done":
            self.go()
        return self.value


def block_diag(w):
    h, d, e = w.shape
    rows = [
        jnp.concatenate([w[i] if i == j else jnp.zeros((d, e), w.dtype) for j in range(h)], axis=1)
        for i in range(h)
    ]
    return jnp.concatenate(rows, axis=0)


def body(n_rows, inputs, segment_ids, mixer_gain, branch_weight, input_weight, conv_weight, conv_bias,
         recur_weight, recur_bias, gate_weight, gate_bias, decay_param, out_weight, mlp_gain, mlp_gate,
         mlp_up, mlp_down, cotangent):
    x = inputs[0]
    cot = cotangent[0]
    rows, d = x.shape
    width = branch_weight.shape[1]
    units = mlp_gate.shape[1]
    heads, hd, _ = recur_weight.shape
    seq = segment_ids.shape[1]
    n = seq // rows
    me = lax.axis_index("ch").astype(jnp.int32)[None]
    gain1 = mixer_gain[None]
    gain2 = mlp_gain[None]
    order = Order()
    row = lax.axis_index("rows").astype(jnp.int32)[None]
    y_half = row % 2 if n_rows == 8 else jnp.zeros((1,), jnp.int32)
    z_half = (row // 2) % 2 if n_rows == 8 else jnp.zeros((1,), jnp.int32)

    split = {k: z_half if v == "z" else y_half for k, v in KINDS.items()}

    def total(keep, send, way, ends):
        if n_rows != 8:
            return Chain(sum_rows_plain(keep, send, ends))
        if way == "line":
            return Chain(sum_rows_line(keep, send, order, ends))
        return Chain(sum_rows_halves(keep, send, order, way, ends))

    x_far, x_near = to_far(x), to_core(x)

    def tables(ids, rw, gw, rb, gb_, dp):
        marks = [
            (jnp.pad(ids, (k, 0), constant_values=-1)[:seq] == ids).astype(F32) for k in (1, 2, 3)
        ]
        masks = jnp.pad(jnp.stack(marks, axis=1), ((0, 0), (0, 125))).reshape(n, rows, 128)
        wrg = jnp.concatenate([block_diag(rw), block_diag(gw)], axis=1)
        return masks, wrg, jnp.concatenate([rb, gb_])[None], (-8.0 * jax.nn.softplus(dp))[None]

    masks, wrg, brg, c8 = order.run(
        tables, segment_ids[0], recur_weight, gate_weight, recur_bias, gate_bias, decay_param
    )
    cb = conv_bias[None]
    blk, narrow, wide = (rows, d), (n, rows, width), (n, rows, units)
    four, two = (n, rows, d), (2, rows, d)
    narrow2, wide2 = (2, rows, width), (2, rows, units)
    dma = pltpu.SemaphoreType.DMA
    normed01, br01, ri01 = order.run(
        functools.partial(
            call, mixer_pre, [(two, BF), (narrow2, F32), (narrow2, F32)], name="mixer_pre", us=0, mib=20,
            places="aahhi", out="hhh", scratch=[
                VMEM(two, BF), VMEM((d, width), BF), VMEM((d, width), BF), VMEM(two, BF), VMEM(narrow2, F32),
                VMEM(narrow2, F32), dma((4,)), dma((3,)),
            ]),
        x, x_near, branch_weight, input_weight, gain1)
    x_far = order.take(x_far)
    x_diag = to_core(x_far)
    cot_far = to_far(cot)
    x_diag = order.take(x_diag)
    fwd = order.run(
        functools.partial(
            call, mixer_fwd,
            [(two, BF), (narrow2, F32), (narrow, BF), (narrow, BF), (narrow, F32), (narrow, BF)] + [(blk, BF)] * 4,
            name="mixer_fwd", us=0, mib=30, places="saahhhhhhhiiiii", out="h" * 6 + "vvvv", scratch=[
                VMEM(two, BF), VMEM((d, width), BF), VMEM((d, width), BF), VMEM((width, 2 * width), BF),
                VMEM((n, rows, 128), F32), VMEM((width, d), BF), VMEM(two, BF), VMEM(narrow, F32),
                VMEM(narrow, F32), VMEM(narrow, BF), VMEM(narrow, BF), VMEM(narrow, F32), VMEM(narrow, BF),
                VMEM((rows + 8, width), F32), VMEM((rows + 8, width), F32), dma((9,)), dma((6,)),
            ]),
        me, x_far, x_diag, branch_weight, input_weight, br01, ri01, wrg, masks, out_weight, gain1, conv_weight, cb,
        brg, c8)
    normed23, br23, ri, cv, sp, mix = fwd[:6]
    cot_far = order.take(cot_far)

    def near_half(own, far, pair):
        got = to_core(pair)
        return order.run(
            functools.partial(call, add_pair, [(blk, BF)] * 2, name="add_pair", us=0, mib=6, places="iii", out="vv"),
            far, own, got)

    send, own = order.run(
        functools.partial(call, add_two, [(blk, BF)] * 2, name="add_two", us=0, mib=6, places="vvii", out="vv"),
        fwd[7], fwd[6], to_core(fwd[8]), to_core(fwd[9]))
    far = to_far(send)
    cot_near, cot_diag = to_core(cot), to_core(cot_far)
    cot_near = order.take(cot_near)
    cot_diag = order.take(cot_diag)
    a1, gl, later, *fs = order.run(
        functools.partial(
            call, mixer_mid, [(narrow, BF), (narrow, BF), (narrow, F32)] + [(narrow, BF)] * 4, name="mixer_mid", us=0,
            mib=30, places="s" + "h" * 6 + "ii", out="h" * 7, scratch=[
                VMEM(narrow, F32), VMEM(narrow, BF), VMEM(narrow, F32), VMEM((width, 2 * width), BF),
                VMEM((n, rows, 128), F32), VMEM(narrow, BF), VMEM(narrow, BF), VMEM(narrow, F32)]
            + [VMEM(narrow, BF)] * 4 + [VMEM((rows + 8, width), F32), dma((6,)), dma((7,))]),
        me, br01, br23, cv, sp, wrg, masks, brg, c8)
    mid, normed2 = order.run(functools.partial(
        call, mid_fwd, [(blk, F32), (blk, BF)], name="mid_fwd", us=0, mib=8, places="ivvi", out="iv"),
        x, own, far, gain2)
    n_far, n_near = to_far(normed2), to_core(normed2)
    n_near = order.take(n_near)
    mlp_scratch = [
        VMEM((d, units), BF), VMEM((d, units), BF), VMEM((units, d), BF)]
    hid01, gg01, gu01, g0, g1 = order.run(
        functools.partial(
            call, mlp_pre, [(wide2, BF)] * 3 + [(blk, BF)] * 2, name="mlp_pre", us=0, mib=30, places="aahhhhh",
            out="h" * 5, scratch=[VMEM(two, BF), VMEM(two, BF)] + mlp_scratch + [VMEM(wide2, BF)] * 3 + [
                VMEM(two, BF), dma((7,)), dma((5,))]),
        normed2, n_near, cot, cot_near, mlp_gate, mlp_up, mlp_down)
    n_far = order.take(n_far)
    n_diag = order.take(to_core(n_far))
    hid23, gg23, gu23, g2, g31, down_keep, down_send = order.run(
        functools.partial(
            call, mlp_main, [(wide2, BF)] * 3 + [(blk, BF), (two, BF)] + [((units // 2, d), BF)] * 2, name="mlp_main",
            us=0, mib=26, places="saahhhhhhhhh", out="hhhvvhh",
            scratch=[VMEM(two, BF), VMEM(four, BF)] + mlp_scratch + [VMEM(wide, BF), VMEM(wide2, BF), VMEM(wide2, BF)] + [
                VMEM(two, BF), VMEM((2, units // 2, d), BF), dma((11,)), dma((7,))]),
        split["d"], n_far, n_diag, cot, cot_near, cot_far, cot_diag, hid01, g1, mlp_gate, mlp_up, mlp_down)
    y_low, z_low = y_half[0] == 0, z_half[0] == 0

    def wide_ends(low, a, b):
        return both(low, a, b).astype(F32)

    def ends_of(kind):
        return functools.partial(wide_ends, y_low if split[kind] is y_half else z_low)

    s_down = total(down_keep, down_send, KINDS["d"], ends_of("d"))
    g_send, g_own = near_half(g0, g2, g31)
    from_far = to_far(g_send)
    post = order.run(
        functools.partial(
            call, mlp_post, [((d // 2, units), BF)] * 4 + [(blk, BF), (blk, BF), (two, BF)], name="mlp_post", us=0,
            mib=26, places="ssaaaahhhhhhh", out="h" * 7, scratch=[
                VMEM(four, BF), VMEM(wide, BF), VMEM(wide, BF), VMEM(wide, BF), VMEM((units, d), BF),
                VMEM((2, d // 2, units), BF), VMEM((2, d // 2, units), BF), VMEM(four, BF), dma((11,)), dma((8,)),
            ]),
        split["g"], split["u"], normed2, n_near, n_far, n_diag, gg01, gg23, gu01, gu23, hid01, hid23, mlp_down)
    s_gate = total(post[0], post[1], KINDS["g"], ends_of("g"))
    s_up = total(post[2], post[3], KINDS["u"], ends_of("u"))
    chains = {"d": s_down, "g": s_gate, "u": s_up}
    live = {}

    def at_rf():
        gm, gb, gsum2 = order.run(functools.partial(
            call, mid_bwd, [(blk, F32), (blk, BF), ((1, d), F32)], name="mid_bwd", us=10, mib=8, places="ivvii", out="ivi"),
            mid, g_own, from_far, gain2, cot)
        g_near, g_far = to_core(gb), to_far(gb)
        live.update(gm=gm, gb=gb, gsum2=gsum2, g_near=g_near, g_far=g_far)

    def at_gf():
        gb = live["gb"]
        g_far = order.take(live["g_far"])
        g_diag = to_core(g_far)
        g_near = order.take(live["g_near"])
        g_diag = order.take(g_diag)
        gs, gbr, p_keep, p_send = order.run(
            functools.partial(
                call, mixer_out, [(narrow, F32), (narrow, BF)] + [((d, width), BF)] * 2, name="mixer_out", us=0, mib=30,
                places="shaaa" + "h" * 6, out="h" * 4, scratch=[
                    VMEM(four, BF), VMEM((width, d), BF), VMEM(narrow, BF), VMEM(narrow, BF), VMEM(four, BF),
                    VMEM(narrow, BF), VMEM(narrow, F32), VMEM(narrow, BF), VMEM((2, d, width), BF), dma((10,)), dma((4,))]),
            split["p"], gb, g_near, g_far, g_diag, out_weight, a1, gl, normed01, normed23, mix)
        chains["p"] = total(p_keep, p_send, KINDS["p"], functools.partial(
            call, ends_branch, [((d, width), F32), ((width, d), F32)], split["p"], name="ends_branch", us=0, mib=16,
            places="sii", out="ii"))
        live.update(gs=gs, gbr=gbr)

    def at_m():
        last_rows = d + 2 * hd + 64
        bwd = order.run(
            functools.partial(
                call, mixer_bwd, [(blk, BF), (blk, BF), (two, BF)] + [((last_rows // 2, width), BF)] * 2,
                name="mixer_bwd", us=0, mib=36, places="ss" + "h" * 15 + "ii", out="h" * 5, scratch=[
                    VMEM(narrow, F32), VMEM(narrow, F32)] + [VMEM(narrow, BF)] * 6 + [
                    VMEM((width, 2 * width), BF), VMEM((n, rows, 128), F32), VMEM(narrow, BF), VMEM(four, BF),
                    VMEM((d, width), BF), VMEM((d, width), BF), VMEM((n, rows, 2 * width), BF), VMEM(narrow, BF),
                    VMEM(four, BF), VMEM((last_rows, width), BF), VMEM((8, width), F32), VMEM((3, rows + 8, width), F32),
                    dma((8, n)), dma((8,)), dma((6,)),
                ]),
            me, split["q"], live["gs"], later, *fs, ri, cv, wrg, masks, live["gbr"], normed01, normed23, branch_weight, input_weight,
            conv_weight, live["gsum2"])
        chains["q"] = total(bwd[3], bwd[4], KINDS["q"], functools.partial(
            call, ends_input, [((d, width), F32), ((heads, hd, hd), F32), ((heads, hd, hd), F32), ((8, width), F32),
             ((2, d), F32)], split["q"], name="ends_input", us=0, mib=16, places="sii", out="iiiii", scratch=[VMEM((last_rows, width), BF)]))

        live.update(bwd=bwd)

    def sum_ch(n0, n2, pair):
        got_i, got_o = to_core(order.gate(pair)), to_core(order.gate(post[6]))
        yield "sent"
        got_i, got_o = order.run(lambda a, b: (a, b), got_i, got_o)
        yield "came"
        send, own_i, own_o = order.run(
            functools.partial(
                call, add_both, [(two, BF), (blk, BF), (blk, BF)], name="add_both", us=0, mib=14, places="iiiiii", out="uuu"),
            n2, n0, post[5], post[4], got_i, got_o)
        far = to_far(send)
        yield "sent"
        far = order.take(far)
        yield "came"
        return order.run(
            functools.partial(
                call, last_bwd, [(blk, F32), (blk, BF)], name="last_bwd", us=0, mib=14, places="iiiiiii", out="ii"),
            x, mid, own_i, own_o, far, gain1, live["gm"])

    events = {"rf": at_rf, "gf": at_gf, "m": at_m}

    def turn(what):
        if what in events:
            events[what]()
            return
        if what == "c":
            if "bwd" in live and "i" not in chains and chains["d"].state == "done":
                chains["i"] = Chain(sum_ch(*live["bwd"][:3]))
            return
        chains[what].go()

    for what in PLAN:
        turn(what)
    while "i" not in chains or any(c.state != "done" for c in chains.values()):
        for what in PLAN_AFTER:
            if what in chains or what == "c":
                turn(what)
    input_grad, output = chains["i"].value
    t_branch, t_out = chains["p"].value
    t_input, t_recur, t_gate_w, ts, gains = chains["q"].value
    t_down, t_gate, t_up = (s.value for s in (s_down, s_gate, s_up))
    others = [lax.ppermute(gains, "ch", [(i, i ^ k) for i in range(4)]) for k in (3, 2, 1)]
    gain1_grad, gain2_grad = order.run(
        lambda own, c, b, a: tuple((own[k] + a[k]) + (b[k] + c[k]) for k in (0, 1)), gains, *others)
    gain1_grad = gain1_grad / mixer_gain
    decay_grad = ts[7] * -8.0 * jax.nn.sigmoid(decay_param)
    return (
        output[None],
        input_grad[None],
        gain1_grad,
        t_branch,
        t_input,
        ts[0:4],
        ts[4],
        t_recur,
        ts[5],
        t_gate_w,
        ts[6],
        decay_grad,
        t_out,
        gain2_grad,
        t_gate,
        t_up,
        t_down,
    )


def solution(mesh):
    rows, ch = P("rows", "ch", None), P("ch")
    cols, lead = P(None, "ch"), P("ch", None)
    heads = P("ch", None, None)
    return jax.shard_map(
        functools.partial(body, mesh.shape["rows"]),
        mesh=mesh,
        in_specs=(rows, P("rows", None), P(), cols, cols, cols, ch, heads, ch, heads, ch, ch, lead, P(),
                  cols, cols, lead, rows),
        out_specs=(rows, rows, P(), cols, cols, cols, ch, heads, ch, heads, ch, ch, lead, P(), cols, cols, lead),
        check_vma=False,
    )
```

```python
import functools

import jax
import jax.numpy as jnp
from jax import lax
from jax.experimental import pallas as pl
from jax.experimental.pallas import tpu as pltpu
from jax.sharding import PartitionSpec as P

EPSILON = 1e-06
BF = jnp.bfloat16
F32 = jnp.float32
MIB = 1024 * 1024
KINDS = {"d": "line", "g": "line", "u": "z", "p": "line", "q": "line"}
PLAN_AFTER = ("u", "g", "d", "p", "q", "i", "c")
PLAN = ("d", "rf", "u", "g", "gf", "d", "m", "u", "g", "d", "p", "q")
GELU_C = 0.7978845608028654
GELU_A = 0.044715


def mm(a, b):
    return lax.dot_general(a, b, (((1,), (0,)), ((), ())), preferred_element_type=F32)


def mm_nt(a, b):
    return lax.dot_general(a, b, (((1,), (1,)), ((), ())), preferred_element_type=F32)


def mm_tn(a, b):
    return lax.dot_general(a, b, (((0,), (0,)), ((), ())), preferred_element_type=F32)


def sigmoid(v):
    return 0.5 * jnp.tanh(0.5 * v) + 0.5


def gelu_both(v):
    sq = v * v
    th = jnp.tanh(GELU_C * v * (1.0 + GELU_A * sq))
    half = 0.5 * th + 0.5
    slope = half + (0.5 * GELU_C) * v * (1.0 - th * th) * (1.0 + (3.0 * GELU_A) * sq)
    return v * half, slope


def gelu_only(v):
    th = jnp.tanh(GELU_C * v * (1.0 + GELU_A * (v * v)))
    return v * (0.5 * th + 0.5)


def scan_groups(mult, add, start, back):
    rows, cols = mult.shape
    a = mult.reshape(rows // 8, 8, cols)
    d = add.reshape(rows // 8, 8, cols)
    sub = lax.broadcasted_iota(jnp.int32, (1, 8, cols), 1)
    for k in (1, 2, 4):
        ok = sub < 8 - k if back else sub >= k
        turn = 8 - k if back else k
        d = d + a * jnp.where(ok, pltpu.roll(d, turn, 1), 0.0)
        a = a * jnp.where(ok, pltpu.roll(a, turn, 1), 1.0)
    state = start
    got = [None] * (rows // 8)
    order = range(rows // 8)
    for g in reversed(order) if back else order:
        now = d[g] + a[g] * state
        state = now[0:1] if back else now[7:8]
        got[g] = now
    return jnp.concatenate(got, axis=0), state


def gate_values(conv, pre, c8, width):
    rg = sigmoid(pre[:, :width])
    ig = sigmoid(pre[:, width:])
    forget = jnp.exp(c8 * rg)
    om = 1.0 - forget * forget
    top = jnp.maximum(om, 0.001)
    inv = lax.rsqrt(top)
    return rg, ig, forget, om, top * inv, inv


def begin(sem, first, *pairs):
    copies = [pltpu.make_async_copy(src, dst, sem.at[first + k]) for k, (src, dst) in enumerate(pairs)]
    for c in copies:
        c.start()
    return copies


def wait(copies):
    for c in copies:
        c.wait()


def project(x, gain, wb, wi):
    x = x.astype(F32)
    inv = lax.rsqrt(jnp.mean(x * x, axis=-1, keepdims=True) + EPSILON)
    normed = (x * inv * gain).astype(BF)
    return normed, mm(normed, wb), mm(normed, wi)


def mixer_pre(b0, b1, wb_h, wi_h, gain, normed_h, br_h, ri_h, wb, wi, xb, normed_v, br_v, ri_v, sem_in, sem_out):
    first = begin(sem_in, 0, (b0, xb.at[0]), (wb_h, wb), (wi_h, wi))
    second = begin(sem_in, 3, (b1, xb.at[1]))
    for i, ready in enumerate((first, second)):
        wait(ready)
        normed_v[i], br_v[i], ri_v[i] = project(xb[i], gain[...], wb[...], wi[...])
    wait(begin(sem_out, 0, (normed_v, normed_h), (br_v, br_h), (ri_v, ri_h)))


def mixer_fwd(
    me_ref, b2, b3, wb, wi, br01, ri01, wrg_h, masks_h, wo_h, gain, cw, cb, brg, c8,
    normed_h, br_h, ri_h, cv_h, sp_h, mix_h, p0, p2, p3, p1,
    xb, wrg, masks, wo, normed_v, br_v, ri_s, ri_v, cv_v, sp_v, mix_v, ext, sext, sem_in, sem_out,
):
    n, rows, width = br_v.shape
    first = begin(sem_in, 0, (b2, xb.at[0]))
    second = begin(sem_in, 3, (b3, xb.at[1]))
    later = begin(sem_in, 4, (ri01, ri_s.at[0:2]), (wrg_h, wrg), (masks_h, masks), (br01, br_v.at[0:2]), (wo_h, wo))
    for i, ready in enumerate((first, second)):
        wait(ready)
        normed_v[i], br_v[2 + i], ri_s[2 + i] = project(xb[i], gain[...], wb[...], wi[...])
    out = begin(sem_out, 0, (normed_v, normed_h), (br_v.at[2:4], br_h))
    ext[0:8] = jnp.zeros((8, width), F32)
    wait(later)

    def block(t, first):
        r = jnp.bitwise_xor(t, me_ref[0])
        ri = ri_s[r]
        ri_v[r] = ri.astype(BF)
        ext[8:8 + rows] = ri
        m = masks[t]
        conv = cb[...] + cw[0:1] * ri
        for k in (1, 2, 3):
            conv = conv + cw[k:k + 1] * (ext[8 - k:8 - k + rows] * m[:, k - 1:k])
        ext[0:8] = ext[rows:rows + 8]
        cv = conv.astype(BF)
        cv_v[r] = cv
        cvf = cv.astype(F32)
        pre = mm(cv, wrg[...]) + brg[...]
        rg, ig, forget, om, scale, _ = gate_values(cvf, pre, c8[...], width)
        keep = m[:, 0:1]
        states, last = scan_groups(forget * keep, scale * ig * cvf, first, False)
        sext[8:8 + rows] = states
        sext[7:8] = first
        sp_v[r] = sext[7:7 + rows] * keep
        mix_v[r] = (gelu_only(br_v[r]) * states).astype(BF)
        return last

    lax.fori_loop(0, n, block, jnp.zeros((1, width), F32))
    out += begin(sem_out, 2, (ri_v, ri_h), (cv_v, cv_h), (sp_v, sp_h), (mix_v, mix_h))
    for i, ref in ((3, p3), (1, p1), (2, p2), (0, p0)):
        ref[...] = mm(mix_v[i], wo[...]).astype(BF)
    wait(out)


def mixer_mid(
    me_ref, br01, br23, cv_h, sp_h, wrg_h, masks_h, brg, c8,
    a1_h, gl_h, later_h, f1_h, f2_h, f3_h, f4_h,
    br, cv, sp, wrg, masks, a1, gl, later, f1, f2, f3, f4, aext, sem_in, sem_out,
):
    n, rows, width = br.shape
    wait(begin(sem_in, 0, (br01, br.at[0:2]), (br23, br.at[2:4]), (cv_h, cv), (wrg_h, wrg), (masks_h, masks), (sp_h, sp)))
    aext[rows:rows + 8] = jnp.zeros((8, width), F32)

    def block(step, _):
        t = n - 1 - step
        r = jnp.bitwise_xor(t, me_ref[0])
        gelu, slope = gelu_both(br[r])
        cvb = cv[r]
        cvf = cvb.astype(F32)
        c8v = c8[...]
        pre = mm(cvb, wrg[...]) + brg[...]
        rg, ig, forget, om, scale, inv = gate_values(cvf, pre, c8v, width)
        m = masks[t]
        before = sp[r]
        igc = ig * cvf
        gl[r] = gelu.astype(BF)
        a1[r] = ((forget * before + scale * igc) * slope).astype(BF)
        aext[0:rows] = forget * m[:, 0:1]
        later[r] = aext[1:1 + rows]
        aext[rows:rows + 8] = aext[0:8]
        q = jnp.where(om > 0.001, -forget * inv, 0.0)
        base = (before + q * igc) * forget * rg
        f1[r] = base.astype(BF)
        f2[r] = (base * (1.0 - rg) * c8v).astype(BF)
        f3[r] = (scale * igc * (1.0 - ig)).astype(BF)
        f4[r] = (scale * ig).astype(BF)
        return 0

    lax.fori_loop(0, n, block, 0)
    wait(begin(sem_out, 0, (a1, a1_h), (gl, gl_h), (later, later_h), (f1, f1_h), (f2, f2_h), (f3, f3_h), (f4, f4_h)))


def flat(ref):
    return ref[...].reshape(ref.shape[0] * ref.shape[1], ref.shape[2])


def mixer_out(
    y_ref, b0, b1, b2, b3, wo_h, a1_h, gl_h, normed01, normed23, mix_h,
    gs_h, gbr_h, keep_o, send_o,
    gb, wo, a1, gl, normed, mix, gs, gbr, pair, sem_in, sem_out,
):
    n = gb.shape[0]
    first = begin(sem_in, 0, (wo_h, wo), (b0, gb.at[0]), (b1, gb.at[1]), (b2, gb.at[2]), (b3, gb.at[3]))
    then = begin(sem_in, 5, (a1_h, a1), (gl_h, gl))
    last = begin(sem_in, 7, (normed01, normed.at[0:2]), (normed23, normed.at[2:4]), (mix_h, mix))
    wait(first)
    for i in range(n):
        gmix = mm_nt(gb[i], wo[...])
        if i == 0:
            wait(then)
        gbr[i] = (gmix * a1[i].astype(F32)).astype(BF)
        gs[i] = gmix * gl[i].astype(F32)
    out = begin(sem_out, 0, (gs, gs_h), (gbr, gbr_h))
    wait(last)
    pair[0] = mm_tn(flat(normed), flat(gbr)).astype(BF)
    pair[1] = mm_tn(flat(gb), flat(mix)).astype(BF)
    for part in (0, 1):
        @pl.when(y_ref[0] == part)
        def _():
            wait(begin(sem_out, 2, (pair.at[part], keep_o), (pair.at[1 - part], send_o)))
    wait(out)


def mixer_bwd(
    me_ref, y_ref, gs_h, later_h, f1_h, f2_h, f3_h, f4_h, ri_h, cv_h, wrg_h, masks_h, gbr_h, normed01, normed23,
    wb_h, wi_h, cw, gain2,
    n0, n2, n31, keep_o, send_o,
    gs, later, f1, f2, f3, f4, ri_v, cv_v, wrg, masks, gbr, normed, wb, wi,
    pair_s, gri_v, p_v, last_v, sm_v, zext, sem_block, sem_in, sem_out,
):
    n, rows, width = gs.shape
    d = normed.shape[2]
    early = begin(sem_in, 0, (wrg_h, wrg), (masks_h, masks))
    blocks = ((gs_h, gs), (later_h, later), (f1_h, f1), (f2_h, f2), (f3_h, f3), (f4_h, f4), (ri_h, ri_v), (cv_h, cv_v))

    def pulls(step):
        r = jnp.bitwise_xor(n - 1 - step, me_ref[0])
        return [pltpu.make_async_copy(src.at[r], dst.at[r], sem_block.at[k, step])
                for k, (src, dst) in enumerate(blocks)]

    for step in range(n):
        for c in pulls(step):
            c.start()
    late = begin(sem_in, 2, (gbr_h, gbr), (normed01, normed.at[0:2]), (normed23, normed.at[2:4]), (wb_h, wb), (wi_h, wi))
    zext[:, rows:rows + 8] = jnp.zeros((3, 8, width), F32)
    sm_v[...] = jnp.zeros(sm_v.shape, F32)
    wait(early)

    def block(step, after):
        wait(pulls(step))
        t = n - 1 - step
        r = jnp.bitwise_xor(t, me_ref[0])
        m = masks[t]
        adj, head = scan_groups(later[r], gs[r], after, True)
        grp = (adj * f2[r].astype(F32)).astype(BF)
        ggp = (adj * f3[r].astype(F32)).astype(BF)
        pair = jnp.concatenate([grp, ggp], axis=1)
        pair_s[r] = pair
        gconv = adj * f4[r].astype(F32) + mm_nt(pair, wrg[...])
        ri = ri_v[r].astype(F32)
        gri = cw[0:1] * gconv
        sums = [jnp.sum(ri * gconv, axis=0, keepdims=True)]
        for k in (1, 2, 3):
            z = gconv * m[:, k - 1:k]
            zext[k - 1, 0:rows] = z
            moved = zext[k - 1, k:k + rows]
            zext[k - 1, rows:rows + 8] = z[0:8]
            gri = gri + cw[k:k + 1] * moved
            sums.append(jnp.sum(ri * moved, axis=0, keepdims=True))
        sums.append(jnp.sum(gconv, axis=0, keepdims=True))
        sums.append(jnp.sum(grp.astype(F32), axis=0, keepdims=True))
        sums.append(jnp.sum(ggp.astype(F32), axis=0, keepdims=True))
        sums.append(jnp.sum(adj * f1[r].astype(F32), axis=0, keepdims=True))
        sm_v[...] += jnp.concatenate(sums, axis=0)
        gri_v[r] = gri.astype(BF)
        return head

    lax.fori_loop(0, n, block, jnp.zeros((1, width), F32))
    wait(late)
    out = []
    gain1 = jnp.zeros((1, d), F32)
    for k, (i, ref) in enumerate(((3, n31.at[0]), (1, n31.at[1]), (2, n2), (0, n0))):
        part = mm_nt(gbr[i], wb[...]) + mm_nt(gri_v[i], wi[...])
        p_v[i] = part.astype(BF)
        out += begin(sem_out, k, (p_v.at[i], ref))
        gain1 = gain1 + jnp.sum(part * normed[i].astype(F32), axis=0, keepdims=True)

    def as_rows(v):
        v = jnp.concatenate([v, jnp.zeros((1, 3 * width - d), F32)], axis=1)
        return [v[:, i * width:(i + 1) * width] for i in range(3)]

    last_v[0:d] = mm_tn(flat(normed), flat(gri_v)).astype(BF)
    dw = mm_tn(flat(cv_v), flat(pair_s))
    hd = width // 2
    left = lax.broadcasted_iota(jnp.int32, (hd, width), 1) < hd
    for k in (0, 1):
        mine = dw[:, k * width:(k + 1) * width]
        last_v[d + k * hd:d + (k + 1) * hd] = jnp.where(left, mine[:hd], mine[hd:]).astype(BF)
    rest = last_v.shape[0] - d - 2 * hd
    few = [sm_v[...]] + as_rows(gain1) + as_rows(gain2[...]) + [jnp.zeros((rest - 14, width), F32)]
    last_v[d + 2 * hd:] = jnp.concatenate(few, axis=0).astype(BF)
    cut = last_v.shape[0] // 2
    halves = last_v.at[0:cut], last_v.at[cut:2 * cut]
    for part in (0, 1):
        @pl.when(y_ref[0] == part)
        def _():
            wait(begin(sem_out, 4, (halves[part], keep_o), (halves[1 - part], send_o)))
    wait(out)


def ends_branch(y_ref, cur, got, branch_o, out_o):
    for part in (0, 1):
        @pl.when(y_ref[0] == part)
        def _():
            pair = (cur, got) if part == 0 else (got, cur)
            branch_o[...] = pair[0][...].astype(F32)
            out_o[...] = pair[1][...].astype(F32).T


def ends_input(y_ref, cur, got, input_o, recur_o, gate_o, few_o, gains_o, whole):
    d, hd = input_o.shape[0], recur_o.shape[1]
    cut = whole.shape[0] // 2
    for part in (0, 1):
        @pl.when(y_ref[0] == part)
        def _():
            whole[part * cut:(part + 1) * cut] = cur[...]
            whole[(1 - part) * cut:(2 - part) * cut] = got[...]
    input_o[...] = whole[0:d].astype(F32)
    for k, ref in enumerate((recur_o, gate_o)):
        both_heads = whole[d + k * hd:d + (k + 1) * hd].astype(F32)
        for i in range(recur_o.shape[0]):
            ref[i] = both_heads[:, i * hd:(i + 1) * hd]
    few = whole[d + 2 * hd:d + 2 * hd + 16].astype(F32)
    few_o[...] = few[0:8]
    for k in (0, 1):
        at = 8 + 3 * k
        gains_o[k:k + 1] = jnp.concatenate([few[at + i:at + i + 1] for i in range(3)], axis=1)[:, :gains_o.shape[1]]


def mlp_blocks(xb, cot, wg, wu, wd, hid, gg, gu, p_v, ready, base):
    for i in range(xb.shape[0]):
        wait(ready[i])
        x = xb[i]
        ga = mm(x, wg[...])
        if i == 0:
            wait(ready[-1][:1])
        ua = mm(x, wu[...])
        if i == 0:
            wait(ready[-1][1:])
        gh = mm_nt(cot[base + i], wd[...])
        gl, slope = gelu_both(ga)
        hid[base + i] = (gl * ua).astype(BF)
        gg[i] = (gh * ua * slope).astype(BF)
        gu[i] = (gh * gl).astype(BF)
    for i in reversed(range(xb.shape[0])):
        p_v[i] = (mm_nt(gg[i], wg[...]) + mm_nt(gu[i], wu[...])).astype(BF)


def mlp_pre(
    b0, b1, c0, c1, wg_h, wu_h, wd_h, hid_h, gg_h, gu_h, n0, n1,
    xb, cot, wg, wu, wd, hid, gg, gu, p_v, sem_in, sem_out,
):
    first = begin(sem_in, 0, (b0, xb.at[0]), (wg_h, wg))
    then = begin(sem_in, 2, (wu_h, wu), (c0, cot.at[0]), (wd_h, wd))
    second = begin(sem_in, 5, (b1, xb.at[1]), (c1, cot.at[1]))
    mlp_blocks(xb, cot, wg, wu, wd, hid, gg, gu, p_v, (first, second, then), 0)
    wait(begin(sem_out, 0, (hid, hid_h), (gg, gg_h), (gu, gu_h), (p_v.at[1], n1), (p_v.at[0], n0)))


def mlp_main(
    y_ref, b2, b3, c0, c1, c2, c3, hid01, n1, wg_h, wu_h, wd_h, hid_h, gg_h, gu_h, n2, n31, dk_o, ds_o,
    xb, cot, wg, wu, wd, hid, gg, gu, p_v, dd, sem_in, sem_out,
):
    rows, units = hid.shape[1:]
    first = begin(sem_in, 0, (b2, xb.at[0]), (wg_h, wg))
    then = begin(sem_in, 2, (wu_h, wu), (c2, cot.at[2]), (wd_h, wd))
    second = begin(sem_in, 5, (b3, xb.at[1]), (c3, cot.at[3]))
    last = begin(sem_in, 7, (c0, cot.at[0]), (c1, cot.at[1]), (hid01, hid.at[0:2]), (n1, n31.at[1]))
    mlp_blocks(xb, cot, wg, wu, wd, hid, gg, gu, p_v, (first, second, then), 2)
    n31[0] = p_v[1]
    n2[...] = p_v[0]
    out = begin(sem_out, 0, (hid.at[2:4], hid_h), (gg, gg_h), (gu, gu_h))
    wait(last)
    call_ = cot[...].reshape(4 * rows, cot.shape[2])
    hall = hid[...].reshape(4 * rows, units)
    half = units // 2
    for part in (0, 1):
        dd[part] = mm_tn(hall[:, part * half:(part + 1) * half], call_).astype(BF)
    for part in (0, 1):
        @pl.when(y_ref[0] == part)
        def _():
            wait(begin(sem_out, 5, (dd.at[part], dk_o), (dd.at[1 - part], ds_o)))
    wait(out)


def mlp_post(
    y_ref, z_ref, b0, b1, b2, b3, gg01, gg23, gu01, gu23, hid01, hid23, wd_h, gk_o, gs_o, uk_o, us_o, m0, m2, m31,
    xb, gg, gu, hid, wd, dg, du, p_v, sem_in, sem_out,
):
    n, rows, units = hid.shape
    first = begin(sem_in, 0, (b0, xb.at[0]), (b1, xb.at[1]), (b2, xb.at[2]), (b3, xb.at[3]),
                  (gg01, gg.at[0:2]), (gg23, gg.at[2:4]))
    second = begin(sem_in, 6, (gu01, gu.at[0:2]), (gu23, gu.at[2:4]))
    third = begin(sem_in, 8, (hid01, hid.at[0:2]), (hid23, hid.at[2:4]), (wd_h, wd))

    def flat(ref):
        return ref[...].reshape(n * rows, ref.shape[2])

    wait(first)
    xall = flat(xb)
    half = dg.shape[1]
    for part in (0, 1):
        dg[part] = mm_tn(xall[:, part * half:(part + 1) * half], flat(gg)).astype(BF)
    wait(second)
    for part in (0, 1):
        du[part] = mm_tn(xall[:, part * half:(part + 1) * half], flat(gu)).astype(BF)
    for part in (0, 1):
        @pl.when(y_ref[0] == part)
        def _():
            begin(sem_out, 4, (dg.at[part], gk_o), (dg.at[1 - part], gs_o))

        @pl.when(z_ref[0] == part)
        def _():
            begin(sem_out, 6, (du.at[part], uk_o), (du.at[1 - part], us_o))
    out = []
    wait(third)
    for k, (i, ref) in enumerate(((3, m31.at[0]), (1, m31.at[1]), (2, m2), (0, m0))):
        p_v[i] = mm(hid[i], wd[...]).astype(BF)
        out += begin(sem_out, k, (p_v.at[i], ref))
    wait(out)
    wait([pltpu.make_async_copy(v.at[0], o, sem_out.at[4 + k])
          for k, (v, o) in enumerate(((dg, gk_o), (dg, gs_o), (du, uk_o), (du, us_o)))])


def add_two(a, b, got_a, got_b, send_o, own_o):
    send_o[...] = plus(a[...], got_a[...]).astype(BF)
    own_o[...] = plus(b[...], got_b[...]).astype(BF)


def add_both(i2, i0, o2, o0, got_i, got_o, send_o, own_i, own_o):
    send_o[0] = plus(i2[...], got_i[0]).astype(BF)
    own_i[...] = plus(i0[...], got_i[1]).astype(BF)
    send_o[1] = plus(o2[...], got_o[0]).astype(BF)
    own_o[...] = plus(o0[...], got_o[1]).astype(BF)


def add_pair(a, b, got, send_o, own_o):
    send_o[...] = plus(a[...], got[0]).astype(BF)
    own_o[...] = plus(b[...], got[1]).astype(BF)


def mid_fwd(x, own, far, gain, mid_o, n_o):
    mid = x[...].astype(F32) + plus(own[...], far[...])
    inv = lax.rsqrt(jnp.mean(mid * mid, axis=-1, keepdims=True) + EPSILON)
    mid_o[...] = mid
    n_o[...] = (mid * inv * gain[...]).astype(BF)


def norm_back(total, values, gain):
    inv = lax.rsqrt(jnp.mean(values * values, axis=-1, keepdims=True) + EPSILON)
    v = total * gain
    scaled = values * inv
    mean = jnp.mean(v * scaled, axis=-1, keepdims=True)
    grad = inv * (v - scaled * mean)
    return grad, jnp.sum(total * scaled, axis=0, keepdims=True)


def mid_bwd(mid, own, far, gain, cot, gm_o, gb_o, gg_o):
    grad, gsum = norm_back(plus(own[...], far[...]), mid[...], gain[...])
    gm = cot[...].astype(F32) + grad
    gm_o[...] = gm
    gb_o[...] = gm.astype(BF)
    gg_o[...] = gsum


def last_bwd(x, mid, own_i, own_o, far, gain, gm, o, out_o):
    grad, _ = norm_back(plus(own_i[...], far[0]), x[...].astype(F32), gain[...])
    o[...] = gm[...] + grad
    out_o[...] = (mid[...] + plus(own_o[...], far[1])).astype(BF)


def cost(us):
    return pl.CostEstimate(flops=1 + int(us * 1.15e9), bytes_accessed=0, transcendentals=0)


HBM, VMEM, SMEM = pltpu.HBM, pltpu.VMEM, pltpu.SMEM


def call(kernel, outs, *args, name, us, mib, places, out, scratch=()):
    spec = {"h": HBM, "v": VMEM, "s": SMEM, "a": pl.ANY}
    args = [
        pltpu.with_memory_space_constraint(a, VMEM if p == "v" else HBM) if p in "hv" else a
        for p, a in zip(places, args, strict=True)
    ]
    return pl.pallas_call(
        kernel,
        out_shape=[(VMEM if p == "v" else HBM)(*o) for p, o in zip(out, outs, strict=True)],
        in_specs=[pl.BlockSpec(memory_space=spec[p]) if p in spec else pl.BlockSpec() for p in places],
        out_specs=[pl.BlockSpec(memory_space=spec[p]) if p in spec else pl.BlockSpec() for p in out],
        scratch_shapes=list(scratch),
        compiler_params=pltpu.CompilerParams(vmem_limit_bytes=mib * MIB),
        cost_estimate=cost(us),
        name=name,
    )(*args)


CORE = [(i, i ^ 1) for i in range(4)]
FAR = [(i, i ^ 2) for i in range(4)]


def to_core(v):
    return lax.ppermute(v, "ch", CORE)


def to_far(v):
    return lax.ppermute(v, "ch", FAR)


class Order:
    def __init__(self):
        self.last = None

    def run(self, work, *values):
        if self.last is not None:
            values = lax.optimization_barrier((*values, *self.last))[:len(values)]
        got = work(*values)
        self.last = tuple(got) if isinstance(got, (tuple, list)) else (got,)
        return got

    def gate(self, value):
        return lax.optimization_barrier((value, *self.last))[0]

    def take(self, value):
        return self.run(lambda v: (v,), value)[0]


def dyn(g, index, size):
    return lax.dynamic_slice_in_dim(g, index * size, size, 0)


def plus(a, b):
    return a.astype(F32) + b.astype(F32)


def add_low(a, b):
    return plus(a, b).astype(BF)


def put(total, piece, index):
    return lax.dynamic_update_slice_in_dim(total, piece.astype(total.dtype), index * piece.shape[0], 0)


Y = [(i, i ^ 1) for i in range(8)]
Z1 = [(i, i ^ 2) for i in range(8)]
Z2 = [(i, i ^ 4) for i in range(8)]
def both(low, a, b):
    return jnp.concatenate([jnp.where(low, a, b), jnp.where(low, b, a)], 0)


def sum_rows_plain(keep, send, ends):
    yield "sent"
    return ends(*(lax.psum(v.astype(F32), "rows").astype(BF) for v in (keep, send)))


INWARD = [(0, 2), (1, 3), (6, 4), (7, 5)]
MIDDLE = [(2, 4), (3, 5), (4, 2), (5, 3)]
OUTWARD = [(2, 0), (3, 1), (4, 6), (5, 7)]


def send_on(value, pairs, order):
    if (yield "ready"):
        value = order.gate(value)
    got = lax.ppermute(value, "rows", pairs)
    yield "sent"
    return order.take(got)


def sum_rows_halves(keep, send, order, way, ends):
    me = lax.axis_index("rows")
    y, z = (Y, me % 2), (Z1, (me // 2) % 2)
    stages = ((y, z) if way == "y" else (z, y)) + ((Z2, me // 4),)
    got = yield from send_on(send, stages[0][0], order)
    yield "came"
    for pairs, bit in stages[1:]:
        half = keep.shape[0] // 2

        def split(a, b, bit=bit, half=half):
            return (add_low(dyn(a, 1 - bit, half), dyn(b, 1 - bit, half)), add_low(dyn(a, bit, half), dyn(b, bit, half)))

        send, keep = order.run(split, keep, got)
        got = yield from send_on(send, pairs, order)
        yield "came"
    cur = order.run(add_low, keep, got)
    for pairs, bit in stages[::-1]:
        got = yield from send_on(cur, pairs, order)
        yield "came"
        if pairs is stages[0][0]:
            return order.run(ends, cur, got)
        cur = order.run(lambda a, b, bit=bit: both(bit == 0, a, b), cur, got)


def sum_rows_line(keep, send, order, ends):
    me = lax.axis_index("rows")
    y, z = me % 2, me // 2
    inner = (z == 1) | (z == 2)
    got = yield from send_on(send, Y, order)
    yield "came"
    cur = order.run(add_low, keep, got)
    for pairs in (INWARD, MIDDLE):
        got = yield from send_on(cur, pairs, order)
        yield "came"
        cur = order.run(add_low, cur, got)
    got = yield from send_on(cur, OUTWARD, order)
    yield "came"
    cur = order.run(lambda a, b: jnp.where(inner, a, b), cur, got)
    got = yield from send_on(cur, Y, order)
    yield "came"
    return order.run(ends, cur, got)


class Chain:
    def __init__(self, steps):
        self.steps, self.value, self.state, self.held = steps, None, None, False
        self.go()

    def step(self, first=False):
        try:
            self.state = self.steps.send(None if self.state is None else self.held)
            self.held = False
        except StopIteration as end:
            self.state, self.value = "done", end.value

    def to(self, state):
        if self.state == "done":
            return
        self.step()
        while self.state not in (state, "done"):
            self.step()
        self.held = state == "ready"

    def come(self):
        if self.state == "sent":
            self.to("came")

    def go(self):
        self.to("sent")

    def finish(self):
        while self.state != "done":
            self.go()
        return self.value


def block_diag(w):
    h, d, e = w.shape
    rows = [
        jnp.concatenate([w[i] if i == j else jnp.zeros((d, e), w.dtype) for j in range(h)], axis=1)
        for i in range(h)
    ]
    return jnp.concatenate(rows, axis=0)


def body(n_rows, inputs, segment_ids, mixer_gain, branch_weight, input_weight, conv_weight, conv_bias,
         recur_weight, recur_bias, gate_weight, gate_bias, decay_param, out_weight, mlp_gain, mlp_gate,
         mlp_up, mlp_down, cotangent):
    x = inputs[0]
    cot = cotangent[0]
    rows, d = x.shape
    width = branch_weight.shape[1]
    units = mlp_gate.shape[1]
    heads, hd, _ = recur_weight.shape
    seq = segment_ids.shape[1]
    n = seq // rows
    me = lax.axis_index("ch").astype(jnp.int32)[None]
    gain1 = mixer_gain[None]
    gain2 = mlp_gain[None]
    order = Order()
    row = lax.axis_index("rows").astype(jnp.int32)[None]
    y_half = row % 2 if n_rows == 8 else jnp.zeros((1,), jnp.int32)
    z_half = (row // 2) % 2 if n_rows == 8 else jnp.zeros((1,), jnp.int32)

    split = {k: z_half if v == "z" else y_half for k, v in KINDS.items()}

    def total(keep, send, way, ends):
        if n_rows != 8:
            return Chain(sum_rows_plain(keep, send, ends))
        if way == "line":
            return Chain(sum_rows_line(keep, send, order, ends))
        return Chain(sum_rows_halves(keep, send, order, way, ends))

    x_far, x_near = to_far(x), to_core(x)

    def tables(ids, rw, gw, rb, gb_, dp):
        marks = [
            (jnp.pad(ids, (k, 0), constant_values=-1)[:seq] == ids).astype(F32) for k in (1, 2, 3)
        ]
        masks = jnp.pad(jnp.stack(marks, axis=1), ((0, 0), (0, 125))).reshape(n, rows, 128)
        wrg = jnp.concatenate([block_diag(rw), block_diag(gw)], axis=1)
        return masks, wrg, jnp.concatenate([rb, gb_])[None], (-8.0 * jax.nn.softplus(dp))[None]

    masks, wrg, brg, c8 = order.run(
        tables, segment_ids[0], recur_weight, gate_weight, recur_bias, gate_bias, decay_param
    )
    cb = conv_bias[None]
    blk, narrow, wide = (rows, d), (n, rows, width), (n, rows, units)
    four, two = (n, rows, d), (2, rows, d)
    narrow2, wide2 = (2, rows, width), (2, rows, units)
    dma = pltpu.SemaphoreType.DMA
    normed01, br01, ri01, wb_v, wi_v = order.run(
        functools.partial(
            call, mixer_pre, [(two, BF), (narrow2, F32), (narrow2, F32), ((d, width), BF), ((d, width), BF)],
            name="mixer_pre", us=0, mib=20, places="aahhi", out="hhhvv", scratch=[
                VMEM(two, BF), VMEM(two, BF), VMEM(narrow2, F32),
                VMEM(narrow2, F32), dma((4,)), dma((3,)),
            ]),
        x, x_near, branch_weight, input_weight, gain1)
    x_far = order.take(x_far)
    x_diag = to_core(x_far)
    cot_far = to_far(cot)
    x_diag = order.take(x_diag)
    fwd = order.run(
        functools.partial(
            call, mixer_fwd,
            [(two, BF), (narrow2, F32), (narrow, BF), (narrow, BF), (narrow, F32), (narrow, BF)] + [(blk, BF)] * 4,
            name="mixer_fwd", us=0, mib=30, places="saavvhhhhhiiiii", out="h" * 6 + "vvvv", scratch=[
                VMEM(two, BF), VMEM((width, 2 * width), BF),
                VMEM((n, rows, 128), F32), VMEM((width, d), BF), VMEM(two, BF), VMEM(narrow, F32),
                VMEM(narrow, F32), VMEM(narrow, BF), VMEM(narrow, BF), VMEM(narrow, F32), VMEM(narrow, BF),
                VMEM((rows + 8, width), F32), VMEM((rows + 8, width), F32), dma((9,)), dma((6,)),
            ]),
        me, x_far, x_diag, wb_v, wi_v, br01, ri01, wrg, masks, out_weight, gain1, conv_weight, cb,
        brg, c8)
    normed23, br23, ri, cv, sp, mix = fwd[:6]
    cot_far = order.take(cot_far)

    def near_half(own, far, pair):
        got = to_core(pair)
        return order.run(
            functools.partial(call, add_pair, [(blk, BF)] * 2, name="add_pair", us=0, mib=6, places="iii", out="vv"),
            far, own, got)

    send, own = order.run(
        functools.partial(call, add_two, [(blk, BF)] * 2, name="add_two", us=0, mib=6, places="vvii", out="vv"),
        fwd[7], fwd[6], to_core(fwd[8]), to_core(fwd[9]))
    far = to_far(send)
    cot_near, cot_diag = to_core(cot), to_core(cot_far)
    cot_near = order.take(cot_near)
    cot_diag = order.take(cot_diag)
    a1, gl, later, *fs = order.run(
        functools.partial(
            call, mixer_mid, [(narrow, BF), (narrow, BF), (narrow, F32)] + [(narrow, BF)] * 4, name="mixer_mid", us=0,
            mib=30, places="s" + "h" * 6 + "ii", out="h" * 7, scratch=[
                VMEM(narrow, F32), VMEM(narrow, BF), VMEM(narrow, F32), VMEM((width, 2 * width), BF),
                VMEM((n, rows, 128), F32), VMEM(narrow, BF), VMEM(narrow, BF), VMEM(narrow, F32)]
            + [VMEM(narrow, BF)] * 4 + [VMEM((rows + 8, width), F32), dma((6,)), dma((7,))]),
        me, br01, br23, cv, sp, wrg, masks, brg, c8)
    mid, normed2 = order.run(functools.partial(
        call, mid_fwd, [(blk, F32), (blk, BF)], name="mid_fwd", us=0, mib=8, places="ivvi", out="iv"),
        x, own, far, gain2)
    n_far, n_near = to_far(normed2), to_core(normed2)
    n_near = order.take(n_near)
    mlp_scratch = [
        VMEM((d, units), BF), VMEM((d, units), BF), VMEM((units, d), BF)]
    hid01, gg01, gu01, g0, g1 = order.run(
        functools.partial(
            call, mlp_pre, [(wide2, BF)] * 3 + [(blk, BF)] * 2, name="mlp_pre", us=0, mib=30, places="aahhhhh",
            out="h" * 5, scratch=[VMEM(two, BF), VMEM(two, BF)] + mlp_scratch + [VMEM(wide2, BF)] * 3 + [
                VMEM(two, BF), dma((7,)), dma((5,))]),
        normed2, n_near, cot, cot_near, mlp_gate, mlp_up, mlp_down)
    n_far = order.take(n_far)
    n_diag = order.take(to_core(n_far))
    hid23, gg23, gu23, g2, g31, down_keep, down_send = order.run(
        functools.partial(
            call, mlp_main, [(wide2, BF)] * 3 + [(blk, BF), (two, BF)] + [((units // 2, d), BF)] * 2, name="mlp_main",
            us=0, mib=26, places="saahhhhhhhhh", out="hhhvvhh",
            scratch=[VMEM(two, BF), VMEM(four, BF)] + mlp_scratch + [VMEM(wide, BF), VMEM(wide2, BF), VMEM(wide2, BF)] + [
                VMEM(two, BF), VMEM((2, units // 2, d), BF), dma((11,)), dma((7,))]),
        split["d"], n_far, n_diag, cot, cot_near, cot_far, cot_diag, hid01, g1, mlp_gate, mlp_up, mlp_down)
    y_low, z_low = y_half[0] == 0, z_half[0] == 0

    def wide_ends(low, a, b):
        return both(low, a, b).astype(F32)

    def ends_of(kind):
        return functools.partial(wide_ends, y_low if split[kind] is y_half else z_low)

    s_down = total(down_keep, down_send, KINDS["d"], ends_of("d"))
    g_send, g_own = near_half(g0, g2, g31)
    from_far = to_far(g_send)
    post = order.run(
        functools.partial(
            call, mlp_post, [((d // 2, units), BF)] * 4 + [(blk, BF), (blk, BF), (two, BF)], name="mlp_post", us=0,
            mib=26, places="ssaaaahhhhhhh", out="h" * 7, scratch=[
                VMEM(four, BF), VMEM(wide, BF), VMEM(wide, BF), VMEM(wide, BF), VMEM((units, d), BF),
                VMEM((2, d // 2, units), BF), VMEM((2, d // 2, units), BF), VMEM(four, BF), dma((11,)), dma((8,)),
            ]),
        split["g"], split["u"], normed2, n_near, n_far, n_diag, gg01, gg23, gu01, gu23, hid01, hid23, mlp_down)
    s_gate = total(post[0], post[1], KINDS["g"], ends_of("g"))
    s_up = total(post[2], post[3], KINDS["u"], ends_of("u"))
    chains = {"d": s_down, "g": s_gate, "u": s_up}
    live = {}

    def at_rf():
        gm, gb, gsum2 = order.run(functools.partial(
            call, mid_bwd, [(blk, F32), (blk, BF), ((1, d), F32)], name="mid_bwd", us=10, mib=8, places="ivvii", out="ivi"),
            mid, g_own, from_far, gain2, cot)
        g_near, g_far = to_core(gb), to_far(gb)
        live.update(gm=gm, gb=gb, gsum2=gsum2, g_near=g_near, g_far=g_far)

    def at_gf():
        gb = live["gb"]
        g_far = order.take(live["g_far"])
        g_diag = to_core(g_far)
        g_near = order.take(live["g_near"])
        g_diag = order.take(g_diag)
        gs, gbr, p_keep, p_send = order.run(
            functools.partial(
                call, mixer_out, [(narrow, F32), (narrow, BF)] + [((d, width), BF)] * 2, name="mixer_out", us=0, mib=30,
                places="shaaa" + "h" * 6, out="h" * 4, scratch=[
                    VMEM(four, BF), VMEM((width, d), BF), VMEM(narrow, BF), VMEM(narrow, BF), VMEM(four, BF),
                    VMEM(narrow, BF), VMEM(narrow, F32), VMEM(narrow, BF), VMEM((2, d, width), BF), dma((10,)), dma((4,))]),
            split["p"], gb, g_near, g_far, g_diag, out_weight, a1, gl, normed01, normed23, mix)
        chains["p"] = total(p_keep, p_send, KINDS["p"], functools.partial(
            call, ends_branch, [((d, width), F32), ((width, d), F32)], split["p"], name="ends_branch", us=0, mib=16,
            places="sii", out="ii"))
        live.update(gs=gs, gbr=gbr)

    def at_m():
        last_rows = d + 2 * hd + 64
        bwd = order.run(
            functools.partial(
                call, mixer_bwd, [(blk, BF), (blk, BF), (two, BF)] + [((last_rows // 2, width), BF)] * 2,
                name="mixer_bwd", us=0, mib=36, places="ss" + "h" * 15 + "ii", out="h" * 5, scratch=[
                    VMEM(narrow, F32), VMEM(narrow, F32)] + [VMEM(narrow, BF)] * 6 + [
                    VMEM((width, 2 * width), BF), VMEM((n, rows, 128), F32), VMEM(narrow, BF), VMEM(four, BF),
                    VMEM((d, width), BF), VMEM((d, width), BF), VMEM((n, rows, 2 * width), BF), VMEM(narrow, BF),
                    VMEM(four, BF), VMEM((last_rows, width), BF), VMEM((8, width), F32), VMEM((3, rows + 8, width), F32),
                    dma((8, n)), dma((8,)), dma((6,)),
                ]),
            me, split["q"], live["gs"], later, *fs, ri, cv, wrg, masks, live["gbr"], normed01, normed23, branch_weight, input_weight,
            conv_weight, live["gsum2"])
        chains["q"] = total(bwd[3], bwd[4], KINDS["q"], functools.partial(
            call, ends_input, [((d, width), F32), ((heads, hd, hd), F32), ((heads, hd, hd), F32), ((8, width), F32),
             ((2, d), F32)], split["q"], name="ends_input", us=0, mib=16, places="sii", out="iiiii", scratch=[VMEM((last_rows, width), BF)]))

        live.update(bwd=bwd)

    def sum_ch(n0, n2, pair):
        got_i, got_o = to_core(order.gate(pair)), to_core(order.gate(post[6]))
        yield "sent"
        got_i, got_o = order.run(lambda a, b: (a, b), got_i, got_o)
        yield "came"
        send, own_i, own_o = order.run(
            functools.partial(
                call, add_both, [(two, BF), (blk, BF), (blk, BF)], name="add_both", us=0, mib=14, places="iiiiii", out="uuu"),
            n2, n0, post[5], post[4], got_i, got_o)
        far = to_far(send)
        yield "sent"
        far = order.take(far)
        yield "came"
        return order.run(
            functools.partial(
                call, last_bwd, [(blk, F32), (blk, BF)], name="last_bwd", us=0, mib=14, places="iiiiiii", out="ii"),
            x, mid, own_i, own_o, far, gain1, live["gm"])

    events = {"rf": at_rf, "gf": at_gf, "m": at_m}

    def turn(what):
        if what in events:
            events[what]()
            return
        if what == "c":
            if "bwd" in live and "i" not in chains and chains["d"].state == "done":
                chains["i"] = Chain(sum_ch(*live["bwd"][:3]))
            return
        chains[what].go()

    for what in PLAN:
        turn(what)
    while "i" not in chains or any(c.state != "done" for c in chains.values()):
        for what in PLAN_AFTER:
            if what in chains or what == "c":
                turn(what)
    input_grad, output = chains["i"].value
    t_branch, t_out = chains["p"].value
    t_input, t_recur, t_gate_w, ts, gains = chains["q"].value
    t_down, t_gate, t_up = (s.value for s in (s_down, s_gate, s_up))
    others = [lax.ppermute(gains, "ch", [(i, i ^ k) for i in range(4)]) for k in (3, 2, 1)]
    gain1_grad, gain2_grad = order.run(
        lambda own, c, b, a: tuple((own[k] + a[k]) + (b[k] + c[k]) for k in (0, 1)), gains, *others)
    gain1_grad = gain1_grad / mixer_gain
    decay_grad = ts[7] * -8.0 * jax.nn.sigmoid(decay_param)
    return (
        output[None],
        input_grad[None],
        gain1_grad,
        t_branch,
        t_input,
        ts[0:4],
        ts[4],
        t_recur,
        ts[5],
        t_gate_w,
        ts[6],
        decay_grad,
        t_out,
        gain2_grad,
        t_gate,
        t_up,
        t_down,
    )


def solution(mesh):
    rows, ch = P("rows", "ch", None), P("ch")
    cols, lead = P(None, "ch"), P("ch", None)
    heads = P("ch", None, None)
    return jax.shard_map(
        functools.partial(body, mesh.shape["rows"]),
        mesh=mesh,
        in_specs=(rows, P("rows", None), P(), cols, cols, cols, ch, heads, ch, heads, ch, ch, lead, P(),
                  cols, cols, lead, rows),
        out_specs=(rows, rows, P(), cols, cols, cols, ch, heads, ch, heads, ch, ch, lead, P(), cols, cols, lead),
        check_vma=False,
    )
```

```python
import functools

import jax
import jax.numpy as jnp
from jax import lax
from jax.experimental import pallas as pl
from jax.experimental.pallas import tpu as pltpu
from jax.sharding import PartitionSpec as P

EPSILON = 1e-06
BF = jnp.bfloat16
F32 = jnp.float32
MIB = 1024 * 1024
KINDS = {"d": "line", "g": "z", "u": "line", "p": "line", "q": "line"}
PLAN_AFTER = ("g", "u", "d", "p", "q", "i", "c")
PLAN = ("d", "rf", "g", "u", "gf", "d", "m", "g", "u", "d", "p", "q")
GELU_C = 0.7978845608028654
GELU_A = 0.044715


def mm(a, b):
    return lax.dot_general(a, b, (((1,), (0,)), ((), ())), preferred_element_type=F32)


def mm_nt(a, b):
    return lax.dot_general(a, b, (((1,), (1,)), ((), ())), preferred_element_type=F32)


def mm_tn(a, b):
    return lax.dot_general(a, b, (((0,), (0,)), ((), ())), preferred_element_type=F32)


def sigmoid(v):
    return 0.5 * jnp.tanh(0.5 * v) + 0.5


def gelu_both(v):
    sq = v * v
    th = jnp.tanh(GELU_C * v * (1.0 + GELU_A * sq))
    half = 0.5 * th + 0.5
    slope = half + (0.5 * GELU_C) * v * (1.0 - th * th) * (1.0 + (3.0 * GELU_A) * sq)
    return v * half, slope


def gelu_only(v):
    th = jnp.tanh(GELU_C * v * (1.0 + GELU_A * (v * v)))
    return v * (0.5 * th + 0.5)


def scan_groups(mult, add, start, back):
    rows, cols = mult.shape
    a = mult.reshape(rows // 8, 8, cols)
    d = add.reshape(rows // 8, 8, cols)
    sub = lax.broadcasted_iota(jnp.int32, (1, 8, cols), 1)
    for k in (1, 2, 4):
        ok = sub < 8 - k if back else sub >= k
        turn = 8 - k if back else k
        d = d + a * jnp.where(ok, pltpu.roll(d, turn, 1), 0.0)
        a = a * jnp.where(ok, pltpu.roll(a, turn, 1), 1.0)
    state = start
    got = [None] * (rows // 8)
    order = range(rows // 8)
    for g in reversed(order) if back else order:
        now = d[g] + a[g] * state
        state = now[0:1] if back else now[7:8]
        got[g] = now
    return jnp.concatenate(got, axis=0), state


def gate_values(conv, pre, c8, width):
    rg = sigmoid(pre[:, :width])
    ig = sigmoid(pre[:, width:])
    forget = jnp.exp(c8 * rg)
    om = 1.0 - forget * forget
    top = jnp.maximum(om, 0.001)
    inv = lax.rsqrt(top)
    return rg, ig, forget, om, top * inv, inv


def begin(sem, first, *pairs):
    copies = [pltpu.make_async_copy(src, dst, sem.at[first + k]) for k, (src, dst) in enumerate(pairs)]
    for c in copies:
        c.start()
    return copies


def wait(copies):
    for c in copies:
        c.wait()


def project(x, gain, wb, wi):
    x = x.astype(F32)
    inv = lax.rsqrt(jnp.mean(x * x, axis=-1, keepdims=True) + EPSILON)
    normed = (x * inv * gain).astype(BF)
    return normed, mm(normed, wb), mm(normed, wi)


def mixer_pre(b0, b1, wb_h, wi_h, gain, normed_h, br_h, ri_h, wb, wi, xb, normed_v, br_v, ri_v, sem_in, sem_out):
    first = begin(sem_in, 0, (b0, xb.at[0]), (wb_h, wb), (wi_h, wi))
    second = begin(sem_in, 3, (b1, xb.at[1]))
    for i, ready in enumerate((first, second)):
        wait(ready)
        normed_v[i], br_v[i], ri_v[i] = project(xb[i], gain[...], wb[...], wi[...])
    wait(begin(sem_out, 0, (normed_v, normed_h), (br_v, br_h), (ri_v, ri_h)))


def mixer_fwd(
    me_ref, b2, b3, wb, wi, br01, ri01, wrg_h, masks_h, wo_h, gain, cw, cb, brg, c8,
    normed_h, br_h, ri_h, cv_h, sp_h, mix_h, p0, p2, p3, p1,
    xb, wrg, masks, wo, normed_v, br_v, ri_s, ri_v, cv_v, sp_v, mix_v, ext, sext, sem_in, sem_out,
):
    n, rows, width = br_v.shape
    first = begin(sem_in, 0, (b2, xb.at[0]))
    second = begin(sem_in, 3, (b3, xb.at[1]))
    later = begin(sem_in, 4, (ri01, ri_s.at[0:2]), (wrg_h, wrg), (masks_h, masks), (br01, br_v.at[0:2]), (wo_h, wo))
    for i, ready in enumerate((first, second)):
        wait(ready)
        normed_v[i], br_v[2 + i], ri_s[2 + i] = project(xb[i], gain[...], wb[...], wi[...])
    out = begin(sem_out, 0, (normed_v, normed_h), (br_v.at[2:4], br_h))
    ext[0:8] = jnp.zeros((8, width), F32)
    wait(later)

    def block(t, first):
        r = jnp.bitwise_xor(t, me_ref[0])
        ri = ri_s[r]
        ri_v[r] = ri.astype(BF)
        ext[8:8 + rows] = ri
        m = masks[t]
        conv = cb[...] + cw[0:1] * ri
        for k in (1, 2, 3):
            conv = conv + cw[k:k + 1] * (ext[8 - k:8 - k + rows] * m[:, k - 1:k])
        ext[0:8] = ext[rows:rows + 8]
        cv = conv.astype(BF)
        cv_v[r] = cv
        cvf = cv.astype(F32)
        pre = mm(cv, wrg[...]) + brg[...]
        rg, ig, forget, om, scale, _ = gate_values(cvf, pre, c8[...], width)
        keep = m[:, 0:1]
        states, last = scan_groups(forget * keep, scale * ig * cvf, first, False)
        sext[8:8 + rows] = states
        sext[7:8] = first
        sp_v[r] = sext[7:7 + rows] * keep
        mix_v[r] = (gelu_only(br_v[r]) * states).astype(BF)
        return last

    lax.fori_loop(0, n, block, jnp.zeros((1, width), F32))
    out += begin(sem_out, 2, (ri_v, ri_h), (cv_v, cv_h), (sp_v, sp_h), (mix_v, mix_h))
    for i, ref in ((3, p3), (1, p1), (2, p2), (0, p0)):
        ref[...] = mm(mix_v[i], wo[...]).astype(BF)
    wait(out)


def mixer_mid(
    me_ref, br01, br23, cv_h, sp_h, wrg_h, masks_h, brg, c8,
    a1_h, gl_h, later_h, f1_h, f2_h, f3_h, f4_h,
    br, cv, sp, wrg, masks, a1, gl, later, f1, f2, f3, f4, aext, sem_in, sem_out,
):
    n, rows, width = br.shape
    wait(begin(sem_in, 0, (br01, br.at[0:2]), (br23, br.at[2:4]), (cv_h, cv), (wrg_h, wrg), (masks_h, masks), (sp_h, sp)))
    aext[rows:rows + 8] = jnp.zeros((8, width), F32)

    def block(step, _):
        t = n - 1 - step
        r = jnp.bitwise_xor(t, me_ref[0])
        gelu, slope = gelu_both(br[r])
        cvb = cv[r]
        cvf = cvb.astype(F32)
        c8v = c8[...]
        pre = mm(cvb, wrg[...]) + brg[...]
        rg, ig, forget, om, scale, inv = gate_values(cvf, pre, c8v, width)
        m = masks[t]
        before = sp[r]
        igc = ig * cvf
        gl[r] = gelu.astype(BF)
        a1[r] = ((forget * before + scale * igc) * slope).astype(BF)
        aext[0:rows] = forget * m[:, 0:1]
        later[r] = aext[1:1 + rows]
        aext[rows:rows + 8] = aext[0:8]
        q = jnp.where(om > 0.001, -forget * inv, 0.0)
        base = (before + q * igc) * forget * rg
        f1[r] = base.astype(BF)
        f2[r] = (base * (1.0 - rg) * c8v).astype(BF)
        f3[r] = (scale * igc * (1.0 - ig)).astype(BF)
        f4[r] = (scale * ig).astype(BF)
        return 0

    lax.fori_loop(0, n, block, 0)
    wait(begin(sem_out, 0, (a1, a1_h), (gl, gl_h), (later, later_h), (f1, f1_h), (f2, f2_h), (f3, f3_h), (f4, f4_h)))


def flat(ref):
    return ref[...].reshape(ref.shape[0] * ref.shape[1], ref.shape[2])


def mixer_out(
    y_ref, b0, b1, b2, b3, wo_h, a1_h, gl_h, normed01, normed23, mix_h,
    gs_h, gbr_h, keep_o, send_o,
    gb, wo, a1, gl, normed, mix, gs, gbr, pair, sem_in, sem_out,
):
    n = gb.shape[0]
    first = begin(sem_in, 0, (wo_h, wo), (b0, gb.at[0]), (b1, gb.at[1]), (b2, gb.at[2]), (b3, gb.at[3]))
    then = begin(sem_in, 5, (a1_h, a1), (gl_h, gl))
    last = begin(sem_in, 7, (normed01, normed.at[0:2]), (normed23, normed.at[2:4]), (mix_h, mix))
    wait(first)
    for i in range(n):
        gmix = mm_nt(gb[i], wo[...])
        if i == 0:
            wait(then)
        gbr[i] = (gmix * a1[i].astype(F32)).astype(BF)
        gs[i] = gmix * gl[i].astype(F32)
    out = begin(sem_out, 0, (gs, gs_h), (gbr, gbr_h))
    wait(last)
    pair[0] = mm_tn(flat(normed), flat(gbr)).astype(BF)
    pair[1] = mm_tn(flat(gb), flat(mix)).astype(BF)
    for part in (0, 1):
        @pl.when(y_ref[0] == part)
        def _():
            wait(begin(sem_out, 2, (pair.at[part], keep_o), (pair.at[1 - part], send_o)))
    wait(out)


def mixer_bwd(
    me_ref, y_ref, gs_h, later_h, f1_h, f2_h, f3_h, f4_h, ri_h, cv_h, wrg_h, masks_h, gbr_h, normed01, normed23,
    wb_h, wi_h, cw, gain2,
    n0, n2, n31, keep_o, send_o,
    gs, later, f1, f2, f3, f4, ri_v, cv_v, wrg, masks, gbr, normed, wb, wi,
    pair_s, gri_v, p_v, last_v, sm_v, zext, sem_block, sem_in, sem_out,
):
    n, rows, width = gs.shape
    d = normed.shape[2]
    early = begin(sem_in, 0, (wrg_h, wrg), (masks_h, masks))
    blocks = ((gs_h, gs), (later_h, later), (f1_h, f1), (f2_h, f2), (f3_h, f3), (f4_h, f4), (ri_h, ri_v), (cv_h, cv_v))

    def pulls(step):
        r = jnp.bitwise_xor(n - 1 - step, me_ref[0])
        return [pltpu.make_async_copy(src.at[r], dst.at[r], sem_block.at[k, step])
                for k, (src, dst) in enumerate(blocks)]

    for step in range(n):
        for c in pulls(step):
            c.start()
    late = begin(sem_in, 2, (gbr_h, gbr), (normed01, normed.at[0:2]), (normed23, normed.at[2:4]), (wb_h, wb), (wi_h, wi))
    zext[:, rows:rows + 8] = jnp.zeros((3, 8, width), F32)
    sm_v[...] = jnp.zeros(sm_v.shape, F32)
    wait(early)

    def block(step, after):
        wait(pulls(step))
        t = n - 1 - step
        r = jnp.bitwise_xor(t, me_ref[0])
        m = masks[t]
        adj, head = scan_groups(later[r], gs[r], after, True)
        grp = (adj * f2[r].astype(F32)).astype(BF)
        ggp = (adj * f3[r].astype(F32)).astype(BF)
        pair = jnp.concatenate([grp, ggp], axis=1)
        pair_s[r] = pair
        gconv = adj * f4[r].astype(F32) + mm_nt(pair, wrg[...])
        ri = ri_v[r].astype(F32)
        gri = cw[0:1] * gconv
        sums = [jnp.sum(ri * gconv, axis=0, keepdims=True)]
        for k in (1, 2, 3):
            z = gconv * m[:, k - 1:k]
            zext[k - 1, 0:rows] = z
            moved = zext[k - 1, k:k + rows]
            zext[k - 1, rows:rows + 8] = z[0:8]
            gri = gri + cw[k:k + 1] * moved
            sums.append(jnp.sum(ri * moved, axis=0, keepdims=True))
        sums.append(jnp.sum(gconv, axis=0, keepdims=True))
        sums.append(jnp.sum(grp.astype(F32), axis=0, keepdims=True))
        sums.append(jnp.sum(ggp.astype(F32), axis=0, keepdims=True))
        sums.append(jnp.sum(adj * f1[r].astype(F32), axis=0, keepdims=True))
        sm_v[...] += jnp.concatenate(sums, axis=0)
        gri_v[r] = gri.astype(BF)
        return head

    lax.fori_loop(0, n, block, jnp.zeros((1, width), F32))
    wait(late)
    out = []
    gain1 = jnp.zeros((1, d), F32)
    for k, (i, ref) in enumerate(((3, n31.at[0]), (1, n31.at[1]), (2, n2), (0, n0))):
        part = mm_nt(gbr[i], wb[...]) + mm_nt(gri_v[i], wi[...])
        p_v[i] = part.astype(BF)
        out += begin(sem_out, k, (p_v.at[i], ref))
        gain1 = gain1 + jnp.sum(part * normed[i].astype(F32), axis=0, keepdims=True)

    def as_rows(v):
        v = jnp.concatenate([v, jnp.zeros((1, 3 * width - d), F32)], axis=1)
        return [v[:, i * width:(i + 1) * width] for i in range(3)]

    last_v[0:d] = mm_tn(flat(normed), flat(gri_v)).astype(BF)
    dw = mm_tn(flat(cv_v), flat(pair_s))
    hd = width // 2
    left = lax.broadcasted_iota(jnp.int32, (hd, width), 1) < hd
    for k in (0, 1):
        mine = dw[:, k * width:(k + 1) * width]
        last_v[d + k * hd:d + (k + 1) * hd] = jnp.where(left, mine[:hd], mine[hd:]).astype(BF)
    rest = last_v.shape[0] - d - 2 * hd
    few = [sm_v[...]] + as_rows(gain1) + as_rows(gain2[...]) + [jnp.zeros((rest - 14, width), F32)]
    last_v[d + 2 * hd:] = jnp.concatenate(few, axis=0).astype(BF)
    cut = last_v.shape[0] // 2
    halves = last_v.at[0:cut], last_v.at[cut:2 * cut]
    for part in (0, 1):
        @pl.when(y_ref[0] == part)
        def _():
            wait(begin(sem_out, 4, (halves[part], keep_o), (halves[1 - part], send_o)))
    wait(out)


def ends_branch(y_ref, cur, got, branch_o, out_o):
    for part in (0, 1):
        @pl.when(y_ref[0] == part)
        def _():
            pair = (cur, got) if part == 0 else (got, cur)
            branch_o[...] = pair[0][...].astype(F32)
            out_o[...] = pair[1][...].astype(F32).T


def ends_input(y_ref, cur, got, input_o, recur_o, gate_o, few_o, gains_o, whole):
    d, hd = input_o.shape[0], recur_o.shape[1]
    cut = whole.shape[0] // 2
    for part in (0, 1):
        @pl.when(y_ref[0] == part)
        def _():
            whole[part * cut:(part + 1) * cut] = cur[...]
            whole[(1 - part) * cut:(2 - part) * cut] = got[...]
    input_o[...] = whole[0:d].astype(F32)
    for k, ref in enumerate((recur_o, gate_o)):
        both_heads = whole[d + k * hd:d + (k + 1) * hd].astype(F32)
        for i in range(recur_o.shape[0]):
            ref[i] = both_heads[:, i * hd:(i + 1) * hd]
    few = whole[d + 2 * hd:d + 2 * hd + 16].astype(F32)
    few_o[...] = few[0:8]
    for k in (0, 1):
        at = 8 + 3 * k
        gains_o[k:k + 1] = jnp.concatenate([few[at + i:at + i + 1] for i in range(3)], axis=1)[:, :gains_o.shape[1]]


def mlp_blocks(xb, cot, wg, wu, wd, hid, gg, gu, p_v, ready, base):
    for i in range(xb.shape[0]):
        wait(ready[i])
        x = xb[i]
        ga = mm(x, wg[...])
        if i == 0:
            wait(ready[-1][:1])
        ua = mm(x, wu[...])
        if i == 0:
            wait(ready[-1][1:])
        gh = mm_nt(cot[base + i], wd[...])
        gl, slope = gelu_both(ga)
        hid[base + i] = (gl * ua).astype(BF)
        gg[i] = (gh * ua * slope).astype(BF)
        gu[i] = (gh * gl).astype(BF)
    for i in reversed(range(xb.shape[0])):
        p_v[i] = (mm_nt(gg[i], wg[...]) + mm_nt(gu[i], wu[...])).astype(BF)


def mlp_pre(
    b0, b1, c0, c1, wg_h, wu_h, wd_h, hid_h, gg_h, gu_h, n0, n1,
    xb, cot, wg, wu, wd, hid, gg, gu, p_v, sem_in, sem_out,
):
    first = begin(sem_in, 0, (b0, xb.at[0]), (wg_h, wg))
    then = begin(sem_in, 2, (wu_h, wu), (c0, cot.at[0]), (wd_h, wd))
    second = begin(sem_in, 5, (b1, xb.at[1]), (c1, cot.at[1]))
    mlp_blocks(xb, cot, wg, wu, wd, hid, gg, gu, p_v, (first, second, then), 0)
    wait(begin(sem_out, 0, (hid, hid_h), (gg, gg_h), (gu, gu_h), (p_v.at[1], n1), (p_v.at[0], n0)))


def mlp_main(
    y_ref, b2, b3, c0, c1, c2, c3, hid01, n1, wg_h, wu_h, wd_h, hid_h, gg_h, gu_h, n2, n31, dk_o, ds_o,
    xb, cot, wg, wu, wd, hid, gg, gu, p_v, dd, sem_in, sem_out,
):
    rows, units = hid.shape[1:]
    first = begin(sem_in, 0, (b2, xb.at[0]), (wg_h, wg))
    then = begin(sem_in, 2, (wu_h, wu), (c2, cot.at[2]), (wd_h, wd))
    second = begin(sem_in, 5, (b3, xb.at[1]), (c3, cot.at[3]))
    last = begin(sem_in, 7, (c0, cot.at[0]), (c1, cot.at[1]), (hid01, hid.at[0:2]), (n1, n31.at[1]))
    mlp_blocks(xb, cot, wg, wu, wd, hid, gg, gu, p_v, (first, second, then), 2)
    n31[0] = p_v[1]
    n2[...] = p_v[0]
    out = begin(sem_out, 0, (hid.at[2:4], hid_h), (gg, gg_h), (gu, gu_h))
    wait(last)
    call_ = cot[...].reshape(4 * rows, cot.shape[2])
    hall = hid[...].reshape(4 * rows, units)
    half = units // 2
    for part in (0, 1):
        dd[part] = mm_tn(hall[:, part * half:(part + 1) * half], call_).astype(BF)
    for part in (0, 1):
        @pl.when(y_ref[0] == part)
        def _():
            wait(begin(sem_out, 5, (dd.at[part], dk_o), (dd.at[1 - part], ds_o)))
    wait(out)


def mlp_post(
    y_ref, z_ref, b0, b1, b2, b3, gg01, gg23, gu01, gu23, gk_o, gs_o, uk_o, us_o,
    xb, gg, gu, dg, du, sem_in, sem_out,
):
    first = begin(sem_in, 0, (b0, xb.at[0]), (b1, xb.at[1]), (b2, xb.at[2]), (b3, xb.at[3]),
                  (gu01, gu.at[0:2]), (gu23, gu.at[2:4]))
    second = begin(sem_in, 6, (gg01, gg.at[0:2]), (gg23, gg.at[2:4]))
    wait(first)
    xall = flat(xb)
    half = dg.shape[1]
    for v, g, keep, send, ref, base in ((du, gu, uk_o, us_o, z_ref, 0), (dg, gg, gk_o, gs_o, y_ref, 2)):
        if base:
            wait(second)
        for k in (0, 1):
            v[k] = mm_tn(xall[:, k * half:(k + 1) * half], flat(g)).astype(BF)
            for part in (0, 1):
                @pl.when(ref[0] == part)
                def _():
                    begin(sem_out, base + k, (v.at[k], keep if part == k else send))
    wait([pltpu.make_async_copy(v.at[k], gk_o, sem_out.at[base + k]) for v, base in ((du, 0), (dg, 2)) for k in (0, 1)])


def mlp_out(hid01, hid23, wd_h, m0, m2, m31, hid, wd, p_v, sem_in, sem_out):
    wait(begin(sem_in, 0, (wd_h, wd), (hid01, hid.at[0:2]), (hid23, hid.at[2:4])))
    out = []
    for k, (i, ref) in enumerate(((3, m31.at[0]), (1, m31.at[1]), (2, m2), (0, m0))):
        p_v[i] = mm(hid[i], wd[...]).astype(BF)
        out += begin(sem_out, k, (p_v.at[i], ref))
    wait(out)


def add_two(a, b, got_a, got_b, send_o, own_o):
    send_o[...] = plus(a[...], got_a[...]).astype(BF)
    own_o[...] = plus(b[...], got_b[...]).astype(BF)


def add_both(i2, i0, o2, o0, got_i, got_o, send_o, own_i, own_o):
    send_o[0] = plus(i2[...], got_i[0]).astype(BF)
    own_i[...] = plus(i0[...], got_i[1]).astype(BF)
    send_o[1] = plus(o2[...], got_o[0]).astype(BF)
    own_o[...] = plus(o0[...], got_o[1]).astype(BF)


def add_pair(a, b, got, send_o, own_o):
    send_o[...] = plus(a[...], got[0]).astype(BF)
    own_o[...] = plus(b[...], got[1]).astype(BF)


def mid_fwd(x, own, far, gain, mid_o, n_o):
    mid = x[...].astype(F32) + plus(own[...], far[...])
    inv = lax.rsqrt(jnp.mean(mid * mid, axis=-1, keepdims=True) + EPSILON)
    mid_o[...] = mid
    n_o[...] = (mid * inv * gain[...]).astype(BF)


def norm_back(total, values, gain):
    inv = lax.rsqrt(jnp.mean(values * values, axis=-1, keepdims=True) + EPSILON)
    v = total * gain
    scaled = values * inv
    mean = jnp.mean(v * scaled, axis=-1, keepdims=True)
    grad = inv * (v - scaled * mean)
    return grad, jnp.sum(total * scaled, axis=0, keepdims=True)


def mid_bwd(mid, own, far, gain, cot, gm_o, gb_o, gg_o):
    grad, gsum = norm_back(plus(own[...], far[...]), mid[...], gain[...])
    gm = cot[...].astype(F32) + grad
    gm_o[...] = gm
    gb_o[...] = gm.astype(BF)
    gg_o[...] = gsum


def last_bwd(x, mid, own_i, own_o, far, gain, gm, o, out_o):
    grad, _ = norm_back(plus(own_i[...], far[0]), x[...].astype(F32), gain[...])
    o[...] = gm[...] + grad
    out_o[...] = (mid[...] + plus(own_o[...], far[1])).astype(BF)


def cost(us):
    return pl.CostEstimate(flops=1 + int(us * 1.15e9), bytes_accessed=0, transcendentals=0)


HBM, VMEM, SMEM = pltpu.HBM, pltpu.VMEM, pltpu.SMEM


def call(kernel, outs, *args, name, us, mib, places, out, scratch=()):
    spec = {"h": HBM, "v": VMEM, "s": SMEM, "a": pl.ANY}
    args = [
        pltpu.with_memory_space_constraint(a, VMEM if p == "v" else HBM) if p in "hv" else a
        for p, a in zip(places, args, strict=True)
    ]
    return pl.pallas_call(
        kernel,
        out_shape=[(VMEM if p == "v" else HBM)(*o) for p, o in zip(out, outs, strict=True)],
        in_specs=[pl.BlockSpec(memory_space=spec[p]) if p in spec else pl.BlockSpec() for p in places],
        out_specs=[pl.BlockSpec(memory_space=spec[p]) if p in spec else pl.BlockSpec() for p in out],
        scratch_shapes=list(scratch),
        compiler_params=pltpu.CompilerParams(vmem_limit_bytes=mib * MIB),
        cost_estimate=cost(us),
        name=name,
    )(*args)


CORE = [(i, i ^ 1) for i in range(4)]
FAR = [(i, i ^ 2) for i in range(4)]


def to_core(v):
    return lax.ppermute(v, "ch", CORE)


def to_far(v):
    return lax.ppermute(v, "ch", FAR)


class Order:
    def __init__(self):
        self.last = None

    def run(self, work, *values):
        if self.last is not None:
            values = lax.optimization_barrier((*values, *self.last))[:len(values)]
        got = work(*values)
        self.last = tuple(got) if isinstance(got, (tuple, list)) else (got,)
        return got

    def gate(self, value):
        return lax.optimization_barrier((value, *self.last))[0]

    def take(self, value):
        return self.run(lambda v: (v,), value)[0]


def dyn(g, index, size):
    return lax.dynamic_slice_in_dim(g, index * size, size, 0)


def plus(a, b):
    return a.astype(F32) + b.astype(F32)


def add_low(a, b):
    return plus(a, b).astype(BF)


def put(total, piece, index):
    return lax.dynamic_update_slice_in_dim(total, piece.astype(total.dtype), index * piece.shape[0], 0)


Y = [(i, i ^ 1) for i in range(8)]
Z1 = [(i, i ^ 2) for i in range(8)]
Z2 = [(i, i ^ 4) for i in range(8)]
def both(low, a, b):
    return jnp.concatenate([jnp.where(low, a, b), jnp.where(low, b, a)], 0)


def sum_rows_plain(keep, send, ends):
    yield "sent"
    return ends(*(lax.psum(v.astype(F32), "rows").astype(BF) for v in (keep, send)))


INWARD = [(0, 2), (1, 3), (6, 4), (7, 5)]
MIDDLE = [(2, 4), (3, 5), (4, 2), (5, 3)]
OUTWARD = [(2, 0), (3, 1), (4, 6), (5, 7)]


def send_on(value, pairs, order):
    if (yield "ready"):
        value = order.gate(value)
    got = lax.ppermute(value, "rows", pairs)
    yield "sent"
    return order.take(got)


def sum_rows_halves(keep, send, order, way, ends):
    me = lax.axis_index("rows")
    y, z = (Y, me % 2), (Z1, (me // 2) % 2)
    stages = ((y, z) if way == "y" else (z, y)) + ((Z2, me // 4),)
    got = yield from send_on(send, stages[0][0], order)
    yield "came"
    for pairs, bit in stages[1:]:
        half = keep.shape[0] // 2

        def split(a, b, bit=bit, half=half):
            return (add_low(dyn(a, 1 - bit, half), dyn(b, 1 - bit, half)), add_low(dyn(a, bit, half), dyn(b, bit, half)))

        send, keep = order.run(split, keep, got)
        got = yield from send_on(send, pairs, order)
        yield "came"
    cur = order.run(add_low, keep, got)
    for pairs, bit in stages[::-1]:
        got = yield from send_on(cur, pairs, order)
        yield "came"
        if pairs is stages[0][0]:
            return order.run(ends, cur, got)
        cur = order.run(lambda a, b, bit=bit: both(bit == 0, a, b), cur, got)


def sum_rows_line(keep, send, order, ends):
    me = lax.axis_index("rows")
    y, z = me % 2, me // 2
    inner = (z == 1) | (z == 2)
    got = yield from send_on(send, Y, order)
    yield "came"
    cur = order.run(add_low, keep, got)
    for pairs in (INWARD, MIDDLE):
        got = yield from send_on(cur, pairs, order)
        yield "came"
        cur = order.run(add_low, cur, got)
    got = yield from send_on(cur, OUTWARD, order)
    yield "came"
    cur = order.run(lambda a, b: jnp.where(inner, a, b), cur, got)
    got = yield from send_on(cur, Y, order)
    yield "came"
    return order.run(ends, cur, got)


class Chain:
    def __init__(self, steps):
        self.steps, self.value, self.state, self.held = steps, None, None, False
        self.go()

    def step(self, first=False):
        try:
            self.state = self.steps.send(None if self.state is None else self.held)
            self.held = False
        except StopIteration as end:
            self.state, self.value = "done", end.value

    def to(self, state):
        if self.state == "done":
            return
        self.step()
        while self.state not in (state, "done"):
            self.step()
        self.held = state == "ready"

    def come(self):
        if self.state == "sent":
            self.to("came")

    def go(self):
        self.to("sent")

    def finish(self):
        while self.state != "done":
            self.go()
        return self.value


def block_diag(w):
    h, d, e = w.shape
    rows = [
        jnp.concatenate([w[i] if i == j else jnp.zeros((d, e), w.dtype) for j in range(h)], axis=1)
        for i in range(h)
    ]
    return jnp.concatenate(rows, axis=0)


def body(n_rows, inputs, segment_ids, mixer_gain, branch_weight, input_weight, conv_weight, conv_bias,
         recur_weight, recur_bias, gate_weight, gate_bias, decay_param, out_weight, mlp_gain, mlp_gate,
         mlp_up, mlp_down, cotangent):
    x = inputs[0]
    cot = cotangent[0]
    rows, d = x.shape
    width = branch_weight.shape[1]
    units = mlp_gate.shape[1]
    heads, hd, _ = recur_weight.shape
    seq = segment_ids.shape[1]
    n = seq // rows
    me = lax.axis_index("ch").astype(jnp.int32)[None]
    gain1 = mixer_gain[None]
    gain2 = mlp_gain[None]
    order = Order()
    row = lax.axis_index("rows").astype(jnp.int32)[None]
    y_half = row % 2 if n_rows == 8 else jnp.zeros((1,), jnp.int32)
    z_half = (row // 2) % 2 if n_rows == 8 else jnp.zeros((1,), jnp.int32)

    split = {k: z_half if v == "z" else y_half for k, v in KINDS.items()}

    def total(keep, send, way, ends):
        if n_rows != 8:
            return Chain(sum_rows_plain(keep, send, ends))
        if way == "line":
            return Chain(sum_rows_line(keep, send, order, ends))
        return Chain(sum_rows_halves(keep, send, order, way, ends))

    x_far, x_near = to_far(x), to_core(x)

    def tables(ids, rw, gw, rb, gb_, dp):
        marks = [
            (jnp.pad(ids, (k, 0), constant_values=-1)[:seq] == ids).astype(F32) for k in (1, 2, 3)
        ]
        masks = jnp.pad(jnp.stack(marks, axis=1), ((0, 0), (0, 125))).reshape(n, rows, 128)
        wrg = jnp.concatenate([block_diag(rw), block_diag(gw)], axis=1)
        return masks, wrg, jnp.concatenate([rb, gb_])[None], (-8.0 * jax.nn.softplus(dp))[None]

    masks, wrg, brg, c8 = order.run(
        tables, segment_ids[0], recur_weight, gate_weight, recur_bias, gate_bias, decay_param
    )
    cb = conv_bias[None]
    blk, narrow, wide = (rows, d), (n, rows, width), (n, rows, units)
    four, two = (n, rows, d), (2, rows, d)
    narrow2, wide2 = (2, rows, width), (2, rows, units)
    dma = pltpu.SemaphoreType.DMA
    normed01, br01, ri01, wb_v, wi_v = order.run(
        functools.partial(
            call, mixer_pre, [(two, BF), (narrow2, F32), (narrow2, F32), ((d, width), BF), ((d, width), BF)],
            name="mixer_pre", us=0, mib=20, places="aahhi", out="hhhvv", scratch=[
                VMEM(two, BF), VMEM(two, BF), VMEM(narrow2, F32),
                VMEM(narrow2, F32), dma((4,)), dma((3,)),
            ]),
        x, x_near, branch_weight, input_weight, gain1)
    x_far = order.take(x_far)
    x_diag = to_core(x_far)
    cot_far = to_far(cot)
    x_diag = order.take(x_diag)
    fwd = order.run(
        functools.partial(
            call, mixer_fwd,
            [(two, BF), (narrow2, F32), (narrow, BF), (narrow, BF), (narrow, F32), (narrow, BF)] + [(blk, BF)] * 4,
            name="mixer_fwd", us=0, mib=30, places="saavvhhhhhiiiii", out="h" * 6 + "vvvv", scratch=[
                VMEM(two, BF), VMEM((width, 2 * width), BF),
                VMEM((n, rows, 128), F32), VMEM((width, d), BF), VMEM(two, BF), VMEM(narrow, F32),
                VMEM(narrow, F32), VMEM(narrow, BF), VMEM(narrow, BF), VMEM(narrow, F32), VMEM(narrow, BF),
                VMEM((rows + 8, width), F32), VMEM((rows + 8, width), F32), dma((9,)), dma((6,)),
            ]),
        me, x_far, x_diag, wb_v, wi_v, br01, ri01, wrg, masks, out_weight, gain1, conv_weight, cb,
        brg, c8)
    normed23, br23, ri, cv, sp, mix = fwd[:6]
    cot_far = order.take(cot_far)

    def near_half(own, far, pair):
        got = to_core(pair)
        return order.run(
            functools.partial(call, add_pair, [(blk, BF)] * 2, name="add_pair", us=0, mib=6, places="iii", out="vv"),
            far, own, got)

    send, own = order.run(
        functools.partial(call, add_two, [(blk, BF)] * 2, name="add_two", us=0, mib=6, places="vvii", out="vv"),
        fwd[7], fwd[6], to_core(fwd[8]), to_core(fwd[9]))
    far = to_far(send)
    cot_near, cot_diag = to_core(cot), to_core(cot_far)
    cot_near = order.take(cot_near)
    cot_diag = order.take(cot_diag)
    a1, gl, later, *fs = order.run(
        functools.partial(
            call, mixer_mid, [(narrow, BF), (narrow, BF), (narrow, F32)] + [(narrow, BF)] * 4, name="mixer_mid", us=0,
            mib=30, places="s" + "h" * 6 + "ii", out="h" * 7, scratch=[
                VMEM(narrow, F32), VMEM(narrow, BF), VMEM(narrow, F32), VMEM((width, 2 * width), BF),
                VMEM((n, rows, 128), F32), VMEM(narrow, BF), VMEM(narrow, BF), VMEM(narrow, F32)]
            + [VMEM(narrow, BF)] * 4 + [VMEM((rows + 8, width), F32), dma((6,)), dma((7,))]),
        me, br01, br23, cv, sp, wrg, masks, brg, c8)
    mid, normed2 = order.run(functools.partial(
        call, mid_fwd, [(blk, F32), (blk, BF)], name="mid_fwd", us=0, mib=8, places="ivvi", out="iv"),
        x, own, far, gain2)
    n_far, n_near = to_far(normed2), to_core(normed2)
    n_near = order.take(n_near)
    mlp_scratch = [
        VMEM((d, units), BF), VMEM((d, units), BF), VMEM((units, d), BF)]
    hid01, gg01, gu01, g0, g1 = order.run(
        functools.partial(
            call, mlp_pre, [(wide2, BF)] * 3 + [(blk, BF)] * 2, name="mlp_pre", us=0, mib=30, places="aahhhhh",
            out="h" * 5, scratch=[VMEM(two, BF), VMEM(two, BF)] + mlp_scratch + [VMEM(wide2, BF)] * 3 + [
                VMEM(two, BF), dma((7,)), dma((5,))]),
        normed2, n_near, cot, cot_near, mlp_gate, mlp_up, mlp_down)
    n_far = order.take(n_far)
    n_diag = order.take(to_core(n_far))
    hid23, gg23, gu23, g2, g31, down_keep, down_send = order.run(
        functools.partial(
            call, mlp_main, [(wide2, BF)] * 3 + [(blk, BF), (two, BF)] + [((units // 2, d), BF)] * 2, name="mlp_main",
            us=0, mib=26, places="saahhhhhhhhh", out="hhhvvhh",
            scratch=[VMEM(two, BF), VMEM(four, BF)] + mlp_scratch + [VMEM(wide, BF), VMEM(wide2, BF), VMEM(wide2, BF)] + [
                VMEM(two, BF), VMEM((2, units // 2, d), BF), dma((11,)), dma((7,))]),
        split["d"], n_far, n_diag, cot, cot_near, cot_far, cot_diag, hid01, g1, mlp_gate, mlp_up, mlp_down)
    y_low, z_low = y_half[0] == 0, z_half[0] == 0

    def wide_ends(low, a, b):
        return both(low, a, b).astype(F32)

    def ends_of(kind):
        return functools.partial(wide_ends, y_low if split[kind] is y_half else z_low)

    s_down = total(down_keep, down_send, KINDS["d"], ends_of("d"))
    g_send, g_own = near_half(g0, g2, g31)
    from_far = to_far(g_send)
    post = order.run(
        functools.partial(
            call, mlp_post, [((d // 2, units), BF)] * 4, name="mlp_post", us=0, mib=26, places="ssaaaahhhh",
            out="h" * 4, scratch=[
                VMEM(four, BF), VMEM(wide, BF), VMEM(wide, BF), VMEM((2, d // 2, units), BF),
                VMEM((2, d // 2, units), BF), dma((8,)), dma((4,)),
            ]),
        split["g"], split["u"], normed2, n_near, n_far, n_diag, gg01, gg23, gu01, gu23)
    s_gate = total(post[0], post[1], KINDS["g"], ends_of("g"))
    s_up = total(post[2], post[3], KINDS["u"], ends_of("u"))
    chains = {"d": s_down, "g": s_gate, "u": s_up}
    live = {}

    def at_rf():
        gm, gb, gsum2 = order.run(functools.partial(
            call, mid_bwd, [(blk, F32), (blk, BF), ((1, d), F32)], name="mid_bwd", us=10, mib=8, places="ivvii", out="ivi"),
            mid, g_own, from_far, gain2, cot)
        g_near, g_far = to_core(gb), to_far(gb)
        part = order.run(
            functools.partial(
                call, mlp_out, [(blk, BF), (blk, BF), (two, BF)], name="mlp_out", us=0, mib=16, places="hhh", out="hhh",
                scratch=[VMEM(wide, BF), VMEM((units, d), BF), VMEM(four, BF), dma((3,)), dma((4,))]),
            hid01, hid23, mlp_down)
        live.update(gm=gm, gb=gb, gsum2=gsum2, g_near=g_near, g_far=g_far, part=part)

    def at_gf():
        gb = live["gb"]
        g_far = order.take(live["g_far"])
        g_diag = to_core(g_far)
        g_near = order.take(live["g_near"])
        g_diag = order.take(g_diag)
        gs, gbr, p_keep, p_send = order.run(
            functools.partial(
                call, mixer_out, [(narrow, F32), (narrow, BF)] + [((d, width), BF)] * 2, name="mixer_out", us=0, mib=30,
                places="shaaa" + "h" * 6, out="h" * 4, scratch=[
                    VMEM(four, BF), VMEM((width, d), BF), VMEM(narrow, BF), VMEM(narrow, BF), VMEM(four, BF),
                    VMEM(narrow, BF), VMEM(narrow, F32), VMEM(narrow, BF), VMEM((2, d, width), BF), dma((10,)), dma((4,))]),
            split["p"], gb, g_near, g_far, g_diag, out_weight, a1, gl, normed01, normed23, mix)
        chains["p"] = total(p_keep, p_send, KINDS["p"], functools.partial(
            call, ends_branch, [((d, width), F32), ((width, d), F32)], split["p"], name="ends_branch", us=0, mib=16,
            places="sii", out="ii"))
        live.update(gs=gs, gbr=gbr)

    def at_m():
        last_rows = d + 2 * hd + 64
        bwd = order.run(
            functools.partial(
                call, mixer_bwd, [(blk, BF), (blk, BF), (two, BF)] + [((last_rows // 2, width), BF)] * 2,
                name="mixer_bwd", us=0, mib=36, places="ss" + "h" * 15 + "ii", out="h" * 5, scratch=[
                    VMEM(narrow, F32), VMEM(narrow, F32)] + [VMEM(narrow, BF)] * 6 + [
                    VMEM((width, 2 * width), BF), VMEM((n, rows, 128), F32), VMEM(narrow, BF), VMEM(four, BF),
                    VMEM((d, width), BF), VMEM((d, width), BF), VMEM((n, rows, 2 * width), BF), VMEM(narrow, BF),
                    VMEM(four, BF), VMEM((last_rows, width), BF), VMEM((8, width), F32), VMEM((3, rows + 8, width), F32),
                    dma((8, n)), dma((8,)), dma((6,)),
                ]),
            me, split["q"], live["gs"], later, *fs, ri, cv, wrg, masks, live["gbr"], normed01, normed23, branch_weight, input_weight,
            conv_weight, live["gsum2"])
        chains["q"] = total(bwd[3], bwd[4], KINDS["q"], functools.partial(
            call, ends_input, [((d, width), F32), ((heads, hd, hd), F32), ((heads, hd, hd), F32), ((8, width), F32),
             ((2, d), F32)], split["q"], name="ends_input", us=0, mib=16, places="sii", out="iiiii", scratch=[VMEM((last_rows, width), BF)]))

        live.update(bwd=bwd)

    def sum_ch(n0, n2, pair):
        got_i, got_o = to_core(order.gate(pair)), to_core(order.gate(live["part"][2]))
        yield "sent"
        got_i, got_o = order.run(lambda a, b: (a, b), got_i, got_o)
        yield "came"
        send, own_i, own_o = order.run(
            functools.partial(
                call, add_both, [(two, BF), (blk, BF), (blk, BF)], name="add_both", us=0, mib=14, places="iiiiii", out="uuu"),
            n2, n0, live["part"][1], live["part"][0], got_i, got_o)
        far = to_far(send)
        yield "sent"
        far = order.take(far)
        yield "came"
        return order.run(
            functools.partial(
                call, last_bwd, [(blk, F32), (blk, BF)], name="last_bwd", us=0, mib=14, places="iiiiiii", out="ii"),
            x, mid, own_i, own_o, far, gain1, live["gm"])

    events = {"rf": at_rf, "gf": at_gf, "m": at_m}

    def turn(what):
        if what in events:
            events[what]()
            return
        if what == "c":
            if "bwd" in live and "i" not in chains and chains["d"].state == "done":
                chains["i"] = Chain(sum_ch(*live["bwd"][:3]))
            return
        chains[what].go()

    for what in PLAN:
        turn(what)
    while "i" not in chains or any(c.state != "done" for c in chains.values()):
        for what in PLAN_AFTER:
            if what in chains or what == "c":
                turn(what)
    input_grad, output = chains["i"].value
    t_branch, t_out = chains["p"].value
    t_input, t_recur, t_gate_w, ts, gains = chains["q"].value
    t_down, t_gate, t_up = (s.value for s in (s_down, s_gate, s_up))
    others = [lax.ppermute(gains, "ch", [(i, i ^ k) for i in range(4)]) for k in (3, 2, 1)]
    gain1_grad, gain2_grad = order.run(
        lambda own, c, b, a: tuple((own[k] + a[k]) + (b[k] + c[k]) for k in (0, 1)), gains, *others)
    gain1_grad = gain1_grad / mixer_gain
    decay_grad = ts[7] * -8.0 * jax.nn.sigmoid(decay_param)
    return (
        output[None],
        input_grad[None],
        gain1_grad,
        t_branch,
        t_input,
        ts[0:4],
        ts[4],
        t_recur,
        ts[5],
        t_gate_w,
        ts[6],
        decay_grad,
        t_out,
        gain2_grad,
        t_gate,
        t_up,
        t_down,
    )


def solution(mesh):
    rows, ch = P("rows", "ch", None), P("ch")
    cols, lead = P(None, "ch"), P("ch", None)
    heads = P("ch", None, None)
    return jax.shard_map(
        functools.partial(body, mesh.shape["rows"]),
        mesh=mesh,
        in_specs=(rows, P("rows", None), P(), cols, cols, cols, ch, heads, ch, heads, ch, ch, lead, P(),
                  cols, cols, lead, rows),
        out_specs=(rows, rows, P(), cols, cols, cols, ch, heads, ch, heads, ch, ch, lead, P(), cols, cols, lead),
        check_vma=False,
    )
```
